256 devices in a mesh: frame: 32 (over x_lo, z, core), quad: 8 (over x_hi, y).
Axes of the slice: x: 4 (x_hi: 2, x_lo: 2; x = x_hi * 2 + x_lo), y: 4, z: 8, core: 2. Of those that a mesh axis runs over, the one named last changes fastest.
Arguments:
- activations: bfloat16 [128, 256, 1280], P('frame', 'quad'), may hold values from -48 to 48
- cotangent: bfloat16 [128, 256, 1280], P('frame', 'quad'), may hold values from -6 to 6
- spatial_weights: bfloat16 [4, 1280, 640], replicated, may hold values from -2 to 2
- spatial_gain: float32 [1280], replicated, may hold values from 0.1 to 1.9
- motion_weights: bfloat16 [4, 1280, 640], P(None, 'quad'), may hold values from -2 to 2
- motion_gain: float32 [1280], replicated, may hold values from 0.1 to 1.9
Outputs:
- block_output: bfloat16 [128, 256, 1280], P('frame', 'quad')
- input_grad: bfloat16 [128, 256, 1280], P('frame', 'quad')
- weight_grad: float32 [4, 1280, 640], P(None, ('frame', 'quad'))
- gain_grad: float32 [1280], P(('frame', 'quad'))
The draws below stay inside these ranges and needn't reach their ends.
All inputs are finite; a program needn't handle non-finite values.
Results may differ from the reference program's by a relative error of at most 0.03.
Values may be sent and summed in bfloat16 or wider, within the bound.
A program may use at most 128 MiB of HBM per device.

```python
import math
import jax
import jax.numpy as jnp
from jax import lax

C = 1280
HEADS = 4
HEAD_DIM = 160
FRAMES = 128
POS = 256


def projection_draw(key, strength_low, strength_high, amplitude):
    pieces = jnp.clip(jax.random.normal(key, (4, C, HEADS * HEAD_DIM), jnp.float32), -4.0, 4.0)
    head_key = jax.random.fold_in(key, 5)
    strength = jnp.exp(jax.random.uniform(head_key, (HEADS,), jnp.float32, math.log(strength_low), math.log(strength_high)))
    strength = jnp.repeat(strength, HEAD_DIM)
    query_part = pieces[0] * C ** (-0.5) * strength
    key_part = pieces[1] * C ** (-0.5) * strength
    value_part = pieces[2] * C ** (-0.5) * amplitude
    output_part = pieces[3] * (HEADS * HEAD_DIM) ** (-0.5) * amplitude
    stacked = jnp.stack([query_part, key_part, value_part, output_part])
    return jnp.clip(stacked, -2.0, 2.0).astype(jnp.bfloat16)


def draw_activations(key, part):
    key = jax.random.fold_in(key, 11)
    base = jnp.clip(jax.random.normal(key, (FRAMES, POS, C), jnp.float32), -4.0, 4.0)
    return base.astype(jnp.bfloat16)


def draw_spatial_weights(key, part):
    key = jax.random.fold_in(key, 21)
    return projection_draw(key, 1.0, 1.0, 2.0)


def draw_motion_weights(key, part):
    key = jax.random.fold_in(key, 31)
    return projection_draw(key, 1.0, 1.0, 1.0)


def strengthened(values, stream_key, source, target, shards_of, factor):
    def block_of(position):
        return (jnp.arange(values.shape[position]) // (values.shape[position] // shards_of)).reshape((-1,) + (1,) * (values.ndim - 1 - position))

    near = jax.random.permutation(stream_key, shards_of)[block_of(target)]
    far = (block_of(target) + shards_of // 2) % shards_of
    return jnp.where((block_of(source) == near) | (block_of(source) == far), factor * values, values)


def block_scale(stream_key, extent, cuts, least, largest):
    loudness, own = 1.0, jax.random.fold_in(stream_key, 6)
    for axis_at, shards_of in cuts:
        heights = jnp.exp(jax.random.uniform(jax.random.fold_in(own, axis_at), (shards_of,), jnp.float32, least / len(cuts), largest / len(cuts)))
        loudness = loudness * jnp.repeat(heights, extent[axis_at] // shards_of).reshape([-1 if axis == axis_at else 1 for axis in range(len(extent))])
    return loudness


def heavy_noise(stream_key, extent, scale, limit, cuts, heavy, held_as=jnp.bfloat16):
    values = scale * jax.random.normal(stream_key, extent, jnp.float32)
    if cuts:
        values = values * block_scale(stream_key, extent, cuts, -0.22, 0.18)
    return jnp.clip(strengthened(values, jax.random.fold_in(stream_key, 3), *heavy), -limit, limit).astype(held_as)


def setup_inputs(seed: int = 0) -> dict:
    key_of = jax.random.split(jax.random.key(seed), 7)
    activations = draw_activations(jax.random.fold_in(key_of[6], 71), 0)
    cotangent = heavy_noise(key_of[1], (FRAMES, POS, C), 1.0, 6.0, ((0, 32), (1, 8)), (0, 2, 32, 2.75))
    spatial_weights = draw_spatial_weights(jax.random.fold_in(key_of[6], 71), 0)
    spatial_gain = jnp.clip(1.0 + 0.18 * jax.random.normal(key_of[3], (C,), jnp.float32), 0.1, 1.9)
    motion_weights = draw_motion_weights(jax.random.fold_in(key_of[6], 71), 0)
    motion_gain = jnp.clip(1.0 + 0.18 * jax.random.normal(key_of[5], (C,), jnp.float32), 0.1, 1.9)
    return {"activations": activations, "cotangent": cotangent, "spatial_weights": spatial_weights, "spatial_gain": spatial_gain, "motion_weights": motion_weights, "motion_gain": motion_gain}


EPSILON = 1e-05

def normalize(values, gain):
    average = lax.optimization_barrier(jnp.mean(values, axis=-1, keepdims=True))
    centred = values - average
    inv_scale = lax.rsqrt(lax.optimization_barrier(jnp.mean(centred * centred, axis=-1, keepdims=True)) + EPSILON)
    unit_rows = centred * inv_scale
    return (unit_rows * gain, unit_rows, inv_scale)

def normalize_back(grad_rows, unit_rows, inv_scale, gain):
    scaled = grad_rows * gain
    first_mean = lax.optimization_barrier(jnp.mean(scaled, axis=-1, keepdims=True))
    second_mean = lax.optimization_barrier(jnp.mean(scaled * unit_rows, axis=-1, keepdims=True))
    return inv_scale * (scaled - first_mean - unit_rows * second_mean)

def positional(frames, channels):
    frame_pos = jnp.arange(frames).astype(jnp.float32)[:, None]
    freq_index = jnp.arange(channels // 2).astype(jnp.float32)[None, :]
    phases = frame_pos * jnp.exp(freq_index * (-2.0 * math.log(10000.0) / channels))
    return jnp.stack([jnp.sin(phases), jnp.cos(phases)], axis=-1).reshape(frames, channels)

def project(row_block, weight):
    flattened = row_block.reshape(-1, row_block.shape[-1])
    result = jnp.dot(flattened, weight, preferred_element_type=jnp.float32)
    return result.reshape(row_block.shape[:-1] + (weight.shape[-1],))

def project_back(row_block, weight):
    flattened = row_block.reshape(-1, row_block.shape[-1])
    result = jnp.dot(flattened, weight.T, preferred_element_type=jnp.float32)
    return result.reshape(row_block.shape[:-1] + (weight.shape[0],))

def outer_sum(left_rows, right_rows):
    left_flat = left_rows.reshape(-1, left_rows.shape[-1])
    right_flat = right_rows.reshape(-1, right_rows.shape[-1])
    return jnp.dot(left_flat.T, right_flat, preferred_element_type=jnp.float32)

def split_heads(tensor):
    return tensor.reshape(tensor.shape[:-1] + (HEADS, HEAD_DIM)).astype(jnp.float32)

def attend(queries, key_rows, value_rows):
    query_heads = split_heads(queries)
    key_heads = split_heads(key_rows)
    value_heads = split_heads(value_rows)
    scores = jnp.einsum('bqhd,bkhd->bhqk', query_heads, key_heads) * HEAD_DIM ** (-0.5)
    highest = lax.optimization_barrier(jnp.max(scores, axis=-1, keepdims=True))
    expo_rows = jnp.exp(scores - highest)
    probs = (expo_rows / lax.optimization_barrier(jnp.sum(expo_rows, axis=-1, keepdims=True))).astype(jnp.bfloat16)
    result = jnp.einsum('bhqk,bkhd->bqhd', probs.astype(jnp.float32), value_heads)
    return result.reshape(queries.shape).astype(jnp.bfloat16)

def score_grads(queries, key_rows, value_rows, grad_rows):
    query_heads = split_heads(queries)
    key_heads = split_heads(key_rows)
    value_heads = split_heads(value_rows)
    grad_heads = split_heads(grad_rows)
    scores = jnp.einsum('bqhd,bkhd->bhqk', query_heads, key_heads) * HEAD_DIM ** (-0.5)
    highest = lax.optimization_barrier(jnp.max(scores, axis=-1, keepdims=True))
    log_total = highest + jnp.log(lax.optimization_barrier(jnp.sum(jnp.exp(scores - highest), axis=-1, keepdims=True)))
    probs = jnp.exp(scores - log_total)
    grad_probs = jnp.einsum('bqhd,bkhd->bhqk', grad_heads, value_heads)
    inner_sum = lax.optimization_barrier(jnp.sum(probs * grad_probs, axis=-1, keepdims=True))
    grad_scores = (probs * (grad_probs - inner_sum) * HEAD_DIM ** (-0.5)).astype(jnp.bfloat16)
    return (probs.astype(jnp.bfloat16), grad_scores)

def attend_back(queries, key_rows, value_rows, grad_rows):
    probs, grad_scores = score_grads(queries, key_rows, value_rows, grad_rows)
    query_heads = split_heads(queries)
    key_heads = split_heads(key_rows)
    grad_heads = split_heads(grad_rows)
    grad_query = jnp.einsum('bhqk,bkhd->bqhd', grad_scores.astype(jnp.float32), key_heads)
    grad_key = jnp.einsum('bhqk,bqhd->bkhd', grad_scores.astype(jnp.float32), query_heads)
    grad_value = jnp.einsum('bhqk,bqhd->bkhd', probs.astype(jnp.float32), grad_heads)
    return (grad_query.reshape(queries.shape).astype(jnp.bfloat16), grad_key.reshape(key_rows.shape).astype(jnp.bfloat16), grad_value.reshape(key_rows.shape).astype(jnp.bfloat16))

def blocked(function, arrays, block_size):
    groups = arrays[0].shape[0] // block_size
    grouped = tuple((member.reshape((groups, block_size) + member.shape[1:]) for member in arrays))
    results = lax.map(lambda members: function(*members), grouped)
    return jax.tree.map(lambda piece: piece.reshape((groups * block_size,) + piece.shape[2:]), results)

def reference(activations, cotangent, spatial_weights, spatial_gain, motion_weights, motion_gain):
    frames, cells, channels = activations.shape
    input_wide = activations.astype(jnp.float32)
    normed, unit_one, scale_one = normalize(input_wide, spatial_gain)
    normed_one = normed.astype(jnp.bfloat16)
    spatial_query = project(normed_one, spatial_weights[0]).astype(jnp.bfloat16)
    spatial_keys = project(normed_one, spatial_weights[1]).astype(jnp.bfloat16)
    spatial_values = project(normed_one, spatial_weights[2]).astype(jnp.bfloat16)
    spatial_out = blocked(attend, (spatial_query, spatial_keys, spatial_values), 8)
    hidden = (input_wide + project_back(spatial_out, spatial_weights[3])).astype(jnp.bfloat16)
    by_cell = jnp.swapaxes(hidden, 0, 1)
    cell_wide = by_cell.astype(jnp.float32)
    normed_t, unit_two, scale_two = normalize(cell_wide, motion_gain)
    normed_two = (normed_t + positional(frames, channels)[None]).astype(jnp.bfloat16)
    motion_query = project(normed_two, motion_weights[0]).astype(jnp.bfloat16)
    motion_keys = project(normed_two, motion_weights[1]).astype(jnp.bfloat16)
    motion_values = project(normed_two, motion_weights[2]).astype(jnp.bfloat16)
    motion_out = blocked(attend, (motion_query, motion_keys, motion_values), 8)
    result_cells = (cell_wide + project_back(motion_out, motion_weights[3])).astype(jnp.bfloat16)
    block_output = jnp.swapaxes(result_cells, 0, 1)
    grad_by_cell = jnp.swapaxes(cotangent, 0, 1)
    grad_motion_out = project(grad_by_cell, motion_weights[3]).astype(jnp.bfloat16)
    grad_out_proj = outer_sum(grad_by_cell, motion_out)
    grad_mq, grad_mk, grad_mv = blocked(attend_back, (motion_query, motion_keys, motion_values, grad_motion_out), 8)
    weight_terms = jnp.stack([outer_sum(normed_two, grad_mq), outer_sum(normed_two, grad_mk), outer_sum(normed_two, grad_mv), grad_out_proj])
    grad_normed_two = project_back(grad_mq, motion_weights[0]) + project_back(grad_mk, motion_weights[1]) + project_back(grad_mv, motion_weights[2])
    gain_terms = lax.optimization_barrier(jnp.sum((grad_normed_two * unit_two).reshape(-1, channels), axis=0))
    grad_hidden_cells = (grad_by_cell.astype(jnp.float32) + normalize_back(grad_normed_two, unit_two, scale_two, motion_gain)).astype(jnp.bfloat16)
    grad_hidden = jnp.swapaxes(grad_hidden_cells, 0, 1)
    grad_spatial_out = project(grad_hidden, spatial_weights[3]).astype(jnp.bfloat16)
    grad_sq, grad_sk, grad_sv = blocked(attend_back, (spatial_query, spatial_keys, spatial_values, grad_spatial_out), 8)
    grad_normed_one = project_back(grad_sq, spatial_weights[0]) + project_back(grad_sk, spatial_weights[1]) + project_back(grad_sv, spatial_weights[2])
    input_grad = (grad_hidden.astype(jnp.float32) + normalize_back(grad_normed_one, unit_one, scale_one, spatial_gain)).astype(jnp.bfloat16)
    factor = 1.0 / math.sqrt(frames * cells)
    return (block_output, input_grad, weight_terms * factor, gain_terms * factor)
```

```python
import math

import jax
import jax.numpy as jnp
import numpy as np
from jax import lax
from jax.experimental import pallas as pl
from jax.experimental.pallas import tpu as pltpu
from jax.sharding import PartitionSpec as P

HEADS = 4
HEAD_DIM = 160
EPSILON = 1e-05
SCALE = HEAD_DIM ** (-0.5)
C = 1280
W = 640
F32 = jnp.float32
BF = jnp.bfloat16
MESH = pl.DeviceIdType.MESH


def nn(a, b):
    return jnp.dot(a, b, preferred_element_type=F32)


def nt(a, b):
    return lax.dot_general(a, b, (((1,), (1,)), ((), ())), preferred_element_type=F32)


def tn(a, b):
    return lax.dot_general(a, b, (((0,), (0,)), ((), ())), preferred_element_type=F32)


def unit(x):
    xc = x - jnp.mean(x, axis=-1, keepdims=True)
    r = lax.rsqrt(jnp.mean(xc * xc, axis=-1, keepdims=True) + EPSILON)
    return xc * r, r


def unit_back(grad, u, r, gain):
    g = grad * gain
    return r * (g - jnp.mean(g, axis=-1, keepdims=True) - u * jnp.mean(g * u, axis=-1, keepdims=True))


def head_of(x, h):
    lane = lax.broadcasted_iota(jnp.int32, x.shape, 1)
    return jnp.where((lane >= h * HEAD_DIM) & (lane < (h + 1) * HEAD_DIM), x, jnp.zeros_like(x))


def split_pair(y):
    return y[:, :384], pltpu.roll(y, 320, 1)[:, :384]


def join_pair(a, b):
    pad = jnp.zeros((a.shape[0], 256), F32)
    left = jnp.concatenate([a, pad], axis=1)
    right = pltpu.roll(jnp.concatenate([b, pad], axis=1), 320, 1)
    lane = lax.broadcasted_iota(jnp.int32, left.shape, 1)
    return jnp.where(lane < 320, left, right)


def row_order():
    row = lax.broadcasted_iota(jnp.int32, (128, 128), 0)
    col = lax.broadcasted_iota(jnp.int32, (128, 128), 1)
    return jnp.where(col == (row % 4) * 32 + row // 4, 1.0, 0.0).astype(BF)


def scatter_rows(to, rows):
    for n in range(32):
        to[n] = rows[4 * n:4 * n + 4, :].astype(BF)


def gather_rows(rows, come):
    for n in range(32):
        rows[4 * n:4 * n + 4, :] = come[n].astype(F32)


def softmax(q, k):
    s = nt(q, k) * SCALE
    e = jnp.exp(s - jnp.max(s, axis=-1, keepdims=True))
    return e / jnp.sum(e, axis=-1, keepdims=True)


def attend_back(q, k, v, g, probs, heads):
    dq = dk = dv = None
    for h in range(heads):
        r = probs[h]
        dr = nt(head_of(g, h), v)
        delta = jnp.sum(r * dr, axis=-1, keepdims=True)
        ds = (r * (dr - delta) * SCALE).astype(BF)
        a, b, c = nn(ds, head_of(k, h)), tn(ds, head_of(q, h)), tn(r.astype(BF), head_of(g, h))
        dq, dk, dv = (a, b, c) if dq is None else (dq + a, dk + b, dv + c)
    return dq, dk, dv


def kernel(act_h, cot_h, spw_h, spg, mw_h, mgn, pe_h, perm_h,
           bo, ig, wg, gn,
           act, cot, spw, mw, pe, perm,
           qkv_s, qkv_r, o_s, o_r, prob_s,
           hid, hid_s, hid_r, g_s, g_r, tx, n2s, u2s, r2s, mqkv, prob_t,
           mo_s, mo_r, lb_s, lb_r, gh, mof,
           gs_s, gs_r, dq_s, dq_r,
           fxs, fys, ax, ay, wa, wb, ra1, rb1, sa1, sb1, ra2, rb2, p3, r3, fin, finr,
           gv1, gr1, gv2, gr2, gv3, gr3, gv4, gr4,
           ld, w_ss, w_rs, f_ss, f_rs, q_ss, q_rs, o_ss, o_rs, h_ss, h_rs, g_ss, g_rs,
           m_ss, m_rs, l_ss, l_rs, gs_ss, gs_rs, dq_ss, dq_rs, x_ss, x_rs,
           a1_ss, a1_rs, b1_ss, b1_rs, a2_ss, a2_rs, b2_ss, b2_rs, r3_ss, r3_rs, e_ss, e_rs,
           v_ss, v_rs):
    i, j = lax.axis_index("frame"), lax.axis_index("quad")
    core, z, x_lo = i % 2, (i // 2) % 8, i // 16
    y, x_hi = j % 4, j // 4
    x = x_hi * 2 + x_lo
    sib = (i + 1 - 2 * core, j)

    def fpeer(d):
        return (i + d) % 32

    def qpeer(d):
        return (j + d) % 8

    def xpeer(d):
        xx = (x + d) % 4
        return ((xx % 2) * 16 + i % 16, (xx // 2) * 4 + y)

    def ypeer(d):
        return (i, x_hi * 4 + (y + d) % 4)

    def zpeer(d):
        return (x_lo * 16 + ((z + d) % 8) * 2 + core, j)

    def remote(src, dst, ss, rs, dev):
        return pltpu.make_async_remote_copy(
            src_ref=src, dst_ref=dst, send_sem=ss, recv_sem=rs, device_id=dev, device_id_type=MESH)

    bar = pltpu.get_barrier_semaphore()

    @pl.loop(1, 32)
    def _(d):
        pl.semaphore_signal(bar, inc=1, device_id=(fpeer(d), j), device_id_type=MESH)

    @pl.loop(1, 8)
    def _(d):
        pl.semaphore_signal(bar, inc=1, device_id=(i, qpeer(d)), device_id_type=MESH)

    diag = (((x_lo + 1) % 2) * 16 + i % 16, ((x_hi + 1) % 2) * 4 + y)
    pl.semaphore_signal(bar, inc=1, device_id=diag, device_id_type=MESH)

    loads = [
        pltpu.make_async_copy(act_h, act, ld.at[0]),
        pltpu.make_async_copy(spw_h.at[0], spw.at[0], ld.at[1]),
        pltpu.make_async_copy(spw_h.at[1], spw.at[1], ld.at[2]),
        pltpu.make_async_copy(spw_h.at[2], spw.at[2], ld.at[3]),
        pltpu.make_async_copy(spw_h.at[3], spw.at[3], ld.at[4]),
        pltpu.make_async_copy(cot_h, cot, ld.at[5]),
        pltpu.make_async_copy(mw_h, mw.at[:, j], ld.at[6]),
        pltpu.make_async_copy(pe_h, pe, ld.at[7]),
        pltpu.make_async_copy(perm_h, perm, ld.at[8]),
    ]
    for c in loads:
        c.start()
    pl.semaphore_wait(bar, 39)

    def w_copy(t, d):
        return remote(mw_h.at[2 * core + t], mw.at[2 * core + t, j], w_ss.at[8 * t + d], w_rs.at[8 * t + d], (i, qpeer(d)))

    def w_forward(t, d):
        part = mw.at[2 * core + t, (j - d + 8) % 8]
        return remote(part, part, f_ss.at[8 * t + d], f_rs.at[8 * t + d], sib)

    for t in range(2):
        @pl.loop(1, 8)
        def _(d, t=t):
            w_copy(t, d).start()

    loads[0].wait()
    u1, _ = unit(act[...].astype(F32))
    n1 = (u1 * spg[...]).astype(BF)
    for t in range(3):
        loads[1 + t].wait()
        for hp, part in enumerate(split_pair(nn(n1, spw[t]))):
            qkv_s[hp * 4:hp * 4 + 4, t] = part.astype(BF).reshape(4, 32, 384)

    def q_copy(d):
        return remote(qkv_s.at[qpeer(d)], qkv_r.at[j], q_ss.at[d], q_rs.at[d], (i, qpeer(d)))

    @pl.loop(1, 8)
    def _(d):
        q_copy(d).start()

    qkv_r[j] = qkv_s[j]

    @pl.loop(1, 8)
    def _(d):
        q_copy(d).wait()

    q, k, v = (qkv_r[:, t].reshape(256, 384) for t in range(3))
    out = None
    for h in range(2):
        probs = softmax(head_of(q, h), k)
        prob_s[h] = probs
        term = nn(probs.astype(BF), head_of(v, h))
        out = term if out is None else out + term
    o_s[...] = out.astype(BF).reshape(8, 32, 384)

    def o_copy(d):
        return remote(o_s.at[qpeer(d)], o_r.at[j], o_ss.at[d], o_rs.at[d], (i, qpeer(d)))

    @pl.loop(1, 8)
    def _(d):
        o_copy(d).start()

    o_r[j] = o_s[j]

    loads[5].wait()
    loads[8].wait()

    @pl.loop(1, 8)
    def _(d):
        o_copy(d).wait()

    loads[4].wait()
    so = join_pair(o_r[0:4].reshape(128, 384).astype(F32), o_r[4:8].reshape(128, 384).astype(F32)).astype(BF)
    hid[...] = (act[...].astype(F32) + nt(so, spw[3])).astype(BF)
    scatter_rows(hid_s, nn(row_order(), hid[...]))

    def h_copy(d):
        return remote(hid_s.at[fpeer(d)], hid_r.at[i], h_ss.at[d], h_rs.at[d], (fpeer(d), j))

    @pl.loop(1, 32)
    def _(d):
        h_copy(d).start()

    hid_r[i] = hid_s[i]

    loads[6].wait()
    for t in range(2):
        @pl.loop(1, 8)
        def _(d, t=t):
            w_copy(t, d).wait()
            w_forward(t, d).start()

    for t in range(2):
        @pl.loop(1, 8)
        def _(d, t=t):
            w_forward(t, d).wait()

    def weight(n):
        return mw[n].reshape(C, W)

    grad_out = nn(cot[...], weight(3)).astype(BF)
    scatter_rows(g_s, nn(row_order(), grad_out))

    def g_copy(d):
        return remote(g_s.at[fpeer(d)], g_r.at[i], g_ss.at[d], g_rs.at[d], (fpeer(d), j))

    @pl.loop(1, 32)
    def _(d):
        g_copy(d).start()

    g_r[i] = g_s[i]

    @pl.loop(1, 32)
    def _(d):
        h_copy(d).wait()

    gather_rows(tx, hid_r)
    loads[7].wait()
    u2, r2 = unit(tx[...])
    u2s[...] = u2
    r2s[...] = jnp.broadcast_to(r2, r2s.shape)
    n2s[...] = (u2 * mgn[...] + pe[...]).astype(BF)
    for t in range(3):
        mqkv[t] = nn(n2s[...], weight(t)).astype(BF)
    out = None
    for h in range(HEADS):
        probs = softmax(head_of(mqkv[0], h), mqkv[1])
        prob_t[h] = probs
        term = nn(probs.astype(BF), head_of(mqkv[2], h))
        out = term if out is None else out + term
    scatter_rows(mo_s, out)

    def m_copy(d):
        return remote(mo_s.at[fpeer(d)], mo_r.at[i], m_ss.at[d], m_rs.at[d], (fpeer(d), j))

    @pl.loop(1, 32)
    def _(d):
        m_copy(d).start()

    mo_r[i] = mo_s[i]

    @pl.loop(1, 32)
    def _(d):
        g_copy(d).wait()

    gather_rows(mof, g_r)
    mg = mof[...].astype(BF)
    dq, dk, dv = attend_back(mqkv[0], mqkv[1], mqkv[2], mg, prob_t, HEADS)
    dq, dk, dv = dq.astype(BF), dk.astype(BF), dv.astype(BF)
    dn2 = nt(dq, weight(0)) + nt(dk, weight(1)) + nt(dv, weight(2))
    u2 = u2s[...]
    gv1[...] = jnp.sum(dn2 * u2, axis=0, keepdims=True)
    back = unit_back(dn2, u2, r2s[:, 0:1], mgn[...])
    scatter_rows(lb_s, back)

    def l_copy(d):
        return remote(lb_s.at[fpeer(d)], lb_r.at[i], l_ss.at[d], l_rs.at[d], (fpeer(d), j))

    @pl.loop(1, 32)
    def _(d):
        l_copy(d).start()

    lb_r[i] = lb_s[i]

    @pl.loop(1, 32)
    def _(d):
        m_copy(d).wait()

    gather_rows(mof, mo_r)
    mo = tn(row_order(), mof[...].astype(BF)).astype(BF)

    n2p = nn(n2s[...], perm[...]).astype(BF)
    ctp = nn(cot[...], perm[...]).astype(BF)
    ax[0, 0:128] = n2p
    fxs[0] = n2p

    @pl.when(core == 0)
    def _():
        ax[1, 0:128] = n2p
        ay[0, 0:128] = dq
        ay[1, 0:128] = dk
        fxs[1] = ctp
        fys[0] = dv
        fys[1] = mo

    @pl.when(core == 1)
    def _():
        ax[1, 0:128] = ctp
        ay[0, 0:128] = dv
        ay[1, 0:128] = mo
        fxs[1] = n2p
        fys[0] = dq
        fys[1] = dk

    swap = [remote(fxs, ax.at[:, 128:256], x_ss.at[0], x_rs.at[0], sib),
            remote(fys, ay.at[:, 128:256], x_ss.at[1], x_rs.at[1], sib)]
    for c in swap:
        c.start()
    bo[...] = (hid[...].astype(F32) + nt(mo, weight(3))).astype(BF)
    for c in swap:
        c.wait()

    wa[...] = tn(ax[0], ay[0]).astype(BF)

    def a1_copy(d):
        to = pl.multiple_of(((x + d) % 4) * 320, 16)
        return remote(wa.at[pl.ds(to, 320)], ra1.at[d - 1], a1_ss.at[d], a1_rs.at[d], xpeer(d))

    def v_copy(src, dst, n, dev):
        return remote(src, dst, v_ss.at[n], v_rs.at[n], dev)

    for d in (1, 3, 2):
        a1_copy(d).start()
    gx = [v_copy(gv1, gr1.at[d - 1], d, xpeer(d)) for d in range(1, 4)]
    for c in gx:
        c.start()

    wb[...] = tn(ax[1], ay[1]).astype(BF)

    def b1_copy(d, n):
        to = pl.multiple_of(n * 320 + ((y + d) % 4) * 80, 16)
        return remote(wb.at[pl.ds(to, 80)], rb1.at[d - 1, n], b1_ss.at[d, n], b1_rs.at[d, n], ypeer(d))

    for d in (1, 3, 2):
        for n in range(4):
            b1_copy(d, n).start()

    @pl.loop(1, 32)
    def _(d):
        l_copy(d).wait()

    gather_rows(tx, lb_r)
    gh[...] = (cot[...].astype(F32) + tn(row_order(), tx[...].astype(BF))).astype(BF)
    ghb = gh[...]
    for hp, part in enumerate(split_pair(nn(ghb, spw[3]))):
        gs_s[hp * 4:hp * 4 + 4] = part.astype(BF).reshape(4, 32, 384)

    def gs_copy(d):
        return remote(gs_s.at[qpeer(d)], gs_r.at[j], gs_ss.at[d], gs_rs.at[d], (i, qpeer(d)))

    @pl.loop(1, 8)
    def _(d):
        gs_copy(d).start()

    gs_r[j] = gs_s[j]

    @pl.loop(1, 8)
    def _(d):
        gs_copy(d).wait()

    q, k, v = (qkv_r[:, t].reshape(256, 384) for t in range(3))
    for t, grad in enumerate(attend_back(q, k, v, gs_r[...].reshape(256, 384), prob_s, 2)):
        dq_s[:, t] = grad.astype(BF).reshape(8, 32, 384)

    def dq_copy(d):
        return remote(dq_s.at[qpeer(d)], dq_r.at[j], dq_ss.at[d], dq_rs.at[d], (i, qpeer(d)))

    @pl.loop(1, 8)
    def _(d):
        dq_copy(d).start()

    dq_r[j] = dq_s[j]

    for d in (1, 3, 2):
        a1_copy(d).wait()
    mine = pl.multiple_of(x * 320, 16)
    sa1[...] = (wa[pl.ds(mine, 320), :].astype(F32) + ra1[0].astype(F32) + ra1[1].astype(F32) + ra1[2].astype(F32)).astype(BF)

    def a2_copy(d):
        to = pl.multiple_of(((y + d) % 4) * 80, 16)
        return remote(sa1.at[pl.ds(to, 80)], ra2.at[d - 1], a2_ss.at[d], a2_rs.at[d], ypeer(d))

    for d in range(1, 4):
        a2_copy(d).start()
    for c in gx:
        c.wait()
    gv2[...] = gv1[...] + gr1[0] + gr1[1] + gr1[2]
    gy = [v_copy(gv2, gr2.at[d - 1], 3 + d, ypeer(d)) for d in range(1, 4)]
    for c in gy:
        c.start()

    for d in (1, 3, 2):
        for n in range(4):
            b1_copy(d, n).wait()
    for n in range(4):
        mine = pl.multiple_of(n * 320 + y * 80, 16)
        sb1[n] = (wb[pl.ds(mine, 80), :].astype(F32) + rb1[0, n].astype(F32) + rb1[1, n].astype(F32) + rb1[2, n].astype(F32)).astype(BF)

    def b2_copy(d):
        return remote(sb1.at[(x + d) % 4], rb2.at[d - 1], b2_ss.at[d], b2_rs.at[d], xpeer(d))

    for d in range(1, 4):
        b2_copy(d).start()
    for c in gy:
        c.wait()
    gv3[...] = gv2[...] + gr2[0] + gr2[1] + gr2[2]
    gz = [v_copy(gv3, gr3.at[d - 1], 6 + d, zpeer(d)) for d in range(1, 8)]
    for c in gz:
        c.start()

    @pl.loop(1, 8)
    def _(d):
        dq_copy(d).wait()

    total = None
    for t in range(3):
        grad = join_pair(dq_r[0:4, t].reshape(128, 384).astype(F32), dq_r[4:8, t].reshape(128, 384).astype(F32)).astype(BF)
        term = nt(grad, spw[t])
        total = term if total is None else total + term
    u1, r1 = unit(act[...].astype(F32))
    ig[...] = (gh[...].astype(F32) + unit_back(total, u1, r1, spg[...])).astype(BF)

    for d in range(1, 4):
        a2_copy(d).wait()
    for d in range(1, 4):
        b2_copy(d).wait()
    row = lax.broadcasted_iota(jnp.int32, (128, 80), 0)
    col = lax.broadcasted_iota(jnp.int32, (128, 80), 1)
    place = jnp.where((row % 16 < 10) & (col == (row // 16) * 10 + row % 16), 1.0, 0.0).astype(BF)
    mine = pl.multiple_of(y * 80, 16)
    s2 = sa1[pl.ds(mine, 80), :].astype(F32) + ra2[0].astype(F32) + ra2[1].astype(F32) + ra2[2].astype(F32)
    p3[:, 0:16] = nn(place, s2.astype(BF)).astype(BF).reshape(8, 16, W)
    s2 = sb1[x].astype(F32) + rb2[0].astype(F32) + rb2[1].astype(F32) + rb2[2].astype(F32)
    p3[:, 16:32] = nn(place, s2.astype(BF)).astype(BF).reshape(8, 16, W)

    def z_copy(d):
        return remote(p3.at[(z + d) % 8], r3.at[d - 1], r3_ss.at[d], r3_rs.at[d], zpeer(d))

    for d in range(1, 8):
        z_copy(d).start()
    for c in gz:
        c.wait()
    total = gv3[...]
    for d in range(7):
        total = total + gr3[d]
    gv4[...] = total
    last_v = v_copy(gv4, gr4, 14, sib)
    last_v.start()
    for d in range(1, 8):
        z_copy(d).wait()
    total = p3[z].astype(F32)
    for d in range(7):
        total = total + r3[d].astype(F32)
    fin[...] = total
    last = remote(fin, finr, e_ss.at[0], e_rs.at[0], sib)
    last.start()
    last_v.wait()
    factor = 1.0 / math.sqrt(128 * 256)
    gn[...] = (gv4[...] + gr4[...]) * factor
    last.wait()

    @pl.when(core == 0)
    def _():
        wg[0] = fin[0:5, :] * factor
        wg[1] = fin[16:21, :] * factor
        wg[2] = finr[0:5, :] * factor
        wg[3] = finr[16:21, :] * factor

    @pl.when(core == 1)
    def _():
        wg[0] = finr[5:10, :] * factor
        wg[1] = finr[21:26, :] * factor
        wg[2] = fin[5:10, :] * factor
        wg[3] = fin[21:26, :] * factor


def positional(frames, channels):
    freq = np.exp(np.arange(channels // 2, dtype=np.float32)[None, :] * np.float32(-2.0 * math.log(10000.0) / channels))
    phases = np.arange(frames, dtype=np.float32)[:, None] * freq.astype(np.float32)
    both = np.stack([np.sin(phases.astype(np.float64)), np.cos(phases.astype(np.float64))], axis=-1)
    return both.reshape(frames, channels).astype(np.float32)


def permutation():
    order = np.arange(C).reshape(2, 8, 2, 2, 4, 5)
    order = order.transpose(3, 0, 4, 1, 2, 5).reshape(-1)
    matrix = np.zeros((C, C), np.float32)
    matrix[order, np.arange(C)] = 1.0
    return matrix


def local(activations, cotangent, spatial_weights, spatial_gain, motion_weights, motion_gain):
    pe = jnp.asarray(positional(128, C))
    perm = jnp.asarray(permutation(), dtype=BF)
    V, D = pltpu.VMEM, pltpu.SemaphoreType.DMA
    any_, vmem = pl.BlockSpec(memory_space=pl.ANY), pl.BlockSpec(memory_space=pltpu.VMEM)
    scratch = [
        V((128, C), BF), V((128, C), BF), V((4, C, W), BF), V((4, 8, 160, W), BF), V((128, C), F32), V((C, C), BF),
        V((8, 3, 32, 384), BF), V((8, 3, 32, 384), BF), V((8, 32, 384), BF), V((8, 32, 384), BF), V((2, 256, 256), F32),
        V((128, C), BF), V((32, 4, C), BF), V((32, 4, C), BF), V((32, 4, W), BF), V((32, 4, W), BF),
        V((128, C), F32), V((128, C), BF), V((128, C), F32), V((128, 128), F32), V((3, 128, W), BF), V((4, 128, 128), F32),
        V((32, 4, W), BF), V((32, 4, W), BF), V((32, 4, C), BF), V((32, 4, C), BF), V((128, C), BF), V((128, W), F32),
        V((8, 32, 384), BF), V((8, 32, 384), BF), V((8, 3, 32, 384), BF), V((8, 3, 32, 384), BF),
        V((2, 128, C), BF), V((2, 128, W), BF), V((2, 256, C), BF), V((2, 256, W), BF), V((C, W), BF), V((C, W), BF),
        V((3, 320, W), BF), V((3, 4, 80, W), BF), V((320, W), BF), V((4, 80, W), BF), V((3, 80, W), BF), V((3, 80, W), BF),
        V((8, 32, W), BF), V((7, 32, W), BF), V((32, W), F32), V((32, W), F32),
        V((1, C), F32), V((3, 1, C), F32), V((1, C), F32), V((3, 1, C), F32), V((1, C), F32), V((7, 1, C), F32),
        V((1, C), F32), V((1, C), F32),
        D((9,)), D((16,)), D((16,)), D((16,)), D((16,)), D((8,)), D((8,)), D((8,)), D((8,)),
        D((32,)), D((32,)), D((32,)), D((32,)), D((32,)), D((32,)), D((32,)), D((32,)),
        D((8,)), D((8,)), D((8,)), D((8,)), D((2,)), D((2,)),
        D((4,)), D((4,)), D((4, 4)), D((4, 4)), D((4,)), D((4,)), D((4,)), D((4,)), D((8,)), D((8,)), D((1,)), D((1,)),
        D((16,)), D((16,)),
    ]
    block_output, input_grad, weight_grad, gain_all = pl.pallas_call(
        kernel,
        out_shape=(
            jax.ShapeDtypeStruct((128, C), BF),
            jax.ShapeDtypeStruct((128, C), BF),
            jax.ShapeDtypeStruct((4, 5, W), F32),
            jax.ShapeDtypeStruct((1, C), F32),
        ),
        in_specs=[any_, any_, any_, vmem, any_, vmem, any_, any_],
        out_specs=(vmem, vmem, vmem, vmem),
        scratch_shapes=scratch,
        compiler_params=pltpu.CompilerParams(
            has_side_effects=True, collective_id=0, vmem_limit_bytes=60 * 2 ** 20),
    )(
        activations.reshape(128, C), cotangent.reshape(128, C), spatial_weights, spatial_gain.reshape(1, C),
        motion_weights, motion_gain.reshape(1, C), pe, perm,
    )
    device = lax.axis_index("frame") * 8 + lax.axis_index("quad")
    gain_grad = lax.dynamic_slice_in_dim(gain_all.reshape(C), device * 5, 5)
    shape = activations.shape
    return block_output.reshape(shape), input_grad.reshape(shape), weight_grad, gain_grad


def solution(mesh):
    in_specs = (
        P("frame", "quad", None),
        P("frame", "quad", None),
        P(),
        P(),
        P(None, "quad", None),
        P(),
    )
    out_specs = (
        P("frame", "quad", None),
        P("frame", "quad", None),
        P(None, ("frame", "quad"), None),
        P(("frame", "quad")),
    )
    return jax.shard_map(local, mesh=mesh, in_specs=in_specs, out_specs=out_specs, check_vma=False)
```

```python
import math

import jax
import jax.numpy as jnp
import numpy as np
from jax import lax
from jax.experimental import pallas as pl
from jax.experimental.pallas import tpu as pltpu
from jax.sharding import PartitionSpec as P

HEADS = 4
HEAD_DIM = 160
EPSILON = 1e-05
SCALE = HEAD_DIM ** (-0.5)
C = 1280
W = 640
F32 = jnp.float32
BF = jnp.bfloat16
MESH = pl.DeviceIdType.MESH


def nn(a, b):
    return jnp.dot(a, b, preferred_element_type=F32)


def nt(a, b):
    return lax.dot_general(a, b, (((1,), (1,)), ((), ())), preferred_element_type=F32)


def tn(a, b):
    return lax.dot_general(a, b, (((0,), (0,)), ((), ())), preferred_element_type=F32)


def unit(x):
    xc = x - jnp.mean(x, axis=-1, keepdims=True)
    r = lax.rsqrt(jnp.mean(xc * xc, axis=-1, keepdims=True) + EPSILON)
    return xc * r, r


def unit_back(grad, u, r, gain):
    g = grad * gain
    return r * (g - jnp.mean(g, axis=-1, keepdims=True) - u * jnp.mean(g * u, axis=-1, keepdims=True))


def head_of(x, h):
    lane = lax.broadcasted_iota(jnp.int32, x.shape, 1)
    return jnp.where((lane >= h * HEAD_DIM) & (lane < (h + 1) * HEAD_DIM), x, jnp.zeros_like(x))


def split_pair(y):
    return y[:, :384], pltpu.roll(y, 320, 1)[:, :384]


def join_pair(a, b):
    pad = jnp.zeros((a.shape[0], 256), F32)
    left = jnp.concatenate([a, pad], axis=1)
    right = pltpu.roll(jnp.concatenate([b, pad], axis=1), 320, 1)
    lane = lax.broadcasted_iota(jnp.int32, left.shape, 1)
    return jnp.where(lane < 320, left, right)


def row_order():
    row = lax.broadcasted_iota(jnp.int32, (128, 128), 0)
    col = lax.broadcasted_iota(jnp.int32, (128, 128), 1)
    return jnp.where(col == (row % 4) * 32 + row // 4, 1.0, 0.0).astype(BF)


def scatter_rows(to, rows):
    for n in range(32):
        to[n] = rows[4 * n:4 * n + 4, :].astype(BF)


def gather_rows(rows, come):
    for n in range(32):
        rows[4 * n:4 * n + 4, :] = come[n].astype(F32)


def softmax(q, k):
    s = nt(q, k) * SCALE
    e = jnp.exp(s - jnp.max(s, axis=-1, keepdims=True))
    return e / jnp.sum(e, axis=-1, keepdims=True)


def attend_back(q, k, v, g, probs, heads):
    dq = dk = dv = None
    for h in range(heads):
        r = probs[h]
        dr = nt(head_of(g, h), v)
        delta = jnp.sum(r * dr, axis=-1, keepdims=True)
        ds = (r * (dr - delta) * SCALE).astype(BF)
        a, b, c = nn(ds, head_of(k, h)), tn(ds, head_of(q, h)), tn(r.astype(BF), head_of(g, h))
        dq, dk, dv = (a, b, c) if dq is None else (dq + a, dk + b, dv + c)
    return dq, dk, dv


def kernel(act_h, cot_h, spw_h, spg, mw_h, mgn, pe_h, perm_h,
           bo_h, ig_h, wg, gn,
           act, cot, spw, mw, pe, perm, bo, ig,
           qkv_s, qkv_r, o_s, o_r, prob_s,
           hid, hid_s, hid_r, ct_s, ct_r, ctt, tx, n2s, u2s, r2s, mqkv, prob_t,
           mo_s, mo_r, lb_s, lb_r, gh, mof,
           gs_s, gs_r, dq_s, dq_r,
           fx, fy, ax, ay, wa, wb, rax, ray, rbx, rby, sax, say, sbx, sby, tax, tay, tbx, tby, p3, r3,
           gv1, gr1, gv2, gr2,
           ld, st, w1_ss, w1_rs, w2_ss, w2_rs, w3_ss, w3_rs, w4_ss, w4_rs,
           q_ss, q_rs, o_ss, o_rs, h_ss, h_rs, c_ss, c_rs,
           m_ss, m_rs, l_ss, l_rs, gs_ss, gs_rs, dq_ss, dq_rs, x_ss, x_rs,
           ax_ss, ax_rs, ay_ss, ay_rs, bx_ss, bx_rs, by_ss, by_rs,
           ax2_ss, ax2_rs, ay2_ss, ay2_rs, bx2_ss, bx2_rs, by2_ss, by2_rs, r3_ss, r3_rs,
           v_ss, v_rs):
    i, j = lax.axis_index("frame"), lax.axis_index("quad")
    core, z, x_lo = i % 2, (i // 2) % 8, i // 16
    y, x_hi = j % 4, j // 4
    x = x_hi * 2 + x_lo
    zc = i % 16
    sib = (i + 1 - 2 * core, j)
    cross = ((1 - x_lo) * 16 + zc, (1 - x_hi) * 4 + y)
    beside = ((1 - x_lo) * 16 + zc, j)

    def fpeer(d):
        return (i + d) % 32

    def qpeer(d):
        return (j + d) % 8

    def xpeer(d):
        xx = (x + d) % 4
        return ((xx % 2) * 16 + zc, (xx // 2) * 4 + y)

    def ypeer(d):
        return (i, x_hi * 4 + (y + d) % 4)

    def remote(src, dst, ss, rs, dev):
        return pltpu.make_async_remote_copy(
            src_ref=src, dst_ref=dst, send_sem=ss, recv_sem=rs, device_id=dev, device_id_type=MESH)

    def arrived(part, ss, rs):
        pltpu.make_async_copy(part, part, ss).wait()
        pltpu.make_async_copy(part, part, rs).wait()

    bar = pltpu.get_barrier_semaphore()

    @pl.loop(1, 32)
    def _(d):
        pl.semaphore_signal(bar, inc=1, device_id=(fpeer(d), j), device_id_type=MESH)

    @pl.loop(1, 8)
    def _(d):
        pl.semaphore_signal(bar, inc=1, device_id=(i, qpeer(d)), device_id_type=MESH)

    pl.semaphore_signal(bar, inc=1, device_id=cross, device_id_type=MESH)

    half = pl.ds(pl.multiple_of(core * 80, 16), 80)
    loads = [
        pltpu.make_async_copy(act_h, act, ld.at[0]),
        pltpu.make_async_copy(spw_h.at[0], spw.at[0], ld.at[1]),
        pltpu.make_async_copy(spw_h.at[1], spw.at[1], ld.at[2]),
        pltpu.make_async_copy(spw_h.at[2], spw.at[2], ld.at[3]),
        pltpu.make_async_copy(cot_h, cot, ld.at[5]),
        pltpu.make_async_copy(mw_h.at[:, half], mw.at[:, j, half], ld.at[6]),
        pltpu.make_async_copy(spw_h.at[3], spw.at[3], ld.at[4]),
        pltpu.make_async_copy(pe_h, pe, ld.at[7]),
        pltpu.make_async_copy(perm_h, perm, ld.at[8]),
    ]
    for c in loads:
        c.start()

    loads[0].wait()
    u1, _ = unit(act[...].astype(F32))
    n1 = (u1 * spg[...].reshape(1, C)).astype(BF)
    for t in range(3):
        loads[1 + t].wait()
        for hp, part in enumerate(split_pair(nn(n1, spw[t]))):
            qkv_s[hp * 4:hp * 4 + 4, t] = part.astype(BF).reshape(4, 32, 384)
    pl.semaphore_wait(bar, 39)

    def q_copy(d):
        return remote(qkv_s.at[qpeer(d)], qkv_r.at[j], q_ss.at[0], q_rs.at[0], (i, qpeer(d)))

    @pl.loop(1, 8)
    def _(d):
        q_copy(d).start()

    def w1_copy(n, d):
        return remote(mw_h.at[n, half], mw.at[n, j, half], w1_ss.at[n], w1_rs.at[n], ypeer(d))

    def w2_copy(n):
        part = mw.at[n, pl.ds(x_hi * 4 + 2 * (1 - x_lo), 2), half]
        return remote(part, part, w2_ss.at[n], w2_rs.at[n], cross)

    def w3_copy(n):
        part = mw.at[n, pl.ds((1 - x_hi) * 4 + 2 * x_lo, 2), half]
        return remote(part, part, w3_ss.at[n], w3_rs.at[n], beside)

    def w4_copy(n):
        part = mw.at[n, :, half]
        return remote(part, part, w4_ss.at[n], w4_rs.at[n], sib)

    def w1_start(n):
        for d in (1, 3, 2):
            w1_copy(n, d).start()

    def w1_pass(n):
        arrived(mw.at[n, 0:3, half], w1_ss.at[n], w1_rs.at[n])
        w2_copy(n).start()

    def w2_pass(n):
        w2_copy(n).wait()
        w3_copy(n).start()

    def w3_pass(n):
        w3_copy(n).wait()
        w4_copy(n).start()

    w1_start(0)
    w1_start(1)

    loads[4].wait()
    scatter_rows(ct_s, nn(row_order(), cot[...]))

    def c_copy(d):
        return remote(ct_s.at[fpeer(d)], ct_r.at[i], c_ss.at[0], c_rs.at[0], (fpeer(d), j))

    @pl.loop(1, 32)
    def _(d):
        c_copy(d).start()

    ct_r[i] = ct_s[i]
    loads[5].wait()
    qkv_r[j] = qkv_s[j]

    arrived(qkv_r.at[0:7], q_ss.at[0], q_rs.at[0])

    q, k, v = (qkv_r[:, t].reshape(256, 384) for t in range(3))
    out = None
    for h in range(2):
        probs = softmax(head_of(q, h), k)
        prob_s[h] = probs
        term = nn(probs.astype(BF), head_of(v, h))
        out = term if out is None else out + term
    o_s[...] = out.astype(BF).reshape(8, 32, 384)

    def o_copy(d):
        return remote(o_s.at[qpeer(d)], o_r.at[j], o_ss.at[0], o_rs.at[0], (i, qpeer(d)))

    @pl.loop(1, 8)
    def _(d):
        o_copy(d).start()

    o_r[j] = o_s[j]
    w1_start(2)
    w1_start(3)
    w1_pass(0)
    w1_pass(1)

    arrived(o_r.at[0:7], o_ss.at[0], o_rs.at[0])

    loads[6].wait()
    so = join_pair(o_r[0:4].reshape(128, 384).astype(F32), o_r[4:8].reshape(128, 384).astype(F32)).astype(BF)
    hid[...] = (act[...].astype(F32) + nt(so, spw[3])).astype(BF)
    scatter_rows(hid_s, nn(row_order(), hid[...]))

    def h_copy(d):
        return remote(hid_s.at[fpeer(d)], hid_r.at[i], h_ss.at[0], h_rs.at[0], (fpeer(d), j))

    @pl.loop(1, 32)
    def _(d):
        h_copy(d).start()

    hid_r[i] = hid_s[i]

    w2_pass(0)

    arrived(ct_r.at[0:31], c_ss.at[0], c_rs.at[0])

    gather_rows(tx, ct_r)
    ctt[...] = tx[...].astype(BF)
    loads[8].wait()
    ctp = nn(ctt[...], perm[...]).astype(BF)

    @pl.when(core == 0)
    def _():
        ax[0, 0:128] = ctp

    @pl.when(core == 1)
    def _():
        fx[0] = ctp

    w2_pass(1)
    w3_pass(0)
    w1_pass(2)
    w3_pass(1)
    w1_pass(3)
    w2_pass(2)
    w3_pass(2)
    w2_pass(3)
    w3_pass(3)

    def weight(n):
        return mw[n].reshape(C, W)

    arrived(hid_r.at[0:31], h_ss.at[0], h_rs.at[0])

    gather_rows(tx, hid_r)
    loads[7].wait()
    gain = mgn[...].reshape(1, C)
    u2, r2 = unit(tx[...])
    u2s[...] = u2
    r2s[...] = jnp.broadcast_to(r2, r2s.shape)
    n2s[...] = (u2 * gain + pe[...]).astype(BF)
    for t in range(3):
        w4_copy(t).wait()
        mqkv[t] = nn(n2s[...], weight(t)).astype(BF)
    out = None
    for h in range(HEADS):
        probs = softmax(head_of(mqkv[0], h), mqkv[1])
        prob_t[h] = probs
        term = nn(probs.astype(BF), head_of(mqkv[2], h))
        out = term if out is None else out + term
    mo_t = out.astype(BF)
    scatter_rows(mo_s, out)

    def m_copy(d):
        return remote(mo_s.at[fpeer(d)], mo_r.at[i], m_ss.at[0], m_rs.at[0], (fpeer(d), j))

    @pl.loop(1, 32)
    def _(d):
        m_copy(d).start()

    mo_r[i] = mo_s[i]

    w4_copy(3).wait()
    mg = nn(ctt[...], weight(3)).astype(BF)
    dv = None
    for h in range(HEADS):
        term = tn(prob_t[h].astype(BF), head_of(mg, h))
        dv = term if dv is None else dv + term
    dv = dv.astype(BF)
    n2p = nn(n2s[...], perm[...]).astype(BF)
    ax[1, 0:128] = n2p
    fx[1] = n2p

    @pl.when(core == 0)
    def _():
        ay[0, 0:128] = mo_t
        fx[0] = n2p
        fy[0] = dv

    @pl.when(core == 1)
    def _():
        ax[0, 0:128] = n2p
        ay[0, 0:128] = dv
        fy[0] = mo_t

    swap = [remote(fx.at[0], ax.at[0, 128:256], x_ss.at[0], x_rs.at[0], sib),
            remote(fy.at[0], ay.at[0, 128:256], x_ss.at[1], x_rs.at[1], sib),
            remote(fx.at[1], ax.at[1, 128:256], x_ss.at[2], x_rs.at[2], sib)]
    for c in swap:
        c.start()

    dq = dk = None
    for h in range(HEADS):
        r = prob_t[h]
        dr = nt(head_of(mg, h), mqkv[2])
        delta = jnp.sum(r * dr, axis=-1, keepdims=True)
        ds = (r * (dr - delta) * SCALE).astype(BF)
        a, b = nn(ds, head_of(mqkv[1], h)), tn(ds, head_of(mqkv[0], h))
        dq, dk = (a, b) if dq is None else (dq + a, dk + b)
    dq, dk = dq.astype(BF), dk.astype(BF)

    @pl.when(core == 0)
    def _():
        ay[1, 0:128] = dq
        fy[1] = dk

    @pl.when(core == 1)
    def _():
        ay[1, 0:128] = dk
        fy[1] = dq

    swap_b = remote(fy.at[1], ay.at[1, 128:256], x_ss.at[3], x_rs.at[3], sib)
    swap_b.start()
    for c in swap:
        c.wait()
    wa[...] = tn(ax[0], ay[0]).astype(BF).reshape(4, 4, 80, W)

    def ax_copy(d):
        return remote(wa.at[(x + d) % 4, :, :, 0:384], rax.at[d - 1], ax_ss.at[0], ax_rs.at[0], xpeer(d))

    def ay_copy(d):
        return remote(wa.at[:, (y + d) % 4, :, 384:640], ray.at[d - 1], ay_ss.at[0], ay_rs.at[0], ypeer(d))

    for d in (1, 3, 2):
        ax_copy(d).start()
        ay_copy(d).start()

    dn2 = nt(dq, weight(0)) + nt(dk, weight(1)) + nt(dv, weight(2))
    u2 = u2s[...]
    gv1[...] = jnp.sum(dn2 * u2, axis=0, keepdims=True)
    back = ctt[...].astype(F32) + unit_back(dn2, u2, r2s[:, 0:1], gain)
    scatter_rows(lb_s, back)

    def l_copy(d):
        return remote(lb_s.at[fpeer(d)], lb_r.at[i], l_ss.at[0], l_rs.at[0], (fpeer(d), j))

    @pl.loop(1, 32)
    def _(d):
        l_copy(d).start()

    lb_r[i] = lb_s[i]

    def v_copy(src, dst, n, dev):
        return remote(src, dst, v_ss.at[n], v_rs.at[n], dev)

    gx = [v_copy(gv1, gr1.at[d - 1], 0, xpeer(d)) for d in range(1, 4)]
    for c in gx:
        c.start()

    swap_b.wait()
    wb[...] = tn(ax[1], ay[1]).astype(BF).reshape(4, 4, 80, W)

    arrived(mo_r.at[0:31], m_ss.at[0], m_rs.at[0])

    gather_rows(mof, mo_r)
    mo = tn(row_order(), mof[...].astype(BF)).astype(BF)
    bo[...] = (hid[...].astype(F32) + nt(mo, weight(3))).astype(BF)
    bo_store = pltpu.make_async_copy(bo, bo_h, st.at[0])
    bo_store.start()

    def bx_copy(d):
        return remote(wb.at[(x + d) % 4, :, :, 0:256], rbx.at[d - 1], bx_ss.at[0], bx_rs.at[0], xpeer(d))

    def by_copy(d):
        return remote(wb.at[:, (y + d) % 4, :, 256:640], rby.at[d - 1], by_ss.at[0], by_rs.at[0], ypeer(d))

    arrived(lb_r.at[0:31], l_ss.at[0], l_rs.at[0])

    gather_rows(tx, lb_r)
    gh[...] = tn(row_order(), tx[...].astype(BF)).astype(BF)
    for hp, part in enumerate(split_pair(nn(gh[...], spw[3]))):
        gs_s[hp * 4:hp * 4 + 4] = part.astype(BF).reshape(4, 32, 384)

    def gs_copy(d):
        return remote(gs_s.at[qpeer(d)], gs_r.at[j], gs_ss.at[0], gs_rs.at[0], (i, qpeer(d)))

    @pl.loop(1, 8)
    def _(d):
        gs_copy(d).start()

    gs_r[j] = gs_s[j]
    for d in (1, 3, 2):
        bx_copy(d).start()
        by_copy(d).start()

    arrived(gs_r.at[0:7], gs_ss.at[0], gs_rs.at[0])

    q, k, v = (qkv_r[:, t].reshape(256, 384) for t in range(3))
    for t, grad in enumerate(attend_back(q, k, v, gs_r[...].reshape(256, 384), prob_s, 2)):
        dq_s[:, t] = grad.astype(BF).reshape(8, 32, 384)

    def dq_copy(d):
        return remote(dq_s.at[qpeer(d)], dq_r.at[j], dq_ss.at[0], dq_rs.at[0], (i, qpeer(d)))

    @pl.loop(1, 8)
    def _(d):
        dq_copy(d).start()

    dq_r[j] = dq_s[j]

    def add4(own, parts):
        return own.astype(F32) + parts[0].astype(F32) + parts[1].astype(F32) + parts[2].astype(F32)

    arrived(rax, ax_ss.at[0], ax_rs.at[0])
    arrived(ray, ay_ss.at[0], ay_rs.at[0])
    sax[...] = add4(wa[x, :, :, 0:384], rax).astype(BF)
    say[...] = add4(wa[:, y, :, 384:640], ray).astype(BF)

    def ax2_copy(d):
        return remote(sax.at[(y + d) % 4], tax.at[d - 1], ax2_ss.at[0], ax2_rs.at[0], ypeer(d))

    def ay2_copy(d):
        return remote(say.at[(x + d) % 4], tay.at[d - 1], ay2_ss.at[0], ay2_rs.at[0], xpeer(d))

    for d in (1, 3, 2):
        ax2_copy(d).start()
        ay2_copy(d).start()
    arrived(gr1, v_ss.at[0], v_rs.at[0])
    gv2[...] = gv1[...] + gr1[0] + gr1[1] + gr1[2]
    gy = [v_copy(gv2, gr2.at[d - 1], 1, ypeer(d)) for d in range(1, 4)]
    for c in gy:
        c.start()

    arrived(rbx, bx_ss.at[0], bx_rs.at[0])
    arrived(rby, by_ss.at[0], by_rs.at[0])
    sbx[...] = add4(wb[x, :, :, 0:256], rbx).astype(BF)
    sby[...] = add4(wb[:, y, :, 256:640], rby).astype(BF)

    def bx2_copy(d):
        return remote(sbx.at[(y + d) % 4], tbx.at[d - 1], bx2_ss.at[0], bx2_rs.at[0], ypeer(d))

    def by2_copy(d):
        return remote(sby.at[(x + d) % 4], tby.at[d - 1], by2_ss.at[0], by2_rs.at[0], xpeer(d))

    for d in (1, 3, 2):
        bx2_copy(d).start()
        by2_copy(d).start()

    arrived(dq_r.at[0:7], dq_ss.at[0], dq_rs.at[0])

    total = None
    for t in range(3):
        grad = join_pair(dq_r[0:4, t].reshape(128, 384).astype(F32), dq_r[4:8, t].reshape(128, 384).astype(F32)).astype(BF)
        term = nt(grad, spw[t])
        total = term if total is None else total + term
    u1, r1 = unit(act[...].astype(F32))
    ig[...] = (gh[...].astype(F32) + unit_back(total, u1, r1, spg[...].reshape(1, C))).astype(BF)
    ig_store = pltpu.make_async_copy(ig, ig_h, st.at[1])
    ig_store.start()

    row = lax.broadcasted_iota(jnp.int32, (256, 80), 0)
    col = lax.broadcasted_iota(jnp.int32, (256, 80), 1)
    first = jnp.where((row % 16 < 5) & (col == (row // 16) * 5 + row % 16), 1.0, 0.0).astype(BF)
    second = jnp.where((row % 16 >= 5) & (row % 16 < 10) & (col == (row // 16) * 5 + row % 16 - 5), 1.0, 0.0).astype(BF)
    arrived(gr2, v_ss.at[1], v_rs.at[1])
    gv = gv2[...] + gr2[0] + gr2[1] + gr2[2]
    arrived(tax, ax2_ss.at[0], ax2_rs.at[0])
    arrived(tay, ay2_ss.at[0], ay2_rs.at[0])
    sum_a = jnp.concatenate([add4(sax[y], tax), add4(say[x], tay)], axis=1).astype(BF)
    arrived(tbx, bx2_ss.at[0], bx2_rs.at[0])
    arrived(tby, by2_ss.at[0], by2_rs.at[0])
    sum_b = jnp.concatenate([add4(sbx[y], tbx), add4(sby[x], tby)], axis=1).astype(BF)
    slabs = nn(first, sum_a) + nn(second, sum_b)
    row = lax.broadcasted_iota(jnp.int32, (256, W), 0) % 16
    slabs = jnp.where(row == 10, gv[:, :W], jnp.where(row == 11, gv[:, W:], slabs))
    p3[...] = slabs.astype(BF).reshape(16, 16, W)

    def z_copy(d):
        to = (zc + d) % 16
        return remote(p3.at[to], r3.at[zc], r3_ss.at[0], r3_rs.at[0], (x_lo * 16 + to, j))

    @pl.loop(1, 16)
    def _(d):
        z_copy(d).start()

    r3[zc] = p3[zc]

    arrived(r3.at[0:15], r3_ss.at[0], r3_rs.at[0])

    factor = 1.0 / math.sqrt(128 * 256)
    sums = []
    for c in range(2):
        total = r3[c].astype(F32)
        for n in range(1, 8):
            total = total + r3[2 * n + c].astype(F32)
        sums.append(total * factor)
    wg[:, 0] = sums[0][5:10]
    wg[:, 1] = sums[1][5:10]
    wg[:, 2] = sums[1][0:5]
    wg[:, 3] = sums[0][0:5]
    both = sums[0] + sums[1]
    gn[...] = jnp.concatenate([both[10:11], both[11:12]], axis=1)
    bo_store.wait()
    ig_store.wait()


def finish(bo_h, ig_h, wg_h, gn, bo, ig, wg, gg, bo_v, ig_v, wg_v, sems):
    moves = [(bo_h, bo_v, bo), (ig_h, ig_v, ig), (wg_h, wg_v, wg)]
    come = [pltpu.make_async_copy(a, b, sems.at[0, n]) for n, (a, b, _) in enumerate(moves)]
    go = [pltpu.make_async_copy(b, c, sems.at[1, n]) for n, (_, b, c) in enumerate(moves)]
    for c in come:
        c.start()
    device = lax.axis_index("frame") * 8 + lax.axis_index("quad")
    gg[...] = pltpu.roll(gn[...], C - device * 5, 1)[0, :5]
    for a, b in zip(come, go):
        a.wait()
        b.start()
    for c in go:
        c.wait()


def positional(frames, channels):
    freq = np.exp(np.arange(channels // 2, dtype=np.float32)[None, :] * np.float32(-2.0 * math.log(10000.0) / channels))
    phases = np.arange(frames, dtype=np.float32)[:, None] * freq.astype(np.float32)
    both = np.stack([np.sin(phases.astype(np.float64)), np.cos(phases.astype(np.float64))], axis=-1)
    return both.reshape(frames, channels).astype(np.float32)


def permutation():
    order = np.arange(C).reshape(2, 8, 2, 2, 4, 5)
    order = order.transpose(3, 0, 4, 1, 2, 5).reshape(-1)
    matrix = np.zeros((C, C), np.float32)
    matrix[order, np.arange(C)] = 1.0
    return matrix


def local(activations, cotangent, spatial_weights, spatial_gain, motion_weights, motion_gain):
    pe = jnp.asarray(positional(128, C))
    perm = jnp.asarray(permutation(), dtype=BF)
    V, D = pltpu.VMEM, pltpu.SemaphoreType.DMA
    any_, vmem = pl.BlockSpec(memory_space=pl.ANY), pl.BlockSpec(memory_space=pltpu.VMEM)
    scratch = [
        V((128, C), BF), V((128, C), BF), V((4, C, W), BF), V((4, 8, 160, W), BF), V((128, C), F32), V((C, C), BF),
        V((128, C), BF), V((128, C), BF),
        V((8, 3, 32, 384), BF), V((8, 3, 32, 384), BF), V((8, 32, 384), BF), V((8, 32, 384), BF), V((2, 256, 256), F32),
        V((128, C), BF), V((32, 4, C), BF), V((32, 4, C), BF), V((32, 4, C), BF), V((32, 4, C), BF), V((128, C), BF),
        V((128, C), F32), V((128, C), BF), V((128, C), F32), V((128, 128), F32), V((3, 128, W), BF), V((4, 128, 128), F32),
        V((32, 4, W), BF), V((32, 4, W), BF), V((32, 4, C), BF), V((32, 4, C), BF), V((128, C), BF), V((128, W), F32),
        V((8, 32, 384), BF), V((8, 32, 384), BF), V((8, 3, 32, 384), BF), V((8, 3, 32, 384), BF),
        V((2, 128, C), BF), V((2, 128, W), BF), V((2, 256, C), BF), V((2, 256, W), BF),
        V((4, 4, 80, W), BF), V((4, 4, 80, W), BF),
        V((3, 4, 80, 384), BF), V((3, 4, 80, 256), BF), V((3, 4, 80, 256), BF), V((3, 4, 80, 384), BF),
        V((4, 80, 384), BF), V((4, 80, 256), BF), V((4, 80, 256), BF), V((4, 80, 384), BF),
        V((3, 80, 384), BF), V((3, 80, 256), BF), V((3, 80, 256), BF), V((3, 80, 384), BF),
        V((16, 16, W), BF), V((16, 16, W), BF),
        V((1, C), F32), V((3, 1, C), F32), V((1, C), F32), V((3, 1, C), F32),
        D((9,)), D((2,))] + [D((4,))] * 8 + [D((1,))] * 16 + [D((4,)), D((4,))] + [D((1,))] * 18 + [
        D((2,)), D((2,)),
    ]
    results = (
        jax.ShapeDtypeStruct((128, C), BF),
        jax.ShapeDtypeStruct((128, C), BF),
        jax.ShapeDtypeStruct((5, 4, W), F32),
    )
    block_output, input_grad, weight_grad, gain_all = pl.pallas_call(
        kernel,
        out_shape=results + (jax.ShapeDtypeStruct((1, C), F32),),
        in_specs=[any_, any_, any_, vmem, any_, vmem, any_, any_],
        out_specs=(any_, any_, vmem, vmem),
        scratch_shapes=scratch,
        compiler_params=pltpu.CompilerParams(
            has_side_effects=True, collective_id=0, vmem_limit_bytes=60 * 2 ** 20),
    )(
        activations.reshape(128, C), cotangent.reshape(128, C), spatial_weights, spatial_gain,
        motion_weights, motion_gain, pe, perm,
    )
    block_output, input_grad, weight_grad, gain_grad = pl.pallas_call(
        finish,
        out_shape=results + (jax.ShapeDtypeStruct((5,), F32),),
        in_specs=[any_, any_, any_, vmem],
        out_specs=(any_, any_, any_, vmem),
        scratch_shapes=[V((128, C), BF), V((128, C), BF), V((5, 4, W), F32), D((2, 3))],
        compiler_params=pltpu.CompilerParams(vmem_limit_bytes=60 * 2 ** 20),
    )(block_output, input_grad, weight_grad, gain_all)
    shape = activations.shape
    return block_output.reshape(shape), input_grad.reshape(shape), weight_grad.transpose(1, 0, 2), gain_grad


def solution(mesh):
    in_specs = (
        P("frame", "quad", None),
        P("frame", "quad", None),
        P(),
        P(),
        P(None, "quad", None),
        P(),
    )
    out_specs = (
        P("frame", "quad", None),
        P("frame", "quad", None),
        P(None, ("frame", "quad"), None),
        P(("frame", "quad")),
    )
    return jax.shard_map(local, mesh=mesh, in_specs=in_specs, out_specs=out_specs, check_vma=False)
```

```python
import math

import jax
import jax.numpy as jnp
import numpy as np
from jax import lax
from jax.experimental import pallas as pl
from jax.experimental.pallas import tpu as pltpu
from jax.sharding import PartitionSpec as P

HEADS = 4
HEAD_DIM = 160
EPSILON = 1e-05
SCALE = HEAD_DIM ** (-0.5)
C = 1280
W = 640
F32 = jnp.float32
BF = jnp.bfloat16
MESH = pl.DeviceIdType.MESH


def nn(a, b):
    return jnp.dot(a, b, preferred_element_type=F32)


def nt(a, b):
    return lax.dot_general(a, b, (((1,), (1,)), ((), ())), preferred_element_type=F32)


def tn(a, b):
    return lax.dot_general(a, b, (((0,), (0,)), ((), ())), preferred_element_type=F32)


def unit(x):
    xc = x - jnp.mean(x, axis=-1, keepdims=True)
    r = lax.rsqrt(jnp.mean(xc * xc, axis=-1, keepdims=True) + EPSILON)
    return xc * r, r


def unit_back(grad, u, r, gain):
    g = grad * gain
    return r * (g - jnp.mean(g, axis=-1, keepdims=True) - u * jnp.mean(g * u, axis=-1, keepdims=True))


def head_of(x, h):
    lane = lax.broadcasted_iota(jnp.int32, x.shape, 1)
    return jnp.where((lane >= h * HEAD_DIM) & (lane < (h + 1) * HEAD_DIM), x, jnp.zeros_like(x))


def split_pair(y):
    return y[:, :384], pltpu.roll(y, 320, 1)[:, :384]


def join_pair(a, b):
    pad = jnp.zeros((a.shape[0], 256), F32)
    left = jnp.concatenate([a, pad], axis=1)
    right = pltpu.roll(jnp.concatenate([b, pad], axis=1), 320, 1)
    lane = lax.broadcasted_iota(jnp.int32, left.shape, 1)
    return jnp.where(lane < 320, left, right)


def row_order():
    row = lax.broadcasted_iota(jnp.int32, (128, 128), 0)
    col = lax.broadcasted_iota(jnp.int32, (128, 128), 1)
    return jnp.where(col == (row % 4) * 32 + row // 4, 1.0, 0.0).astype(BF)


def scatter_rows(to, rows):
    for n in range(32):
        to[n] = rows[4 * n:4 * n + 4, :].astype(BF)


def gather_rows(rows, come):
    for n in range(32):
        rows[4 * n:4 * n + 4, :] = come[n].astype(F32)


def softmax(q, k):
    s = nt(q, k) * SCALE
    e = jnp.exp(s - jnp.max(s, axis=-1, keepdims=True))
    return e / jnp.sum(e, axis=-1, keepdims=True)


def attend_back(q, k, v, g, probs, heads):
    dq = dk = dv = None
    for h in range(heads):
        r = probs[h]
        dr = nt(head_of(g, h), v)
        delta = jnp.sum(r * dr, axis=-1, keepdims=True)
        ds = (r * (dr - delta) * SCALE).astype(BF)
        a, b, c = nn(ds, head_of(k, h)), tn(ds, head_of(q, h)), tn(r.astype(BF), head_of(g, h))
        dq, dk, dv = (a, b, c) if dq is None else (dq + a, dk + b, dv + c)
    return dq, dk, dv


def kernel(act_h, cot_h, spw_h, spg, mw_h, mgn, pe_h, perm_h,
           bo_h, ig_h, wg, gn,
           act, cot, spw, mw, pe, perm, bo, ig,
           qkv_s, qkv_r, o_s, o_r, prob_s,
           hid, hid_s, hid_r, ct_s, ct_r, ctt, tx, n2s, u2s, r2s, mqkv, prob_t,
           mo_s, mo_r, lb_s, lb_r, gh, mof,
           gs_s, gs_r, dq_s, dq_r,
           fx, fy, ax, ay, wa, wb, rax, ray, rbx, rby, sax, say, sbx, sby, tax, tay, tbx, tby, p3, r3,
           gv1, gr1, gv2, gr2,
           ld, st, w1_ss, w1_rs, w2_ss, w2_rs, w3_ss, w3_rs, w4_ss, w4_rs,
           q_ss, q_rs, o_ss, o_rs, h_ss, h_rs, c_ss, c_rs,
           m_ss, m_rs, l_ss, l_rs, gs_ss, gs_rs, dq_ss, dq_rs, x_ss, x_rs,
           ax_ss, ax_rs, ay_ss, ay_rs, bx_ss, bx_rs, by_ss, by_rs,
           ax2_ss, ax2_rs, ay2_ss, ay2_rs, bx2_ss, bx2_rs, by2_ss, by2_rs, r3_ss, r3_rs,
           v_ss, v_rs):
    i, j = lax.axis_index("frame"), lax.axis_index("quad")
    core, z, x_lo = i % 2, (i // 2) % 8, i // 16
    y, x_hi = j % 4, j // 4
    x = x_hi * 2 + x_lo
    zc = i % 16
    sib = (i + 1 - 2 * core, j)
    cross = ((1 - x_lo) * 16 + zc, (1 - x_hi) * 4 + y)
    beside = ((1 - x_lo) * 16 + zc, j)

    def fpeer(d):
        return (i + d) % 32

    def qpeer(d):
        return (j + d) % 8

    def xpeer(d):
        xx = (x + d) % 4
        return ((xx % 2) * 16 + zc, (xx // 2) * 4 + y)

    def ypeer(d):
        return (i, x_hi * 4 + (y + d) % 4)

    def remote(src, dst, ss, rs, dev):
        return pltpu.make_async_remote_copy(
            src_ref=src, dst_ref=dst, send_sem=ss, recv_sem=rs, device_id=dev, device_id_type=MESH)

    def arrived(part, ss, rs):
        pltpu.make_async_copy(part, part, ss).wait()
        pltpu.make_async_copy(part, part, rs).wait()

    bar = pltpu.get_barrier_semaphore()

    @pl.loop(1, 32)
    def _(d):
        pl.semaphore_signal(bar, inc=1, device_id=(fpeer(d), j), device_id_type=MESH)

    @pl.loop(1, 8)
    def _(d):
        pl.semaphore_signal(bar, inc=1, device_id=(i, qpeer(d)), device_id_type=MESH)

    pl.semaphore_signal(bar, inc=1, device_id=cross, device_id_type=MESH)

    half = pl.ds(pl.multiple_of(core * 80, 16), 80)
    loads = [
        pltpu.make_async_copy(act_h, act, ld.at[0]),
        pltpu.make_async_copy(spw_h.at[0], spw.at[0], ld.at[1]),
        pltpu.make_async_copy(spw_h.at[1], spw.at[1], ld.at[2]),
        pltpu.make_async_copy(spw_h.at[2], spw.at[2], ld.at[3]),
        pltpu.make_async_copy(cot_h, cot, ld.at[5]),
        pltpu.make_async_copy(mw_h.at[:, half], mw.at[:, j, half], ld.at[6]),
        pltpu.make_async_copy(spw_h.at[3], spw.at[3], ld.at[4]),
        pltpu.make_async_copy(pe_h, pe, ld.at[7]),
        pltpu.make_async_copy(perm_h, perm, ld.at[8]),
    ]
    for c in loads:
        c.start()

    loads[0].wait()
    u1, _ = unit(act[...].astype(F32))
    n1 = (u1 * spg[...].reshape(1, C)).astype(BF)
    for t in range(3):
        loads[1 + t].wait()
        for hp, part in enumerate(split_pair(nn(n1, spw[t]))):
            qkv_s[hp * 4:hp * 4 + 4, t] = part.astype(BF).reshape(4, 32, 384)
    pl.semaphore_wait(bar, 39)

    def q_copy(d):
        return remote(qkv_s.at[qpeer(d)], qkv_r.at[j], q_ss.at[0], q_rs.at[0], (i, qpeer(d)))

    @pl.loop(1, 8)
    def _(d):
        q_copy(d).start()

    def w1_copy(n, d):
        return remote(mw_h.at[n, half], mw.at[n, j, half], w1_ss.at[n], w1_rs.at[n], ypeer(d))

    def w2_copy(n):
        part = mw.at[n, pl.ds(x_hi * 4 + 2 * (1 - x_lo), 2), half]
        return remote(part, part, w2_ss.at[n], w2_rs.at[n], cross)

    def w3_copy(n):
        part = mw.at[n, pl.ds((1 - x_hi) * 4 + 2 * x_lo, 2), half]
        return remote(part, part, w3_ss.at[n], w3_rs.at[n], beside)

    def w4_copy(n):
        part = mw.at[n, :, half]
        return remote(part, part, w4_ss.at[n], w4_rs.at[n], sib)

    def w1_start(n):
        for d in (1, 3, 2):
            w1_copy(n, d).start()

    def w1_pass(n):
        arrived(mw.at[n, 0:3, half], w1_ss.at[n], w1_rs.at[n])
        w2_copy(n).start()

    def w2_pass(n):
        w2_copy(n).wait()
        w3_copy(n).start()

    def w3_pass(n):
        w3_copy(n).wait()
        w4_copy(n).start()

    w1_start(0)
    w1_start(1)

    loads[4].wait()
    scatter_rows(ct_s, nn(row_order(), cot[...]))

    def c_copy(d):
        return remote(ct_s.at[fpeer(d)], ct_r.at[i], c_ss.at[0], c_rs.at[0], (fpeer(d), j))

    @pl.loop(1, 32)
    def _(d):
        c_copy(d).start()

    ct_r[i] = ct_s[i]
    loads[5].wait()
    qkv_r[j] = qkv_s[j]

    arrived(qkv_r.at[0:7], q_ss.at[0], q_rs.at[0])

    q, k, v = (qkv_r[:, t].reshape(256, 384) for t in range(3))
    out = None
    for h in range(2):
        probs = softmax(head_of(q, h), k)
        prob_s[h] = probs
        term = nn(probs.astype(BF), head_of(v, h))
        out = term if out is None else out + term
    o_s[...] = out.astype(BF).reshape(8, 32, 384)

    def o_copy(d):
        return remote(o_s.at[qpeer(d)], o_r.at[j], o_ss.at[0], o_rs.at[0], (i, qpeer(d)))

    @pl.loop(1, 8)
    def _(d):
        o_copy(d).start()

    o_r[j] = o_s[j]
    w1_start(2)
    w1_start(3)
    w1_pass(0)
    w1_pass(1)
    w2_pass(0)

    arrived(o_r.at[0:7], o_ss.at[0], o_rs.at[0])

    loads[6].wait()
    so = join_pair(o_r[0:4].reshape(128, 384).astype(F32), o_r[4:8].reshape(128, 384).astype(F32)).astype(BF)
    hid[...] = (act[...].astype(F32) + nt(so, spw[3])).astype(BF)
    scatter_rows(hid_s, nn(row_order(), hid[...]))

    def h_copy(d):
        return remote(hid_s.at[fpeer(d)], hid_r.at[i], h_ss.at[0], h_rs.at[0], (fpeer(d), j))

    @pl.loop(1, 32)
    def _(d):
        h_copy(d).start()

    hid_r[i] = hid_s[i]

    arrived(ct_r.at[0:31], c_ss.at[0], c_rs.at[0])

    gather_rows(tx, ct_r)
    ctt[...] = tx[...].astype(BF)
    loads[8].wait()
    ctp = nn(ctt[...], perm[...]).astype(BF)

    @pl.when(core == 0)
    def _():
        ax[0, 0:128] = ctp

    @pl.when(core == 1)
    def _():
        fx[0] = ctp

    w2_pass(1)
    w1_pass(2)
    w3_pass(0)
    w1_pass(3)
    w3_pass(1)
    w2_pass(2)
    w2_pass(3)
    w3_pass(2)

    def weight(n):
        return mw[n].reshape(C, W)

    arrived(hid_r.at[0:31], h_ss.at[0], h_rs.at[0])

    gather_rows(tx, hid_r)
    loads[7].wait()
    gain = mgn[...].reshape(1, C)
    u2, r2 = unit(tx[...])
    u2s[...] = u2
    r2s[...] = jnp.broadcast_to(r2, r2s.shape)
    n2s[...] = (u2 * gain + pe[...]).astype(BF)
    for t in range(3):
        w4_copy(t).wait()
        mqkv[t] = nn(n2s[...], weight(t)).astype(BF)
    out = None
    for h in range(HEADS):
        probs = softmax(head_of(mqkv[0], h), mqkv[1])
        prob_t[h] = probs
        term = nn(probs.astype(BF), head_of(mqkv[2], h))
        out = term if out is None else out + term
    mo_t = out.astype(BF)
    scatter_rows(mo_s, out)

    def m_copy(d):
        return remote(mo_s.at[fpeer(d)], mo_r.at[i], m_ss.at[0], m_rs.at[0], (fpeer(d), j))

    @pl.loop(1, 32)
    def _(d):
        m_copy(d).start()

    mo_r[i] = mo_s[i]

    w3_pass(3)
    w4_copy(3).wait()
    mg = nn(ctt[...], weight(3)).astype(BF)
    dv = None
    for h in range(HEADS):
        term = tn(prob_t[h].astype(BF), head_of(mg, h))
        dv = term if dv is None else dv + term
    dv = dv.astype(BF)
    n2p = nn(n2s[...], perm[...]).astype(BF)
    ax[1, 0:128] = n2p
    fx[1] = n2p

    @pl.when(core == 0)
    def _():
        ay[0, 0:128] = mo_t
        fx[0] = n2p
        fy[0] = dv

    @pl.when(core == 1)
    def _():
        ax[0, 0:128] = n2p
        ay[0, 0:128] = dv
        fy[0] = mo_t

    swap = [remote(fx.at[0], ax.at[0, 128:256], x_ss.at[0], x_rs.at[0], sib),
            remote(fy.at[0], ay.at[0, 128:256], x_ss.at[1], x_rs.at[1], sib),
            remote(fx.at[1], ax.at[1, 128:256], x_ss.at[2], x_rs.at[2], sib)]
    for c in swap:
        c.start()

    dq = dk = None
    for h in range(HEADS):
        r = prob_t[h]
        dr = nt(head_of(mg, h), mqkv[2])
        delta = jnp.sum(r * dr, axis=-1, keepdims=True)
        ds = (r * (dr - delta) * SCALE).astype(BF)
        a, b = nn(ds, head_of(mqkv[1], h)), tn(ds, head_of(mqkv[0], h))
        dq, dk = (a, b) if dq is None else (dq + a, dk + b)
    dq, dk = dq.astype(BF), dk.astype(BF)

    @pl.when(core == 0)
    def _():
        ay[1, 0:128] = dq
        fy[1] = dk

    @pl.when(core == 1)
    def _():
        ay[1, 0:128] = dk
        fy[1] = dq

    swap_b = remote(fy.at[1], ay.at[1, 128:256], x_ss.at[3], x_rs.at[3], sib)
    swap_b.start()
    for c in swap:
        c.wait()
    wa[...] = tn(ax[0], ay[0]).astype(BF).reshape(4, 4, 80, W)

    def ax_copy(d):
        return remote(wa.at[(x + d) % 4, :, :, 0:384], rax.at[d - 1], ax_ss.at[0], ax_rs.at[0], xpeer(d))

    def ay_copy(d):
        return remote(wa.at[:, (y + d) % 4, :, 384:640], ray.at[d - 1], ay_ss.at[0], ay_rs.at[0], ypeer(d))

    for d in (1, 3, 2):
        ay_copy(d).start()

    dn2 = nt(dq, weight(0)) + nt(dk, weight(1)) + nt(dv, weight(2))
    u2 = u2s[...]
    gv1[...] = jnp.sum(dn2 * u2, axis=0, keepdims=True)
    back = ctt[...].astype(F32) + unit_back(dn2, u2, r2s[:, 0:1], gain)
    scatter_rows(lb_s, back)

    def l_copy(d):
        return remote(lb_s.at[fpeer(d)], lb_r.at[i], l_ss.at[0], l_rs.at[0], (fpeer(d), j))

    @pl.loop(1, 32)
    def _(d):
        l_copy(d).start()

    lb_r[i] = lb_s[i]

    def v_copy(src, dst, n, dev):
        return remote(src, dst, v_ss.at[n], v_rs.at[n], dev)

    for d in (1, 3, 2):
        ax_copy(d).start()
    gx = [v_copy(gv1, gr1.at[d - 1], 0, xpeer(d)) for d in range(1, 4)]
    for c in gx:
        c.start()

    swap_b.wait()
    wb[...] = tn(ax[1], ay[1]).astype(BF).reshape(4, 4, 80, W)

    def bx_copy(d):
        return remote(wb.at[(x + d) % 4, :, :, 0:256], rbx.at[d - 1], bx_ss.at[0], bx_rs.at[0], xpeer(d))

    def by_copy(d):
        return remote(wb.at[:, (y + d) % 4, :, 256:640], rby.at[d - 1], by_ss.at[0], by_rs.at[0], ypeer(d))

    for d in (1, 3, 2):
        bx_copy(d).start()
        by_copy(d).start()

    arrived(mo_r.at[0:31], m_ss.at[0], m_rs.at[0])

    gather_rows(mof, mo_r)
    mo = tn(row_order(), mof[...].astype(BF)).astype(BF)
    bo[...] = (hid[...].astype(F32) + nt(mo, weight(3))).astype(BF)
    bo_store = pltpu.make_async_copy(bo, bo_h, st.at[0])
    bo_store.start()

    arrived(lb_r.at[0:31], l_ss.at[0], l_rs.at[0])

    gather_rows(tx, lb_r)
    gh[...] = tn(row_order(), tx[...].astype(BF)).astype(BF)
    for hp, part in enumerate(split_pair(nn(gh[...], spw[3]))):
        gs_s[hp * 4:hp * 4 + 4] = part.astype(BF).reshape(4, 32, 384)

    def gs_copy(d):
        return remote(gs_s.at[qpeer(d)], gs_r.at[j], gs_ss.at[0], gs_rs.at[0], (i, qpeer(d)))

    @pl.loop(1, 8)
    def _(d):
        gs_copy(d).start()

    gs_r[j] = gs_s[j]

    def add4(own, parts):
        return own.astype(F32) + parts[0].astype(F32) + parts[1].astype(F32) + parts[2].astype(F32)

    arrived(rax, ax_ss.at[0], ax_rs.at[0])
    arrived(ray, ay_ss.at[0], ay_rs.at[0])
    sax[...] = add4(wa[x, :, :, 0:384], rax).astype(BF)
    say[...] = add4(wa[:, y, :, 384:640], ray).astype(BF)

    def ax2_copy(d):
        return remote(sax.at[(y + d) % 4], tax.at[d - 1], ax2_ss.at[0], ax2_rs.at[0], ypeer(d))

    def ay2_copy(d):
        return remote(say.at[(x + d) % 4], tay.at[d - 1], ay2_ss.at[0], ay2_rs.at[0], xpeer(d))

    for d in (1, 3, 2):
        ax2_copy(d).start()
        ay2_copy(d).start()
    arrived(gr1, v_ss.at[0], v_rs.at[0])
    gv2[...] = gv1[...] + gr1[0] + gr1[1] + gr1[2]
    gy = [v_copy(gv2, gr2.at[d - 1], 1, ypeer(d)) for d in range(1, 4)]
    for c in gy:
        c.start()

    arrived(rbx, bx_ss.at[0], bx_rs.at[0])
    arrived(rby, by_ss.at[0], by_rs.at[0])
    sbx[...] = add4(wb[x, :, :, 0:256], rbx).astype(BF)
    sby[...] = add4(wb[:, y, :, 256:640], rby).astype(BF)

    def bx2_copy(d):
        return remote(sbx.at[(y + d) % 4], tbx.at[d - 1], bx2_ss.at[0], bx2_rs.at[0], ypeer(d))

    def by2_copy(d):
        return remote(sby.at[(x + d) % 4], tby.at[d - 1], by2_ss.at[0], by2_rs.at[0], xpeer(d))

    for d in (1, 3, 2):
        bx2_copy(d).start()
        by2_copy(d).start()

    arrived(gs_r.at[0:7], gs_ss.at[0], gs_rs.at[0])

    q, k, v = (qkv_r[:, t].reshape(256, 384) for t in range(3))
    for t, grad in enumerate(attend_back(q, k, v, gs_r[...].reshape(256, 384), prob_s, 2)):
        dq_s[:, t] = grad.astype(BF).reshape(8, 32, 384)

    def dq_copy(d):
        return remote(dq_s.at[qpeer(d)], dq_r.at[j], dq_ss.at[0], dq_rs.at[0], (i, qpeer(d)))

    @pl.loop(1, 8)
    def _(d):
        dq_copy(d).start()

    dq_r[j] = dq_s[j]

    row = lax.broadcasted_iota(jnp.int32, (256, 80), 0)
    col = lax.broadcasted_iota(jnp.int32, (256, 80), 1)
    first = jnp.where((row % 16 < 5) & (col == (row // 16) * 5 + row % 16), 1.0, 0.0).astype(BF)
    second = jnp.where((row % 16 >= 5) & (row % 16 < 10) & (col == (row // 16) * 5 + row % 16 - 5), 1.0, 0.0).astype(BF)
    arrived(gr2, v_ss.at[1], v_rs.at[1])
    gv = gv2[...] + gr2[0] + gr2[1] + gr2[2]
    arrived(tax, ax2_ss.at[0], ax2_rs.at[0])
    arrived(tay, ay2_ss.at[0], ay2_rs.at[0])
    sum_a = jnp.concatenate([add4(sax[y], tax), add4(say[x], tay)], axis=1).astype(BF)
    arrived(tbx, bx2_ss.at[0], bx2_rs.at[0])
    arrived(tby, by2_ss.at[0], by2_rs.at[0])
    sum_b = jnp.concatenate([add4(sbx[y], tbx), add4(sby[x], tby)], axis=1).astype(BF)
    slabs = nn(first, sum_a) + nn(second, sum_b)
    row = lax.broadcasted_iota(jnp.int32, (256, W), 0) % 16
    slabs = jnp.where(row == 10, gv[:, :W], jnp.where(row == 11, gv[:, W:], slabs))
    p3[...] = slabs.astype(BF).reshape(16, 16, W)

    def z_copy(d):
        to = (zc + d) % 16
        return remote(p3.at[to], r3.at[zc], r3_ss.at[0], r3_rs.at[0], (x_lo * 16 + to, j))

    @pl.loop(1, 16)
    def _(d):
        z_copy(d).start()

    r3[zc] = p3[zc]

    arrived(dq_r.at[0:7], dq_ss.at[0], dq_rs.at[0])

    total = None
    for t in range(3):
        grad = join_pair(dq_r[0:4, t].reshape(128, 384).astype(F32), dq_r[4:8, t].reshape(128, 384).astype(F32)).astype(BF)
        term = nt(grad, spw[t])
        total = term if total is None else total + term
    u1, r1 = unit(act[...].astype(F32))
    ig[...] = (gh[...].astype(F32) + unit_back(total, u1, r1, spg[...].reshape(1, C))).astype(BF)
    ig_store = pltpu.make_async_copy(ig, ig_h, st.at[1])
    ig_store.start()

    arrived(r3.at[0:15], r3_ss.at[0], r3_rs.at[0])

    factor = 1.0 / math.sqrt(128 * 256)
    sums = []
    for c in range(2):
        total = r3[c].astype(F32)
        for n in range(1, 8):
            total = total + r3[2 * n + c].astype(F32)
        sums.append(total * factor)
    wg[:, 0] = sums[0][5:10]
    wg[:, 1] = sums[1][5:10]
    wg[:, 2] = sums[1][0:5]
    wg[:, 3] = sums[0][0:5]
    both = sums[0] + sums[1]
    gn[...] = jnp.concatenate([both[10:11], both[11:12]], axis=1)
    bo_store.wait()
    ig_store.wait()


def finish(bo_h, ig_h, wg_h, gn, bo, ig, wg, gg, bo_v, ig_v, wg_v, sems):
    moves = [(bo_h, bo_v, bo), (ig_h, ig_v, ig), (wg_h, wg_v, wg)]
    come = [pltpu.make_async_copy(a, b, sems.at[0, n]) for n, (a, b, _) in enumerate(moves)]
    go = [pltpu.make_async_copy(b, c, sems.at[1, n]) for n, (_, b, c) in enumerate(moves)]
    for c in come:
        c.start()
    device = lax.axis_index("frame") * 8 + lax.axis_index("quad")
    gg[...] = pltpu.roll(gn[...], C - device * 5, 1)[0, :5]
    for a, b in zip(come, go):
        a.wait()
        b.start()
    for c in go:
        c.wait()


def positional(frames, channels):
    freq = np.exp(np.arange(channels // 2, dtype=np.float32)[None, :] * np.float32(-2.0 * math.log(10000.0) / channels))
    phases = np.arange(frames, dtype=np.float32)[:, None] * freq.astype(np.float32)
    both = np.stack([np.sin(phases.astype(np.float64)), np.cos(phases.astype(np.float64))], axis=-1)
    return both.reshape(frames, channels).astype(np.float32)


def permutation():
    order = np.arange(C).reshape(2, 8, 2, 2, 4, 5)
    order = order.transpose(3, 0, 4, 1, 2, 5).reshape(-1)
    matrix = np.zeros((C, C), np.float32)
    matrix[order, np.arange(C)] = 1.0
    return matrix


def local(activations, cotangent, spatial_weights, spatial_gain, motion_weights, motion_gain):
    pe = jnp.asarray(positional(128, C))
    perm = jnp.asarray(permutation(), dtype=BF)
    V, D = pltpu.VMEM, pltpu.SemaphoreType.DMA
    any_, vmem = pl.BlockSpec(memory_space=pl.ANY), pl.BlockSpec(memory_space=pltpu.VMEM)
    scratch = [
        V((128, C), BF), V((128, C), BF), V((4, C, W), BF), V((4, 8, 160, W), BF), V((128, C), F32), V((C, C), BF),
        V((128, C), BF), V((128, C), BF),
        V((8, 3, 32, 384), BF), V((8, 3, 32, 384), BF), V((8, 32, 384), BF), V((8, 32, 384), BF), V((2, 256, 256), F32),
        V((128, C), BF), V((32, 4, C), BF), V((32, 4, C), BF), V((32, 4, C), BF), V((32, 4, C), BF), V((128, C), BF),
        V((128, C), F32), V((128, C), BF), V((128, C), F32), V((128, 128), F32), V((3, 128, W), BF), V((4, 128, 128), F32),
        V((32, 4, W), BF), V((32, 4, W), BF), V((32, 4, C), BF), V((32, 4, C), BF), V((128, C), BF), V((128, W), F32),
        V((8, 32, 384), BF), V((8, 32, 384), BF), V((8, 3, 32, 384), BF), V((8, 3, 32, 384), BF),
        V((2, 128, C), BF), V((2, 128, W), BF), V((2, 256, C), BF), V((2, 256, W), BF),
        V((4, 4, 80, W), BF), V((4, 4, 80, W), BF),
        V((3, 4, 80, 384), BF), V((3, 4, 80, 256), BF), V((3, 4, 80, 256), BF), V((3, 4, 80, 384), BF),
        V((4, 80, 384), BF), V((4, 80, 256), BF), V((4, 80, 256), BF), V((4, 80, 384), BF),
        V((3, 80, 384), BF), V((3, 80, 256), BF), V((3, 80, 256), BF), V((3, 80, 384), BF),
        V((16, 16, W), BF), V((16, 16, W), BF),
        V((1, C), F32), V((3, 1, C), F32), V((1, C), F32), V((3, 1, C), F32),
        D((9,)), D((2,))] + [D((4,))] * 8 + [D((1,))] * 16 + [D((4,)), D((4,))] + [D((1,))] * 18 + [
        D((2,)), D((2,)),
    ]
    results = (
        jax.ShapeDtypeStruct((128, C), BF),
        jax.ShapeDtypeStruct((128, C), BF),
        jax.ShapeDtypeStruct((5, 4, W), F32),
    )
    block_output, input_grad, weight_grad, gain_all = pl.pallas_call(
        kernel,
        out_shape=results + (jax.ShapeDtypeStruct((1, C), F32),),
        in_specs=[any_, any_, any_, vmem, any_, vmem, any_, any_],
        out_specs=(any_, any_, vmem, vmem),
        scratch_shapes=scratch,
        compiler_params=pltpu.CompilerParams(
            has_side_effects=True, collective_id=0, vmem_limit_bytes=60 * 2 ** 20),
    )(
        activations.reshape(128, C), cotangent.reshape(128, C), spatial_weights, spatial_gain,
        motion_weights, motion_gain, pe, perm,
    )
    block_output, input_grad, weight_grad, gain_grad = pl.pallas_call(
        finish,
        out_shape=results + (jax.ShapeDtypeStruct((5,), F32),),
        in_specs=[any_, any_, any_, vmem],
        out_specs=(any_, any_, any_, vmem),
        scratch_shapes=[V((128, C), BF), V((128, C), BF), V((5, 4, W), F32), D((2, 3))],
        compiler_params=pltpu.CompilerParams(vmem_limit_bytes=60 * 2 ** 20),
    )(block_output, input_grad, weight_grad, gain_all)
    shape = activations.shape
    return block_output.reshape(shape), input_grad.reshape(shape), weight_grad.transpose(1, 0, 2), gain_grad


def solution(mesh):
    in_specs = (
        P("frame", "quad", None),
        P("frame", "quad", None),
        P(),
        P(),
        P(None, "quad", None),
        P(),
    )
    out_specs = (
        P("frame", "quad", None),
        P("frame", "quad", None),
        P(None, ("frame", "quad"), None),
        P(("frame", "quad")),
    )
    return jax.shard_map(local, mesh=mesh, in_specs=in_specs, out_specs=out_specs, check_vma=False)
```

```python
import math

import jax
import jax.numpy as jnp
import numpy as np
from jax import lax
from jax.experimental import pallas as pl
from jax.experimental.pallas import tpu as pltpu
from jax.sharding import PartitionSpec as P

HEADS = 4
HEAD_DIM = 160
EPSILON = 1e-05
SCALE = HEAD_DIM ** (-0.5)
C = 1280
W = 640
F32 = jnp.float32
BF = jnp.bfloat16
XA, XB, YA, YB, ZA, ZB = range(6)
DIGIT = {XB: 0, XA: 1, YB: 2, YA: 3, ZA: 4, ZB: 4}
PARTS = (
    (0, 0, 256, (XB, ZA)),
    (0, 256, 256, (YA, ZB)),
    (0, 512, 128, (YB, ZA)),
    (1, 0, 256, (XA, ZB)),
    (1, 256, 256, (YB, ZA)),
    (1, 512, 128, (XB, ZB)),
)
MESH = pl.DeviceIdType.MESH


def nn(a, b):
    return jnp.dot(a, b, preferred_element_type=F32)


def nt(a, b):
    return lax.dot_general(a, b, (((1,), (1,)), ((), ())), preferred_element_type=F32)


def tn(a, b):
    return lax.dot_general(a, b, (((0,), (0,)), ((), ())), preferred_element_type=F32)


def unit(x):
    xc = x - jnp.mean(x, axis=-1, keepdims=True)
    r = lax.rsqrt(jnp.mean(xc * xc, axis=-1, keepdims=True) + EPSILON)
    return xc * r, r


def unit_back(grad, u, r, gain):
    g = grad * gain
    return r * (g - jnp.mean(g, axis=-1, keepdims=True) - u * jnp.mean(g * u, axis=-1, keepdims=True))


def head_of(x, h):
    lane = lax.broadcasted_iota(jnp.int32, x.shape, 1)
    return jnp.where((lane >= h * HEAD_DIM) & (lane < (h + 1) * HEAD_DIM), x, jnp.zeros_like(x))


def split_pair(y):
    return y[:, :384], pltpu.roll(y, 320, 1)[:, :384]


def join_pair(a, b):
    pad = jnp.zeros((a.shape[0], 256), F32)
    left = jnp.concatenate([a, pad], axis=1)
    right = pltpu.roll(jnp.concatenate([b, pad], axis=1), 320, 1)
    lane = lax.broadcasted_iota(jnp.int32, left.shape, 1)
    return jnp.where(lane < 320, left, right)


def row_order():
    row = lax.broadcasted_iota(jnp.int32, (128, 128), 0)
    col = lax.broadcasted_iota(jnp.int32, (128, 128), 1)
    return jnp.where(col == (row % 4) * 32 + row // 4, 1.0, 0.0).astype(BF)


def scatter_rows(to, rows):
    for n in range(32):
        to[n] = rows[4 * n:4 * n + 4, :].astype(BF)


def gather_rows(rows, come):
    for n in range(32):
        rows[4 * n:4 * n + 4, :] = come[n].astype(F32)


def softmax(q, k):
    s = nt(q, k) * SCALE
    e = jnp.exp(s - jnp.max(s, axis=-1, keepdims=True))
    return e / jnp.sum(e, axis=-1, keepdims=True)


def attend_back(q, k, v, g, probs, heads):
    dq = dk = dv = None
    for h in range(heads):
        r = probs[h]
        dr = nt(head_of(g, h), v)
        delta = jnp.sum(r * dr, axis=-1, keepdims=True)
        ds = (r * (dr - delta) * SCALE).astype(BF)
        a, b, c = nn(ds, head_of(k, h)), tn(ds, head_of(q, h)), tn(r.astype(BF), head_of(g, h))
        dq, dk, dv = (a, b, c) if dq is None else (dq + a, dk + b, dv + c)
    return dq, dk, dv


def kernel(act_h, cot_h, spw_h, spg, mw_h, mgn, pe_h, perm_h,
           bo_h, ig_h, wg, gn,
           act, cot, spw, mw, pe, perm, bo, ig,
           qkv_s, qkv_r, o_s, o_r, prob_s,
           hid, hid_s, hid_r, ct_s, ct_r, ctt, tx, n2s, u2s, r2s, mqkv, prob_t,
           mo_s, mo_r, lb_s, lb_r, gh, mof,
           gs_s, gs_r, dq_s, dq_r,
           fx, fy, ax, ay, wa, wb, p3, r3,
           gv1, gr1, gv2, gr2, gv3, gr3,
           ld, st, w1_ss, w1_rs, w2_ss, w2_rs, w3_ss, w3_rs, w4_ss, w4_rs, wz_ss, wz_rs,
           q_ss, q_rs, o_ss, o_rs, h_ss, h_rs, c_ss, c_rs,
           m_ss, m_rs, l_ss, l_rs, gs_ss, gs_rs, dq_ss, dq_rs, x_ss, x_rs,
           p_ss, p_rs, r3_ss, r3_rs,
           v_ss, v_rs, *buffers):
    i, j = lax.axis_index("frame"), lax.axis_index("quad")
    core, z, x_lo = i % 2, (i // 2) % 8, i // 16
    y, x_hi = j % 4, j // 4
    x = x_hi * 2 + x_lo
    zc = i % 16
    sib = (i + 1 - 2 * core, j)
    cross = ((1 - x_lo) * 16 + zc, (1 - x_hi) * 4 + y)
    beside = ((1 - x_lo) * 16 + zc, j)
    even = z % 2
    above = (x_lo * 16 + (zc + 2) % 16, j)
    below = (x_lo * 16 + (zc + 14) % 16, j)

    def fpeer(d):
        return (i + d) % 32

    def qpeer(d):
        return (j + d) % 8

    def xpeer(d):
        xx = (x + d) % 4
        return ((xx % 2) * 16 + zc, (xx // 2) * 4 + y)

    def ypeer(d):
        return (i, x_hi * 4 + (y + d) % 4)

    def remote(src, dst, ss, rs, dev):
        return pltpu.make_async_remote_copy(
            src_ref=src, dst_ref=dst, send_sem=ss, recv_sem=rs, device_id=dev, device_id_type=MESH)

    def arrived(part, ss, rs):
        pltpu.make_async_copy(part, part, ss).wait()
        pltpu.make_async_copy(part, part, rs).wait()

    bar = pltpu.get_barrier_semaphore()

    @pl.loop(1, 32)
    def _(d):
        pl.semaphore_signal(bar, inc=1, device_id=(fpeer(d), j), device_id_type=MESH)

    @pl.loop(1, 8)
    def _(d):
        pl.semaphore_signal(bar, inc=1, device_id=(i, qpeer(d)), device_id_type=MESH)

    @pl.loop(1, 8)
    def _(d):
        pl.semaphore_signal(bar, inc=1, device_id=((1 - x_lo) * 16 + zc, qpeer(d)), device_id_type=MESH)

    half = pl.ds(pl.multiple_of(core * 80, 16), 80)
    loads = [
        pltpu.make_async_copy(act_h, act, ld.at[0]),
        pltpu.make_async_copy(spw_h.at[0], spw.at[0], ld.at[1]),
        pltpu.make_async_copy(spw_h.at[1], spw.at[1], ld.at[2]),
        pltpu.make_async_copy(spw_h.at[2], spw.at[2], ld.at[3]),
        pltpu.make_async_copy(cot_h, cot, ld.at[5]),
        pltpu.make_async_copy(mw_h.at[even, half], mw.at[even, j, half], ld.at[6]),
        pltpu.make_async_copy(mw_h.at[2:4, half], mw.at[2:4, j, half], ld.at[9]),
        pltpu.make_async_copy(spw_h.at[3], spw.at[3], ld.at[4]),
        pltpu.make_async_copy(pe_h, pe, ld.at[7]),
        pltpu.make_async_copy(perm_h, perm, ld.at[8]),
    ]
    for c in loads:
        c.start()

    loads[0].wait()
    u1, _ = unit(act[...].astype(F32))
    n1 = (u1 * spg[...].reshape(1, C)).astype(BF)
    for t in range(3):
        loads[1 + t].wait()
        for hp, part in enumerate(split_pair(nn(n1, spw[t]))):
            qkv_s[hp * 4:hp * 4 + 4, t] = part.astype(BF).reshape(4, 32, 384)
    pl.semaphore_wait(bar, 45)

    def q_copy(d):
        return remote(qkv_s.at[qpeer(d)], qkv_r.at[j], q_ss.at[0], q_rs.at[0], (i, qpeer(d)))

    @pl.loop(1, 8)
    def _(d):
        q_copy(d).start()

    matrix = (even, 1 - even, 2, 3)

    def w1_copy(n, d):
        m = matrix[n]
        return remote(mw_h.at[m, half], mw.at[m, j, half], w1_ss.at[n], w1_rs.at[n], ypeer(d))

    def w2_copy(n):
        part = mw.at[matrix[n], pl.ds(x_hi * 4 + 2 * (1 - x_lo), 2), half]
        return remote(part, part, w2_ss.at[n], w2_rs.at[n], cross)

    def w3_copy(n):
        part = mw.at[matrix[n], pl.ds((1 - x_hi) * 4 + 2 * x_lo, 2), half]
        return remote(part, part, w3_ss.at[n], w3_rs.at[n], beside)

    def w4_copy(n):
        part = mw.at[matrix[n], :, half]
        return remote(part, part, w4_ss.at[n], w4_rs.at[n], sib)

    def wz_copies(group, n):
        up, down = mw.at[even, pl.ds(group * 4, 2), half], mw.at[even, pl.ds(group * 4 + 2, 2), half]
        return [remote(up, up, wz_ss.at[n], wz_rs.at[n], above),
                remote(down, down, wz_ss.at[n + 1], wz_rs.at[n + 1], below)]

    wz = wz_copies(x_hi, 0) + wz_copies(1 - x_hi, 2)

    def w1_start(n):
        for d in (1, 3, 2):
            w1_copy(n, d).start()

    def w1_pass(n):
        arrived(mw.at[matrix[n], 0:3, half], w1_ss.at[n], w1_rs.at[n])
        w2_copy(n).start()

    def w2_pass(n):
        w2_copy(n).wait()
        w3_copy(n).start()

    def w3_pass(n):
        w3_copy(n).wait()
        w4_copy(n).start()

    w1_start(0)

    loads[4].wait()
    scatter_rows(ct_s, nn(row_order(), cot[...]))

    def c_copy(d):
        return remote(ct_s.at[fpeer(d)], ct_r.at[i], c_ss.at[0], c_rs.at[0], (fpeer(d), j))

    @pl.loop(1, 32)
    def _(d):
        c_copy(d).start()

    ct_r[i] = ct_s[i]
    loads[5].wait()
    loads[6].wait()
    qkv_r[j] = qkv_s[j]

    arrived(qkv_r.at[0:7], q_ss.at[0], q_rs.at[0])

    q, k, v = (qkv_r[:, t].reshape(256, 384) for t in range(3))
    out = None
    for h in range(2):
        probs = softmax(head_of(q, h), k)
        prob_s[h] = probs
        term = nn(probs.astype(BF), head_of(v, h))
        out = term if out is None else out + term
    o_s[...] = out.astype(BF).reshape(8, 32, 384)

    def o_copy(d):
        return remote(o_s.at[qpeer(d)], o_r.at[j], o_ss.at[0], o_rs.at[0], (i, qpeer(d)))

    @pl.loop(1, 8)
    def _(d):
        o_copy(d).start()

    o_r[j] = o_s[j]
    w1_start(2)
    w1_start(3)
    w1_pass(0)
    wz[0].start()
    wz[1].start()
    w2_pass(0)

    arrived(o_r.at[0:7], o_ss.at[0], o_rs.at[0])

    loads[7].wait()
    so = join_pair(o_r[0:4].reshape(128, 384).astype(F32), o_r[4:8].reshape(128, 384).astype(F32)).astype(BF)
    hid[...] = (act[...].astype(F32) + nt(so, spw[3])).astype(BF)
    scatter_rows(hid_s, nn(row_order(), hid[...]))

    def h_copy(d):
        return remote(hid_s.at[fpeer(d)], hid_r.at[i], h_ss.at[0], h_rs.at[0], (fpeer(d), j))

    @pl.loop(1, 32)
    def _(d):
        h_copy(d).start()

    hid_r[i] = hid_s[i]

    w1_pass(2)
    w3_pass(0)
    wz[2].start()
    wz[3].start()

    arrived(ct_r.at[0:31], c_ss.at[0], c_rs.at[0])

    gather_rows(tx, ct_r)
    ctt[...] = tx[...].astype(BF)
    loads[9].wait()
    ctp = nn(ctt[...], perm[...]).astype(BF)

    @pl.when(core == 0)
    def _():
        ax[0, 0:128] = ctp

    @pl.when(core == 1)
    def _():
        fx[0] = ctp

    w1_pass(3)
    w2_pass(2)
    for c in wz:
        c.wait()
    w4_copy(1).start()
    w2_pass(3)
    w3_pass(2)

    def weight(n):
        return mw[n].reshape(C, W)

    arrived(hid_r.at[0:31], h_ss.at[0], h_rs.at[0])

    gather_rows(tx, hid_r)
    loads[8].wait()
    gain = mgn[...].reshape(1, C)
    u2, r2 = unit(tx[...])
    u2s[...] = u2
    r2s[...] = jnp.broadcast_to(r2, r2s.shape)
    n2s[...] = (u2 * gain + pe[...]).astype(BF)
    w4_copy(0).wait()
    w4_copy(1).wait()
    for t in range(3):
        if t == 2:
            w4_copy(2).wait()
        mqkv[t] = nn(n2s[...], weight(t)).astype(BF)
    w3_pass(3)
    out = None
    for h in range(HEADS):
        probs = softmax(head_of(mqkv[0], h), mqkv[1])
        prob_t[h] = probs
        term = nn(probs.astype(BF), head_of(mqkv[2], h))
        out = term if out is None else out + term
    mo_t = out.astype(BF)
    scatter_rows(mo_s, out)

    def m_copy(d):
        return remote(mo_s.at[fpeer(d)], mo_r.at[i], m_ss.at[0], m_rs.at[0], (fpeer(d), j))

    @pl.loop(1, 32)
    def _(d):
        m_copy(d).start()

    mo_r[i] = mo_s[i]

    w4_copy(3).wait()
    mg = nn(ctt[...], weight(3)).astype(BF)
    dv = None
    for h in range(HEADS):
        term = tn(prob_t[h].astype(BF), head_of(mg, h))
        dv = term if dv is None else dv + term
    dv = dv.astype(BF)
    n2p = nn(n2s[...], perm[...]).astype(BF)
    ax[1, 0:128] = n2p
    fx[1] = n2p

    @pl.when(core == 0)
    def _():
        ay[0, 0:128] = mo_t
        fx[0] = n2p
        fy[0] = dv

    @pl.when(core == 1)
    def _():
        ax[0, 0:128] = n2p
        ay[0, 0:128] = dv
        fy[0] = mo_t

    swap = [remote(fx.at[0], ax.at[0, 128:256], x_ss.at[0], x_rs.at[0], sib),
            remote(fy.at[0], ay.at[0, 128:256], x_ss.at[1], x_rs.at[1], sib),
            remote(fx.at[1], ax.at[1, 128:256], x_ss.at[2], x_rs.at[2], sib)]
    for c in swap:
        c.start()

    dq = dk = None
    for h in range(HEADS):
        r = prob_t[h]
        dr = nt(head_of(mg, h), mqkv[2])
        delta = jnp.sum(r * dr, axis=-1, keepdims=True)
        ds = (r * (dr - delta) * SCALE).astype(BF)
        a, b = nn(ds, head_of(mqkv[1], h)), tn(ds, head_of(mqkv[0], h))
        dq, dk = (a, b) if dq is None else (dq + a, dk + b)
    dq, dk = dq.astype(BF), dk.astype(BF)

    @pl.when(core == 0)
    def _():
        ay[1, 0:128] = dq
        fy[1] = dk

    @pl.when(core == 1)
    def _():
        ay[1, 0:128] = dk
        fy[1] = dq

    swap_b = remote(fy.at[1], ay.at[1, 128:256], x_ss.at[3], x_rs.at[3], sib)
    swap_b.start()
    for c in swap:
        c.wait()
    wa[...] = tn(ax[0], ay[0]).reshape(2, 2, 2, 2, 2, 40, W).astype(BF)

    own = (x_hi, (x_hi + x_lo) % 2, y // 2, (y // 2 + y) % 2, z % 2)

    def zpeer(zz):
        return (x_lo * 16 + (zz + 8) % 8 * 2 + core, j)

    partner = {
        XA: beside, XB: cross,
        YA: (i, x_hi * 4 + y + 1 - 2 * (y % 2)), YB: (i, x_hi * 4 + 3 - y),
        ZA: zpeer(z + 1 - 2 * (z % 2)), ZB: zpeer(z - 1 + 2 * (z % 2)),
    }

    def left(p, step):
        return [n for n in range(5) if n not in [DIGIT[link] for link in PARTS[p][3][:step]]]

    def block(p, step, digits):
        which, lane, lanes, _ = PARTS[p]
        ref, columns = ((wa, wb)[which], slice(lane, lane + lanes)) if step == 0 else (buffers[6 * p + 2 * step - 1], slice(None))
        return ref, tuple(digits.get(n, slice(None)) for n in left(p, step)) + (slice(None), columns)

    def step_copy(p, step):
        link = PARTS[p][3][step]
        ref, at = block(p, step, {DIGIT[link]: 1 - own[DIGIT[link]]})
        return remote(ref.at[at], buffers[6 * p + 2 * step], p_ss.at[3 * p + step], p_rs.at[3 * p + step], partner[link])

    def direct(p):
        digits = left(p, 2)
        for mask in range(1, 8):
            to = [own[n] for n in range(4)]
            for bit, n in enumerate(digits):
                if mask >> bit & 1:
                    to[n] = 1 - own[n]
            ref, at = block(p, 2, {n: to[n] for n in digits})
            device = ((to[0] + to[1]) % 2 * 16 + zc, to[0] * 4 + to[2] * 2 + (to[2] + to[3]) % 2)
            remote(ref.at[at], buffers[6 * p + 4].at[mask - 1], p_ss.at[3 * p + 2], p_rs.at[3 * p + 2], device).start()

    done = [0] * 6

    def begin(p):
        step_copy(p, 0).start()

    def advance(p):
        step = done[p]
        step_copy(p, step).wait()
        link = PARTS[p][3][step]
        ref, at = block(p, step, {DIGIT[link]: own[DIGIT[link]]})
        buffers[6 * p + 2 * step + 1][...] = (
            ref[at].astype(F32) + buffers[6 * p + 2 * step][...].astype(F32)).astype(BF)
        done[p] = step + 1
        if step == 0:
            step_copy(p, 1).start()
        else:
            direct(p)

    def result(p):
        come = buffers[6 * p + 4]
        arrived(come, p_ss.at[3 * p + 2], p_rs.at[3 * p + 2])
        ref, at = block(p, 2, {n: own[n] for n in left(p, 2)})
        total = ref[at].astype(F32)
        for n in range(7):
            total = total + come[n].astype(F32)
        return total.astype(BF)

    for p in (0, 1, 2):
        begin(p)
    dn2 = nt(dq, weight(0)) + nt(dk, weight(1)) + nt(dv, weight(2))
    u2 = u2s[...]
    gv1[...] = jnp.sum(dn2 * u2, axis=0, keepdims=True)
    back = ctt[...].astype(F32) + unit_back(dn2, u2, r2s[:, 0:1], gain)
    scatter_rows(lb_s, back)

    def l_copy(d):
        return remote(lb_s.at[fpeer(d)], lb_r.at[i], l_ss.at[0], l_rs.at[0], (fpeer(d), j))

    @pl.loop(1, 32)
    def _(d):
        l_copy(d).start()

    lb_r[i] = lb_s[i]

    def v_copy(src, dst, n, dev):
        return remote(src, dst, v_ss.at[n], v_rs.at[n], dev)

    gx = [v_copy(gv1, gr1.at[d - 1], 0, xpeer(d)) for d in range(1, 4)]
    for c in gx:
        c.start()

    swap_b.wait()
    wb[...] = tn(ax[1], ay[1]).reshape(2, 2, 2, 2, 2, 40, W).astype(BF)

    for p in (3, 4, 5):
        begin(p)

    arrived(mo_r.at[0:31], m_ss.at[0], m_rs.at[0])

    gather_rows(mof, mo_r)
    mo = tn(row_order(), mof[...].astype(BF)).astype(BF)
    bo[...] = (hid[...].astype(F32) + nt(mo, weight(3))).astype(BF)
    bo_store = pltpu.make_async_copy(bo, bo_h, st.at[0])
    bo_store.start()

    advance(2)
    advance(0)
    advance(1)

    arrived(lb_r.at[0:31], l_ss.at[0], l_rs.at[0])

    gather_rows(tx, lb_r)
    gh[...] = tn(row_order(), tx[...].astype(BF)).astype(BF)
    for hp, part in enumerate(split_pair(nn(gh[...], spw[3]))):
        gs_s[hp * 4:hp * 4 + 4] = part.astype(BF).reshape(4, 32, 384)

    def gs_copy(d):
        return remote(gs_s.at[qpeer(d)], gs_r.at[j], gs_ss.at[0], gs_rs.at[0], (i, qpeer(d)))

    @pl.loop(1, 8)
    def _(d):
        gs_copy(d).start()

    gs_r[j] = gs_s[j]

    arrived(gr1, v_ss.at[0], v_rs.at[0])
    gv2[...] = gv1[...] + gr1[0] + gr1[1] + gr1[2]
    gy = [v_copy(gv2, gr2.at[d - 1], 1, ypeer(d)) for d in range(1, 4)]
    for c in gy:
        c.start()
    advance(4)
    advance(5)
    advance(3)
    arrived(gs_r.at[0:7], gs_ss.at[0], gs_rs.at[0])
    advance(2)
    advance(0)
    advance(1)
    advance(4)
    advance(5)
    advance(3)

    q, k, v = (qkv_r[:, t].reshape(256, 384) for t in range(3))
    for t, grad in enumerate(attend_back(q, k, v, gs_r[...].reshape(256, 384), prob_s, 2)):
        dq_s[:, t] = grad.astype(BF).reshape(8, 32, 384)

    def dq_copy(d):
        return remote(dq_s.at[qpeer(d)], dq_r.at[j], dq_ss.at[0], dq_rs.at[0], (i, qpeer(d)))

    @pl.loop(1, 8)
    def _(d):
        dq_copy(d).start()

    dq_r[j] = dq_s[j]

    arrived(gr2, v_ss.at[1], v_rs.at[1])
    gv3[...] = gv2[...] + gr2[0] + gr2[1] + gr2[2]
    gz = v_copy(gv3, gr3, 2, partner[ZA])
    gz.start()

    row = lax.broadcasted_iota(jnp.int32, (128, 40), 0)
    col = lax.broadcasted_iota(jnp.int32, (128, 40), 1)
    first = jnp.where((row % 16 < 5) & (col == (row // 16) * 5 + row % 16), 1.0, 0.0).astype(BF)
    second = jnp.where((row % 16 >= 5) & (row % 16 < 10) & (col == (row // 16) * 5 + row % 16 - 5), 1.0, 0.0).astype(BF)
    gz.wait()
    gv = gv3[...] + gr3[...]
    sum_a = jnp.concatenate([result(p) for p in (0, 1, 2)], axis=1)
    sum_b = jnp.concatenate([result(p) for p in (3, 4, 5)], axis=1)
    slabs = nn(first, sum_a) + nn(second, sum_b)
    row = lax.broadcasted_iota(jnp.int32, (128, W), 0) % 16
    slabs = jnp.where(row == 10, gv[:, :W], jnp.where(row == 11, gv[:, W:], slabs))
    p3[...] = slabs.astype(BF).reshape(8, 16, W)
    place = z // 2 * 2 + core

    def z_copy(d):
        to = (place + d) % 8
        return remote(p3.at[to], r3.at[place], r3_ss.at[0], r3_rs.at[0],
                      (x_lo * 16 + to // 2 * 4 + z % 2 * 2 + to % 2, j))

    @pl.loop(1, 8)
    def _(d):
        z_copy(d).start()

    r3[place] = p3[place]

    arrived(dq_r.at[0:7], dq_ss.at[0], dq_rs.at[0])

    total = None
    for t in range(3):
        grad = join_pair(dq_r[0:4, t].reshape(128, 384).astype(F32), dq_r[4:8, t].reshape(128, 384).astype(F32)).astype(BF)
        term = nt(grad, spw[t])
        total = term if total is None else total + term
    u1, r1 = unit(act[...].astype(F32))
    ig[...] = (gh[...].astype(F32) + unit_back(total, u1, r1, spg[...].reshape(1, C))).astype(BF)
    ig_store = pltpu.make_async_copy(ig, ig_h, st.at[1])
    ig_store.start()

    arrived(r3.at[0:7], r3_ss.at[0], r3_rs.at[0])

    factor = 1.0 / math.sqrt(128 * 256)
    sums = []
    for c in range(2):
        total = r3[c].astype(F32)
        for n in range(1, 4):
            total = total + r3[2 * n + c].astype(F32)
        sums.append(total * factor)
    wg[:, 0] = sums[0][5:10]
    wg[:, 1] = sums[1][5:10]
    wg[:, 2] = sums[1][0:5]
    wg[:, 3] = sums[0][0:5]
    both = sums[0] + sums[1]
    gn[...] = jnp.concatenate([both[10:11], both[11:12]], axis=1)
    bo_store.wait()
    ig_store.wait()


def finish(bo_h, ig_h, wg_h, gn, bo, ig, wg, gg, bo_v, ig_v, wg_v, sems):
    moves = [(bo_h, bo_v, bo), (ig_h, ig_v, ig), (wg_h, wg_v, wg)]
    come = [pltpu.make_async_copy(a, b, sems.at[0, n]) for n, (a, b, _) in enumerate(moves)]
    go = [pltpu.make_async_copy(b, c, sems.at[1, n]) for n, (_, b, c) in enumerate(moves)]
    for c in come:
        c.start()
    device = lax.axis_index("frame") * 8 + lax.axis_index("quad")
    gg[...] = pltpu.roll(gn[...], C - device * 5, 1)[0, :5]
    for a, b in zip(come, go):
        a.wait()
        b.start()
    for c in go:
        c.wait()


def positional(frames, channels):
    freq = np.exp(np.arange(channels // 2, dtype=np.float32)[None, :] * np.float32(-2.0 * math.log(10000.0) / channels))
    phases = np.arange(frames, dtype=np.float32)[:, None] * freq.astype(np.float32)
    both = np.stack([np.sin(phases.astype(np.float64)), np.cos(phases.astype(np.float64))], axis=-1)
    return both.reshape(frames, channels).astype(np.float32)


def permutation():
    matrix = np.zeros((C, C), np.float32)
    for m in range(C):
        rest, r = divmod(m, 5)
        rest, core = divmod(rest, 2)
        rest, z_high = divmod(rest, 4)
        xb, xa, yb, ya, z_low = (rest // 16) % 2, (rest // 8) % 2, (rest // 4) % 2, (rest // 2) % 2, rest % 2
        y = yb * 2 + (yb + ya) % 2
        n = (xb + xa) % 2 * 640 + (z_high * 2 + z_low) * 80 + core * 40 + xb * 20 + y * 5 + r
        matrix[n, m] = 1.0
    return matrix


def part_buffers():
    shapes = []
    for _, _, lanes, _ in PARTS:
        shapes += [pltpu.VMEM((2, 2, 2, 2, 40, lanes), BF)] * 2 + [pltpu.VMEM((2, 2, 2, 40, lanes), BF)] * 2
        shapes += [pltpu.VMEM((7, 40, lanes), BF), pltpu.VMEM((8, 128), BF)]
    return shapes


def local(activations, cotangent, spatial_weights, spatial_gain, motion_weights, motion_gain):
    pe = jnp.asarray(positional(128, C))
    perm = jnp.asarray(permutation(), dtype=BF)
    V, D = pltpu.VMEM, pltpu.SemaphoreType.DMA
    any_, vmem = pl.BlockSpec(memory_space=pl.ANY), pl.BlockSpec(memory_space=pltpu.VMEM)
    scratch = [
        V((128, C), BF), V((128, C), BF), V((4, C, W), BF), V((4, 8, 160, W), BF), V((128, C), F32), V((C, C), BF),
        V((128, C), BF), V((128, C), BF),
        V((8, 3, 32, 384), BF), V((8, 3, 32, 384), BF), V((8, 32, 384), BF), V((8, 32, 384), BF), V((2, 256, 256), F32),
        V((128, C), BF), V((32, 4, C), BF), V((32, 4, C), BF), V((32, 4, C), BF), V((32, 4, C), BF), V((128, C), BF),
        V((128, C), F32), V((128, C), BF), V((128, C), F32), V((128, 128), F32), V((3, 128, W), BF), V((4, 128, 128), F32),
        V((32, 4, W), BF), V((32, 4, W), BF), V((32, 4, C), BF), V((32, 4, C), BF), V((128, C), BF), V((128, W), F32),
        V((8, 32, 384), BF), V((8, 32, 384), BF), V((8, 3, 32, 384), BF), V((8, 3, 32, 384), BF),
        V((2, 128, C), BF), V((2, 128, W), BF), V((2, 256, C), BF), V((2, 256, W), BF),
        V((2, 2, 2, 2, 2, 40, W), BF), V((2, 2, 2, 2, 2, 40, W), BF), V((8, 16, W), BF), V((8, 16, W), BF),
        V((1, C), F32), V((3, 1, C), F32), V((1, C), F32), V((3, 1, C), F32), V((1, C), F32), V((1, C), F32),
        D((10,)), D((2,))] + [D((4,))] * 10 + [D((1,))] * 16 + [
        D((4,)), D((4,)), D((18,)), D((18,)), D((1,)), D((1,)),
        D((3,)), D((3,)),
    ] + part_buffers()
    results = (
        jax.ShapeDtypeStruct((128, C), BF),
        jax.ShapeDtypeStruct((128, C), BF),
        jax.ShapeDtypeStruct((5, 4, W), F32),
    )
    block_output, input_grad, weight_grad, gain_all = pl.pallas_call(
        kernel,
        out_shape=results + (jax.ShapeDtypeStruct((1, C), F32),),
        in_specs=[any_, any_, any_, vmem, any_, vmem, any_, any_],
        out_specs=(any_, any_, vmem, vmem),
        scratch_shapes=scratch,
        compiler_params=pltpu.CompilerParams(
            has_side_effects=True, collective_id=0, vmem_limit_bytes=60 * 2 ** 20),
    )(
        activations.reshape(128, C), cotangent.reshape(128, C), spatial_weights, spatial_gain,
        motion_weights, motion_gain, pe, perm,
    )
    block_output, input_grad, weight_grad, gain_grad = pl.pallas_call(
        finish,
        out_shape=results + (jax.ShapeDtypeStruct((5,), F32),),
        in_specs=[any_, any_, any_, vmem],
        out_specs=(any_, any_, any_, vmem),
        scratch_shapes=[V((128, C), BF), V((128, C), BF), V((5, 4, W), F32), D((2, 3))],
        compiler_params=pltpu.CompilerParams(vmem_limit_bytes=60 * 2 ** 20),
    )(block_output, input_grad, weight_grad, gain_all)
    shape = activations.shape
    return block_output.reshape(shape), input_grad.reshape(shape), weight_grad.transpose(1, 0, 2), gain_grad


def solution(mesh):
    in_specs = (
        P("frame", "quad", None),
        P("frame", "quad", None),
        P(),
        P(),
        P(None, "quad", None),
        P(),
    )
    out_specs = (
        P("frame", "quad", None),
        P("frame", "quad", None),
        P(None, ("frame", "quad"), None),
        P(("frame", "quad")),
    )
    return jax.shard_map(local, mesh=mesh, in_specs=in_specs, out_specs=out_specs, check_vma=False)
```

```python
import math

import jax
import jax.numpy as jnp
import numpy as np
from jax import lax
from jax.experimental import pallas as pl
from jax.experimental.pallas import tpu as pltpu
from jax.sharding import PartitionSpec as P

HEADS = 4
HEAD_DIM = 160
EPSILON = 1e-05
SCALE = HEAD_DIM ** (-0.5)
C = 1280
W = 640
F32 = jnp.float32
BF = jnp.bfloat16
XA, XB, YA, YB, ZA, ZB = range(6)
DIGIT = {XB: 0, XA: 1, YB: 2, YA: 3, ZA: 4, ZB: 4}
PARTS = (
    (0, 0, 256, (XB, ZA)),
    (0, 256, 256, (YA, ZB)),
    (0, 512, 128, (YB, ZA)),
    (1, 0, 256, (XA, ZB)),
    (1, 256, 256, (YB, ZA)),
    (1, 512, 128, (XB, ZB)),
)
MESH = pl.DeviceIdType.MESH


def nn(a, b):
    return jnp.dot(a, b, preferred_element_type=F32)


def nt(a, b):
    return lax.dot_general(a, b, (((1,), (1,)), ((), ())), preferred_element_type=F32)


def tn(a, b):
    return lax.dot_general(a, b, (((0,), (0,)), ((), ())), preferred_element_type=F32)


def unit(x):
    xc = x - jnp.mean(x, axis=-1, keepdims=True)
    r = lax.rsqrt(jnp.mean(xc * xc, axis=-1, keepdims=True) + EPSILON)
    return xc * r, r


def unit_back(grad, u, r, gain):
    g = grad * gain
    return r * (g - jnp.mean(g, axis=-1, keepdims=True) - u * jnp.mean(g * u, axis=-1, keepdims=True))


def head_of(x, h):
    lane = lax.broadcasted_iota(jnp.int32, x.shape, 1)
    return jnp.where((lane >= h * HEAD_DIM) & (lane < (h + 1) * HEAD_DIM), x, jnp.zeros_like(x))


def split_pair(y):
    return y[:, :384], pltpu.roll(y, 320, 1)[:, :384]


def join_pair(a, b):
    pad = jnp.zeros((a.shape[0], 256), F32)
    left = jnp.concatenate([a, pad], axis=1)
    right = pltpu.roll(jnp.concatenate([b, pad], axis=1), 320, 1)
    lane = lax.broadcasted_iota(jnp.int32, left.shape, 1)
    return jnp.where(lane < 320, left, right)


def row_order():
    row = lax.broadcasted_iota(jnp.int32, (128, 128), 0)
    col = lax.broadcasted_iota(jnp.int32, (128, 128), 1)
    return jnp.where(col == (row % 4) * 32 + row // 4, 1.0, 0.0).astype(BF)


def scatter_rows(to, rows):
    for n in range(32):
        to[n] = rows[4 * n:4 * n + 4, :].astype(BF)


def gather_rows(rows, come):
    for n in range(32):
        rows[4 * n:4 * n + 4, :] = come[n].astype(F32)


def softmax(q, k):
    s = nt(q, k) * SCALE
    e = jnp.exp(s - jnp.max(s, axis=-1, keepdims=True))
    return e / jnp.sum(e, axis=-1, keepdims=True)


def attend_back(q, k, v, g, probs, heads):
    dq = dk = dv = None
    for h in range(heads):
        r = probs[h]
        dr = nt(head_of(g, h), v)
        delta = jnp.sum(r * dr, axis=-1, keepdims=True)
        ds = (r * (dr - delta) * SCALE).astype(BF)
        a, b, c = nn(ds, head_of(k, h)), tn(ds, head_of(q, h)), tn(r.astype(BF), head_of(g, h))
        dq, dk, dv = (a, b, c) if dq is None else (dq + a, dk + b, dv + c)
    return dq, dk, dv


def kernel(act_h, cot_h, spw_h, spg, mw_h, mgn, pe_h, perm_h,
           bo_h, ig_h, wg, gn,
           act, cot, spw, spt, mw, pe, perm, bo, ig,
           qkv_s, qkv_r, o_s, o_r, prob_s,
           hid, hid_s, hid_r, ct_s, ct_r, ctt, tx, n2s, u2s, r2s, mqkv, prob_t,
           mo_s, mo_r, lb_s, lb_r, gh, mof,
           gs_s, gs_r, dq_s, dq_r,
           fx, fy, ax, ay, wa, wb, p3, r3,
           gv1, gr1, gv2, gr2, gv3, gr3,
           ld, st, w1_ss, w1_rs, w2_ss, w2_rs, w3_ss, w3_rs, w4_ss, w4_rs, wz_ss, wz_rs, wx_ss, wx_rs, wy_ss, wy_rs,
           q_ss, q_rs, o_ss, o_rs, h_ss, h_rs, c_ss, c_rs,
           m_ss, m_rs, l_ss, l_rs, gs_ss, gs_rs, dq_ss, dq_rs, x_ss, x_rs,
           p_ss, p_rs, r3_ss, r3_rs,
           v_ss, v_rs, *buffers):
    i, j = lax.axis_index("frame"), lax.axis_index("quad")
    core, z, x_lo = i % 2, (i // 2) % 8, i // 16
    y, x_hi = j % 4, j // 4
    x = x_hi * 2 + x_lo
    zc = i % 16
    sib = (i + 1 - 2 * core, j)
    cross = ((1 - x_lo) * 16 + zc, (1 - x_hi) * 4 + y)
    beside = ((1 - x_lo) * 16 + zc, j)
    even = z % 2
    above = (x_lo * 16 + (zc + 2) % 16, j)
    below = (x_lo * 16 + (zc + 14) % 16, j)

    def fpeer(d):
        return (i + d) % 32

    def qpeer(d):
        return (j + d) % 8

    def xpeer(d):
        xx = (x + d) % 4
        return ((xx % 2) * 16 + zc, (xx // 2) * 4 + y)

    def ypeer(d):
        return (i, x_hi * 4 + (y + d) % 4)

    def remote(src, dst, ss, rs, dev):
        return pltpu.make_async_remote_copy(
            src_ref=src, dst_ref=dst, send_sem=ss, recv_sem=rs, device_id=dev, device_id_type=MESH)

    def arrived(part, ss, rs):
        pltpu.make_async_copy(part, part, ss).wait()
        pltpu.make_async_copy(part, part, rs).wait()

    half = pl.ds(pl.multiple_of(core * 80, 16), 80)
    loads = [
        pltpu.make_async_copy(act_h, act, ld.at[0]),
        pltpu.make_async_copy(spw_h.at[0], spw.at[0], ld.at[1]),
        pltpu.make_async_copy(spw_h.at[1], spw.at[1], ld.at[2]),
        pltpu.make_async_copy(spw_h.at[2], spw.at[2], ld.at[3]),
        pltpu.make_async_copy(cot_h, cot, ld.at[5]),
        pltpu.make_async_copy(mw_h.at[even, half], mw.at[even, j, half], ld.at[6]),
        pltpu.make_async_copy(mw_h.at[2:4, half], mw.at[2:4, j, half], ld.at[9]),
        pltpu.make_async_copy(spw_h.at[3], spw.at[3], ld.at[4]),
        pltpu.make_async_copy(pe_h, pe, ld.at[7]),
        pltpu.make_async_copy(perm_h, perm, ld.at[8]),
    ]
    for c in loads:
        c.start()

    bar = pltpu.get_barrier_semaphore()

    @pl.loop(1, 32)
    def _(d):
        pl.semaphore_signal(bar, inc=1, device_id=(fpeer(d), j), device_id_type=MESH)

    @pl.loop(1, 8)
    def _(d):
        pl.semaphore_signal(bar, inc=1, device_id=(i, qpeer(d)), device_id_type=MESH)

    @pl.loop(1, 8)
    def _(d):
        pl.semaphore_signal(bar, inc=1, device_id=((1 - x_lo) * 16 + zc, qpeer(d)), device_id_type=MESH)

    loads[0].wait()
    u1, _ = unit(act[...].astype(F32))
    n1 = (u1 * spg[...].reshape(1, C)).astype(BF)
    for t in range(3):
        loads[1 + t].wait()
        for hp, part in enumerate(split_pair(nn(n1, spw[t]))):
            qkv_s[hp * 4:hp * 4 + 4, t] = part.astype(BF).reshape(4, 32, 384)
    pl.semaphore_wait(bar, 45)

    def q_copy(d):
        return remote(qkv_s.at[qpeer(d)], qkv_r.at[j], q_ss.at[0], q_rs.at[0], (i, qpeer(d)))

    @pl.loop(1, 8)
    def _(d):
        q_copy(d).start()

    matrix = (even, 1 - even, 2, 3)

    def w1_copy(n, d):
        m = matrix[n]
        return remote(mw_h.at[m, half], mw.at[m, j, half], w1_ss.at[n], w1_rs.at[n], ypeer(d))

    def w2_copy(n):
        part = mw.at[matrix[n], pl.ds(x_hi * 4 + 2 * (1 - x_lo), 2), half]
        return remote(part, part, w2_ss.at[n], w2_rs.at[n], cross)

    def w3_copy(n):
        part = mw.at[matrix[n], pl.ds((1 - x_hi) * 4 + 2 * x_lo, 2), half]
        return remote(part, part, w3_ss.at[n], w3_rs.at[n], beside)

    def w4_copy(n):
        part = mw.at[matrix[n], :, half]
        return remote(part, part, w4_ss.at[n], w4_rs.at[n], sib)

    up, down = mw.at[even, pl.ds(x_hi * 4, 2), half], mw.at[even, pl.ds(x_hi * 4 + 2, 2), half]
    wz = [remote(up, up, wz_ss.at[0], wz_rs.at[0], above),
          remote(down, down, wz_ss.at[1], wz_rs.at[1], below)]

    def wx_copy(n):
        m = matrix[n]
        return remote(mw_h.at[m, half], mw.at[m, j, half], wx_ss.at[n], wx_rs.at[n], cross)

    def wy_copy(n, d):
        part = mw.at[matrix[n], (1 - x_hi) * 4 + y, half]
        return remote(part, part, wy_ss.at[n], wy_rs.at[n], ypeer(d))

    def w1_start(n):
        for d in (1, 3, 2):
            w1_copy(n, d).start()

    def w1_wait(n):
        arrived(mw.at[matrix[n], 0:3, half], w1_ss.at[n], w1_rs.at[n])

    def wy_start(n):
        wx_copy(n).wait()
        for d in (1, 3, 2):
            wy_copy(n, d).start()

    def wy_pass(n):
        arrived(mw.at[matrix[n], 0:3, half], wy_ss.at[n], wy_rs.at[n])
        w4_copy(n).start()

    def w2_pass(n):
        w2_copy(n).wait()
        w3_copy(n).start()

    def w3_pass(n):
        w3_copy(n).wait()
        w4_copy(n).start()

    wx_copy(1).start()
    wx_copy(3).start()
    w1_start(0)

    loads[4].wait()
    scatter_rows(ct_s, nn(row_order(), cot[...]))

    def c_copy(d):
        return remote(ct_s.at[fpeer(d)], ct_r.at[i], c_ss.at[0], c_rs.at[0], (fpeer(d), j))

    @pl.loop(1, 32)
    def _(d):
        c_copy(d).start()

    ct_r[i] = ct_s[i]
    loads[5].wait()
    loads[6].wait()
    qkv_r[j] = qkv_s[j]

    loads[7].wait()
    for t in range(4):
        spt[t] = spw[t].T

    arrived(qkv_r.at[0:7], q_ss.at[0], q_rs.at[0])

    q, k, v = (qkv_r[:, t].reshape(256, 384) for t in range(3))
    out = None
    for h in range(2):
        probs = softmax(head_of(q, h), k)
        prob_s[h] = probs
        term = nn(probs.astype(BF), head_of(v, h))
        out = term if out is None else out + term
    o_s[...] = out.astype(BF).reshape(8, 32, 384)

    def o_copy(d):
        return remote(o_s.at[qpeer(d)], o_r.at[j], o_ss.at[0], o_rs.at[0], (i, qpeer(d)))

    @pl.loop(1, 8)
    def _(d):
        o_copy(d).start()

    o_r[j] = o_s[j]
    w1_start(2)
    w1_wait(0)
    w2_copy(0).start()
    for c in wz:
        c.start()
    wy_start(1)
    w1_start(3)
    w2_pass(0)

    arrived(o_r.at[0:7], o_ss.at[0], o_rs.at[0])

    wy_start(3)
    so = join_pair(o_r[0:4].reshape(128, 384).astype(F32), o_r[4:8].reshape(128, 384).astype(F32)).astype(BF)
    hid[...] = (act[...].astype(F32) + nn(so, spt[3])).astype(BF)
    scatter_rows(hid_s, nn(row_order(), hid[...]))

    def h_copy(d):
        return remote(hid_s.at[fpeer(d)], hid_r.at[i], h_ss.at[0], h_rs.at[0], (fpeer(d), j))

    @pl.loop(1, 32)
    def _(d):
        h_copy(d).start()

    hid_r[i] = hid_s[i]
    w1_wait(2)
    w2_copy(2).start()

    arrived(ct_r.at[0:31], c_ss.at[0], c_rs.at[0])

    gather_rows(tx, ct_r)
    ctt[...] = tx[...].astype(BF)
    loads[9].wait()
    ctp = nn(ctt[...], perm[...]).astype(BF)

    @pl.when(core == 0)
    def _():
        ax[0, 0:128] = ctp

    @pl.when(core == 1)
    def _():
        fx[0] = ctp

    for c in wz:
        c.wait()
    w3_pass(0)
    wy_pass(1)
    w2_pass(2)

    def weight(n):
        return mw[n].reshape(C, W)

    arrived(hid_r.at[0:31], h_ss.at[0], h_rs.at[0])

    gather_rows(tx, hid_r)
    loads[8].wait()
    gain = mgn[...].reshape(1, C)
    u2, r2 = unit(tx[...])
    u2s[...] = u2
    r2s[...] = jnp.broadcast_to(r2, r2s.shape)
    n2s[...] = (u2 * gain + pe[...]).astype(BF)
    n2p = nn(n2s[...], perm[...]).astype(BF)
    ax[1, 0:128] = n2p
    fx[1] = n2p
    w3_pass(2)
    w4_copy(0).wait()
    w4_copy(1).wait()
    for t in range(2):
        mqkv[t] = nn(n2s[...], weight(t)).astype(BF)
    w1_wait(3)
    wy_pass(3)
    for h in range(HEADS):
        prob_t[h] = softmax(head_of(mqkv[0], h), mqkv[1])
    w4_copy(2).wait()
    mqkv[2] = nn(n2s[...], weight(2)).astype(BF)
    out = None
    for h in range(HEADS):
        term = nn(prob_t[h].astype(BF), head_of(mqkv[2], h))
        out = term if out is None else out + term
    mo_t = out.astype(BF)
    w4_copy(3).wait()
    mg = nn(ctt[...], weight(3)).astype(BF)
    dv = None
    for h in range(HEADS):
        term = tn(prob_t[h].astype(BF), head_of(mg, h))
        dv = term if dv is None else dv + term
    dv = dv.astype(BF)

    @pl.when(core == 0)
    def _():
        ay[0, 0:128] = mo_t
        fx[0] = n2p
        fy[0] = dv

    @pl.when(core == 1)
    def _():
        ax[0, 0:128] = n2p
        ay[0, 0:128] = dv
        fy[0] = mo_t

    swap = [remote(fx.at[0], ax.at[0, 128:256], x_ss.at[0], x_rs.at[0], sib),
            remote(fy.at[0], ay.at[0, 128:256], x_ss.at[1], x_rs.at[1], sib),
            remote(fx.at[1], ax.at[1, 128:256], x_ss.at[2], x_rs.at[2], sib)]
    for c in swap:
        c.start()

    scatter_rows(mo_s, mo_t.astype(F32))

    def m_copy(d):
        return remote(mo_s.at[fpeer(d)], mo_r.at[i], m_ss.at[0], m_rs.at[0], (fpeer(d), j))

    @pl.loop(1, 32)
    def _(d):
        m_copy(d).start()

    mo_r[i] = mo_s[i]

    dq = dk = None
    for h in range(HEADS):
        r = prob_t[h]
        dr = nt(head_of(mg, h), mqkv[2])
        delta = jnp.sum(r * dr, axis=-1, keepdims=True)
        ds = (r * (dr - delta) * SCALE).astype(BF)
        a, b = nn(ds, head_of(mqkv[1], h)), tn(ds, head_of(mqkv[0], h))
        dq, dk = (a, b) if dq is None else (dq + a, dk + b)
    dq, dk = dq.astype(BF), dk.astype(BF)

    @pl.when(core == 0)
    def _():
        ay[1, 0:128] = dq
        fy[1] = dk

    @pl.when(core == 1)
    def _():
        ay[1, 0:128] = dk
        fy[1] = dq

    swap_b = remote(fy.at[1], ay.at[1, 128:256], x_ss.at[3], x_rs.at[3], sib)
    swap_b.start()
    for c in swap:
        c.wait()
    wa[...] = tn(ax[0], ay[0]).reshape(2, 2, 2, 2, 2, 40, W).astype(BF)

    own = (x_hi, (x_hi + x_lo) % 2, y // 2, (y // 2 + y) % 2, z % 2)

    def zpeer(zz):
        return (x_lo * 16 + (zz + 8) % 8 * 2 + core, j)

    partner = {
        XA: beside, XB: cross,
        YA: (i, x_hi * 4 + y + 1 - 2 * (y % 2)), YB: (i, x_hi * 4 + 3 - y),
        ZA: zpeer(z + 1 - 2 * (z % 2)), ZB: zpeer(z - 1 + 2 * (z % 2)),
    }

    def left(p, step):
        return [n for n in range(5) if n not in [DIGIT[link] for link in PARTS[p][3][:step]]]

    def block(p, step, digits):
        which, lane, lanes, _ = PARTS[p]
        ref, columns = ((wa, wb)[which], slice(lane, lane + lanes)) if step == 0 else (buffers[6 * p + 2 * step - 1], slice(None))
        return ref, tuple(digits.get(n, slice(None)) for n in left(p, step)) + (slice(None), columns)

    def step_copy(p, step):
        link = PARTS[p][3][step]
        ref, at = block(p, step, {DIGIT[link]: 1 - own[DIGIT[link]]})
        return remote(ref.at[at], buffers[6 * p + 2 * step], p_ss.at[3 * p + step], p_rs.at[3 * p + step], partner[link])

    def direct(p):
        digits = left(p, 2)
        for mask in range(1, 8):
            to = [own[n] for n in range(4)]
            for bit, n in enumerate(digits):
                if mask >> bit & 1:
                    to[n] = 1 - own[n]
            ref, at = block(p, 2, {n: to[n] for n in digits})
            device = ((to[0] + to[1]) % 2 * 16 + zc, to[0] * 4 + to[2] * 2 + (to[2] + to[3]) % 2)
            remote(ref.at[at], buffers[6 * p + 4].at[mask - 1], p_ss.at[3 * p + 2], p_rs.at[3 * p + 2], device).start()

    done = [0] * 6

    def begin(p):
        step_copy(p, 0).start()

    def advance(p):
        step = done[p]
        step_copy(p, step).wait()
        link = PARTS[p][3][step]
        ref, at = block(p, step, {DIGIT[link]: own[DIGIT[link]]})
        buffers[6 * p + 2 * step + 1][...] = (
            ref[at].astype(F32) + buffers[6 * p + 2 * step][...].astype(F32)).astype(BF)
        done[p] = step + 1
        if step == 0:
            step_copy(p, 1).start()
        else:
            direct(p)

    def result(p):
        come = buffers[6 * p + 4]
        arrived(come, p_ss.at[3 * p + 2], p_rs.at[3 * p + 2])
        ref, at = block(p, 2, {n: own[n] for n in left(p, 2)})
        total = ref[at].astype(F32)
        for n in range(7):
            total = total + come[n].astype(F32)
        return total.astype(BF)

    for p in (0, 1, 2):
        begin(p)
    dn2 = nt(dq, weight(0)) + nt(dk, weight(1)) + nt(dv, weight(2))
    u2 = u2s[...]
    gv1[...] = jnp.sum(dn2 * u2, axis=0, keepdims=True)
    back = ctt[...].astype(F32) + unit_back(dn2, u2, r2s[:, 0:1], gain)
    scatter_rows(lb_s, back)

    def l_copy(d):
        return remote(lb_s.at[fpeer(d)], lb_r.at[i], l_ss.at[0], l_rs.at[0], (fpeer(d), j))

    @pl.loop(1, 32)
    def _(d):
        l_copy(d).start()

    lb_r[i] = lb_s[i]

    def v_copy(src, dst, n, dev):
        return remote(src, dst, v_ss.at[n], v_rs.at[n], dev)

    gx = [v_copy(gv1, gr1.at[d - 1], 0, xpeer(d)) for d in range(1, 4)]
    for c in gx:
        c.start()

    swap_b.wait()
    wb[...] = tn(ax[1], ay[1]).reshape(2, 2, 2, 2, 2, 40, W).astype(BF)

    for p in (3, 4, 5):
        begin(p)

    arrived(mo_r.at[0:31], m_ss.at[0], m_rs.at[0])

    gather_rows(mof, mo_r)
    mo = tn(row_order(), mof[...].astype(BF)).astype(BF)
    bo[...] = (hid[...].astype(F32) + nt(mo, weight(3))).astype(BF)
    bo_store = pltpu.make_async_copy(bo, bo_h, st.at[0])
    bo_store.start()

    advance(2)
    advance(0)
    advance(1)

    arrived(lb_r.at[0:31], l_ss.at[0], l_rs.at[0])

    gather_rows(tx, lb_r)
    gh[...] = tn(row_order(), tx[...].astype(BF)).astype(BF)
    for hp, part in enumerate(split_pair(nn(gh[...], spw[3]))):
        gs_s[hp * 4:hp * 4 + 4] = part.astype(BF).reshape(4, 32, 384)

    def gs_copy(d):
        return remote(gs_s.at[qpeer(d)], gs_r.at[j], gs_ss.at[0], gs_rs.at[0], (i, qpeer(d)))

    @pl.loop(1, 8)
    def _(d):
        gs_copy(d).start()

    gs_r[j] = gs_s[j]

    arrived(gr1, v_ss.at[0], v_rs.at[0])
    gv2[...] = gv1[...] + gr1[0] + gr1[1] + gr1[2]
    gy = [v_copy(gv2, gr2.at[d - 1], 1, ypeer(d)) for d in range(1, 4)]
    for c in gy:
        c.start()
    advance(4)
    advance(5)
    advance(3)
    arrived(gs_r.at[0:7], gs_ss.at[0], gs_rs.at[0])
    advance(2)
    advance(0)
    advance(1)
    advance(4)
    advance(5)
    advance(3)

    q, k, v = (qkv_r[:, t].reshape(256, 384) for t in range(3))
    for t, grad in enumerate(attend_back(q, k, v, gs_r[...].reshape(256, 384), prob_s, 2)):
        dq_s[:, t] = grad.astype(BF).reshape(8, 32, 384)

    def dq_copy(d):
        return remote(dq_s.at[qpeer(d)], dq_r.at[j], dq_ss.at[0], dq_rs.at[0], (i, qpeer(d)))

    @pl.loop(1, 8)
    def _(d):
        dq_copy(d).start()

    dq_r[j] = dq_s[j]

    arrived(gr2, v_ss.at[1], v_rs.at[1])
    gv3[...] = gv2[...] + gr2[0] + gr2[1] + gr2[2]
    gz = v_copy(gv3, gr3, 2, partner[ZA])
    gz.start()

    row = lax.broadcasted_iota(jnp.int32, (128, 40), 0)
    col = lax.broadcasted_iota(jnp.int32, (128, 40), 1)
    first = jnp.where((row % 16 < 5) & (col == (row // 16) * 5 + row % 16), 1.0, 0.0).astype(BF)
    second = jnp.where((row % 16 >= 5) & (row % 16 < 10) & (col == (row // 16) * 5 + row % 16 - 5), 1.0, 0.0).astype(BF)
    gz.wait()
    gv = gv3[...] + gr3[...]
    sum_a = jnp.concatenate([result(p) for p in (0, 1, 2)], axis=1)
    sum_b = jnp.concatenate([result(p) for p in (3, 4, 5)], axis=1)
    slabs = nn(first, sum_a) + nn(second, sum_b)
    row = lax.broadcasted_iota(jnp.int32, (128, W), 0) % 16
    slabs = jnp.where(row == 10, gv[:, :W], jnp.where(row == 11, gv[:, W:], slabs))
    p3[...] = slabs.astype(BF).reshape(8, 16, W)
    place = z // 2 * 2 + core

    def z_copy(d):
        to = (place + d) % 8
        return remote(p3.at[to], r3.at[place], r3_ss.at[0], r3_rs.at[0],
                      (x_lo * 16 + to // 2 * 4 + z % 2 * 2 + to % 2, j))

    @pl.loop(1, 8)
    def _(d):
        z_copy(d).start()

    r3[place] = p3[place]

    arrived(dq_r.at[0:7], dq_ss.at[0], dq_rs.at[0])

    total = None
    for t in range(3):
        grad = join_pair(dq_r[0:4, t].reshape(128, 384).astype(F32), dq_r[4:8, t].reshape(128, 384).astype(F32)).astype(BF)
        term = nn(grad, spt[t])
        total = term if total is None else total + term
    u1, r1 = unit(act[...].astype(F32))
    ig[...] = (gh[...].astype(F32) + unit_back(total, u1, r1, spg[...].reshape(1, C))).astype(BF)
    ig_store = pltpu.make_async_copy(ig, ig_h, st.at[1])
    ig_store.start()

    arrived(r3.at[0:7], r3_ss.at[0], r3_rs.at[0])

    factor = 1.0 / math.sqrt(128 * 256)
    sums = []
    for c in range(2):
        total = r3[c].astype(F32)
        for n in range(1, 4):
            total = total + r3[2 * n + c].astype(F32)
        sums.append(total * factor)
    wg[:, 0] = sums[0][5:10]
    wg[:, 1] = sums[1][5:10]
    wg[:, 2] = sums[1][0:5]
    wg[:, 3] = sums[0][0:5]
    both = sums[0] + sums[1]
    gn[...] = jnp.concatenate([both[10:11], both[11:12]], axis=1)
    bo_store.wait()
    ig_store.wait()


def finish(bo_h, ig_h, wg_h, gn, bo, ig, wg, gg, bo_v, ig_v, wg_v, sems):
    moves = [(bo_h, bo_v, bo), (ig_h, ig_v, ig), (wg_h, wg_v, wg)]
    come = [pltpu.make_async_copy(a, b, sems.at[0, n]) for n, (a, b, _) in enumerate(moves)]
    go = [pltpu.make_async_copy(b, c, sems.at[1, n]) for n, (_, b, c) in enumerate(moves)]
    for c in come:
        c.start()
    device = lax.axis_index("frame") * 8 + lax.axis_index("quad")
    gg[...] = pltpu.roll(gn[...], C - device * 5, 1)[0, :5]
    for a, b in zip(come, go):
        a.wait()
        b.start()
    for c in go:
        c.wait()


def positional(frames, channels):
    freq = np.exp(np.arange(channels // 2, dtype=np.float32)[None, :] * np.float32(-2.0 * math.log(10000.0) / channels))
    phases = np.arange(frames, dtype=np.float32)[:, None] * freq.astype(np.float32)
    both = np.stack([np.sin(phases.astype(np.float64)), np.cos(phases.astype(np.float64))], axis=-1)
    return both.reshape(frames, channels).astype(np.float32)


def permutation():
    matrix = np.zeros((C, C), np.float32)
    for m in range(C):
        rest, r = divmod(m, 5)
        rest, core = divmod(rest, 2)
        rest, z_high = divmod(rest, 4)
        xb, xa, yb, ya, z_low = (rest // 16) % 2, (rest // 8) % 2, (rest // 4) % 2, (rest // 2) % 2, rest % 2
        y = yb * 2 + (yb + ya) % 2
        n = (xb + xa) % 2 * 640 + (z_high * 2 + z_low) * 80 + core * 40 + xb * 20 + y * 5 + r
        matrix[n, m] = 1.0
    return matrix


def part_buffers():
    shapes = []
    for _, _, lanes, _ in PARTS:
        shapes += [pltpu.VMEM((2, 2, 2, 2, 40, lanes), BF)] * 2 + [pltpu.VMEM((2, 2, 2, 40, lanes), BF)] * 2
        shapes += [pltpu.VMEM((7, 40, lanes), BF), pltpu.VMEM((8, 128), BF)]
    return shapes


def local(activations, cotangent, spatial_weights, spatial_gain, motion_weights, motion_gain):
    pe = jnp.asarray(positional(128, C))
    perm = jnp.asarray(permutation(), dtype=BF)
    V, D = pltpu.VMEM, pltpu.SemaphoreType.DMA
    any_, vmem = pl.BlockSpec(memory_space=pl.ANY), pl.BlockSpec(memory_space=pltpu.VMEM)
    scratch = [
        V((128, C), BF), V((128, C), BF), V((4, C, W), BF), V((4, W, C), BF), V((4, 8, 160, W), BF), V((128, C), F32), V((C, C), BF),
        V((128, C), BF), V((128, C), BF),
        V((8, 3, 32, 384), BF), V((8, 3, 32, 384), BF), V((8, 32, 384), BF), V((8, 32, 384), BF), V((2, 256, 256), F32),
        V((128, C), BF), V((32, 4, C), BF), V((32, 4, C), BF), V((32, 4, C), BF), V((32, 4, C), BF), V((128, C), BF),
        V((128, C), F32), V((128, C), BF), V((128, C), F32), V((128, 128), F32), V((3, 128, W), BF), V((4, 128, 128), F32),
        V((32, 4, W), BF), V((32, 4, W), BF), V((32, 4, C), BF), V((32, 4, C), BF), V((128, C), BF), V((128, W), F32),
        V((8, 32, 384), BF), V((8, 32, 384), BF), V((8, 3, 32, 384), BF), V((8, 3, 32, 384), BF),
        V((2, 128, C), BF), V((2, 128, W), BF), V((2, 256, C), BF), V((2, 256, W), BF),
        V((2, 2, 2, 2, 2, 40, W), BF), V((2, 2, 2, 2, 2, 40, W), BF), V((8, 16, W), BF), V((8, 16, W), BF),
        V((1, C), F32), V((3, 1, C), F32), V((1, C), F32), V((3, 1, C), F32), V((1, C), F32), V((1, C), F32),
        D((10,)), D((2,))] + [D((4,))] * 14 + [D((1,))] * 16 + [
        D((4,)), D((4,)), D((18,)), D((18,)), D((1,)), D((1,)),
        D((3,)), D((3,)),
    ] + part_buffers()
    results = (
        jax.ShapeDtypeStruct((128, C), BF),
        jax.ShapeDtypeStruct((128, C), BF),
        jax.ShapeDtypeStruct((5, 4, W), F32),
    )
    block_output, input_grad, weight_grad, gain_all = pl.pallas_call(
        kernel,
        out_shape=results + (jax.ShapeDtypeStruct((1, C), F32),),
        in_specs=[any_, any_, any_, vmem, any_, vmem, any_, any_],
        out_specs=(any_, any_, vmem, vmem),
        scratch_shapes=scratch,
        compiler_params=pltpu.CompilerParams(
            has_side_effects=True, collective_id=0, vmem_limit_bytes=60 * 2 ** 20),
    )(
        activations.reshape(128, C), cotangent.reshape(128, C), spatial_weights, spatial_gain,
        motion_weights, motion_gain, pe, perm,
    )
    block_output, input_grad, weight_grad, gain_grad = pl.pallas_call(
        finish,
        out_shape=results + (jax.ShapeDtypeStruct((5,), F32),),
        in_specs=[any_, any_, any_, vmem],
        out_specs=(any_, any_, any_, vmem),
        scratch_shapes=[V((128, C), BF), V((128, C), BF), V((5, 4, W), F32), D((2, 3))],
        compiler_params=pltpu.CompilerParams(vmem_limit_bytes=60 * 2 ** 20),
    )(block_output, input_grad, weight_grad, gain_all)
    shape = activations.shape
    return block_output.reshape(shape), input_grad.reshape(shape), weight_grad.transpose(1, 0, 2), gain_grad


def solution(mesh):
    in_specs = (
        P("frame", "quad", None),
        P("frame", "quad", None),
        P(),
        P(),
        P(None, "quad", None),
        P(),
    )
    out_specs = (
        P("frame", "quad", None),
        P("frame", "quad", None),
        P(None, ("frame", "quad"), None),
        P(("frame", "quad")),
    )
    return jax.shard_map(local, mesh=mesh, in_specs=in_specs, out_specs=out_specs, check_vma=False)
```

```python
import math

import jax
import jax.numpy as jnp
import numpy as np
from jax import lax
from jax.experimental import pallas as pl
from jax.experimental.pallas import tpu as pltpu
from jax.sharding import PartitionSpec as P

HEADS = 4
HEAD_DIM = 160
EPSILON = 1e-05
SCALE = HEAD_DIM ** (-0.5)
C = 1280
W = 640
F32 = jnp.float32
BF = jnp.bfloat16
XA, XB, YA, YB, ZA, ZB = range(6)
DIGIT = {XB: 0, XA: 1, YB: 2, YA: 3, ZA: 4, ZB: 4}
PARTS = (
    (0, 0, 256, (XB, ZA)),
    (0, 256, 256, (YA, ZB)),
    (0, 512, 128, (YB, ZA)),
    (1, 0, 128, (XA, YA)),
    (1, 128, 256, (YB, XB)),
    (1, 384, 128, (XB, YB)),
    (1, 512, 128, (YA, XA)),
)
MESH = pl.DeviceIdType.MESH


def nn(a, b):
    return jnp.dot(a, b, preferred_element_type=F32)


def nt(a, b):
    return lax.dot_general(a, b, (((1,), (1,)), ((), ())), preferred_element_type=F32)


def tn(a, b):
    return lax.dot_general(a, b, (((0,), (0,)), ((), ())), preferred_element_type=F32)


def unit(x):
    xc = x - jnp.mean(x, axis=-1, keepdims=True)
    r = lax.rsqrt(jnp.mean(xc * xc, axis=-1, keepdims=True) + EPSILON)
    return xc * r, r


def unit_back(grad, u, r, gain):
    g = grad * gain
    return r * (g - jnp.mean(g, axis=-1, keepdims=True) - u * jnp.mean(g * u, axis=-1, keepdims=True))


def head_of(x, h):
    lane = lax.broadcasted_iota(jnp.int32, x.shape, 1)
    return jnp.where((lane >= h * HEAD_DIM) & (lane < (h + 1) * HEAD_DIM), x, jnp.zeros_like(x))


def split_pair(y):
    return y[:, :384], pltpu.roll(y, 320, 1)[:, :384]


def join_pair(a, b):
    pad = jnp.zeros((a.shape[0], 256), F32)
    left = jnp.concatenate([a, pad], axis=1)
    right = pltpu.roll(jnp.concatenate([b, pad], axis=1), 320, 1)
    lane = lax.broadcasted_iota(jnp.int32, left.shape, 1)
    return jnp.where(lane < 320, left, right)


def row_order():
    row = lax.broadcasted_iota(jnp.int32, (128, 128), 0)
    col = lax.broadcasted_iota(jnp.int32, (128, 128), 1)
    return jnp.where(col == (row % 4) * 32 + row // 4, 1.0, 0.0).astype(BF)


def scatter_rows(to, rows):
    for n in range(32):
        to[n] = rows[4 * n:4 * n + 4, :].astype(BF)


def gather_rows(rows, come):
    for n in range(32):
        rows[4 * n:4 * n + 4, :] = come[n].astype(F32)


def softmax(q, k):
    s = nt(q, k) * SCALE
    e = jnp.exp(s - jnp.max(s, axis=-1, keepdims=True))
    return e / jnp.sum(e, axis=-1, keepdims=True)


def attend_back(q, k, v, g, probs, heads):
    dq = dk = dv = None
    for h in range(heads):
        r = probs[h]
        dr = nt(head_of(g, h), v)
        delta = jnp.sum(r * dr, axis=-1, keepdims=True)
        ds = (r * (dr - delta) * SCALE).astype(BF)
        a, b, c = nn(ds, head_of(k, h)), tn(ds, head_of(q, h)), tn(r.astype(BF), head_of(g, h))
        dq, dk, dv = (a, b, c) if dq is None else (dq + a, dk + b, dv + c)
    return dq, dk, dv


def kernel(act_h, cot_h, spw_h, spg, mw_h, mgn, pe_h, perm_h,
           bo_h, ig_h, wg_h,
           act, cot, spw, spt, mw, pe, perm, bo, ig, wg,
           qkv_s, qkv_r, o_s, o_r, prob_s,
           hid, hid_s, hid_r, ct_s, ct_r, ctt, tx, n2s, u2s, r2s, mqkv, prob_t,
           mo_s, mo_r, lb_s, lb_r, gh, mof,
           gs_s, gs_r, dq_s, dq_r,
           fx, fy, ax, ay, wa, wb, p3, r3,
           gv1, gr1, gv2, gr2, gv3, gr3,
           ld, st, w1_ss, w1_rs, w2_ss, w2_rs, w3_ss, w3_rs, w4_ss, w4_rs, wz_ss, wz_rs, wx_ss, wx_rs, wy_ss, wy_rs,
           q_ss, q_rs, o_ss, o_rs, h_ss, h_rs, c_ss, c_rs,
           m_ss, m_rs, l_ss, l_rs, gs_ss, gs_rs, dq_ss, dq_rs, x_ss, x_rs,
           p_ss, p_rs, r3_ss, r3_rs,
           v_ss, v_rs, *buffers):
    i, j = lax.axis_index("frame"), lax.axis_index("quad")
    core, z, x_lo = i % 2, (i // 2) % 8, i // 16
    y, x_hi = j % 4, j // 4
    x = x_hi * 2 + x_lo
    zc = i % 16
    sib = (i + 1 - 2 * core, j)
    cross = ((1 - x_lo) * 16 + zc, (1 - x_hi) * 4 + y)
    beside = ((1 - x_lo) * 16 + zc, j)
    even = z % 2
    above = (x_lo * 16 + (zc + 2) % 16, j)
    below = (x_lo * 16 + (zc + 14) % 16, j)

    def fpeer(d):
        return (i + d) % 32

    def qpeer(d):
        return (j + d) % 8

    def xpeer(d):
        xx = (x + d) % 4
        return ((xx % 2) * 16 + zc, (xx // 2) * 4 + y)

    def ypeer(d):
        return (i, x_hi * 4 + (y + d) % 4)

    def remote(src, dst, ss, rs, dev):
        return pltpu.make_async_remote_copy(
            src_ref=src, dst_ref=dst, send_sem=ss, recv_sem=rs, device_id=dev, device_id_type=MESH)

    def arrived(part, ss, rs):
        pltpu.make_async_copy(part, part, ss).wait()
        pltpu.make_async_copy(part, part, rs).wait()

    half = pl.ds(pl.multiple_of(core * 80, 16), 80)
    loads = [
        pltpu.make_async_copy(act_h, act, ld.at[0]),
        pltpu.make_async_copy(spw_h.at[0], spw.at[0], ld.at[1]),
        pltpu.make_async_copy(spw_h.at[1], spw.at[1], ld.at[2]),
        pltpu.make_async_copy(spw_h.at[2], spw.at[2], ld.at[3]),
        pltpu.make_async_copy(cot_h, cot, ld.at[5]),
        pltpu.make_async_copy(mw_h.at[even, half], mw.at[even, j, half], ld.at[6]),
        pltpu.make_async_copy(mw_h.at[2:4, half], mw.at[2:4, j, half], ld.at[9]),
        pltpu.make_async_copy(spw_h.at[3], spw.at[3], ld.at[4]),
        pltpu.make_async_copy(pe_h, pe, ld.at[7]),
        pltpu.make_async_copy(perm_h, perm, ld.at[8]),
    ]
    for c in loads:
        c.start()

    bar = pltpu.get_barrier_semaphore()

    @pl.loop(1, 32)
    def _(d):
        pl.semaphore_signal(bar, inc=1, device_id=(fpeer(d), j), device_id_type=MESH)

    @pl.loop(1, 8)
    def _(d):
        pl.semaphore_signal(bar, inc=1, device_id=(i, qpeer(d)), device_id_type=MESH)

    @pl.loop(1, 8)
    def _(d):
        pl.semaphore_signal(bar, inc=1, device_id=((1 - x_lo) * 16 + zc, qpeer(d)), device_id_type=MESH)
        for n in range(2):
            near = n * 16 + z // 2 * 4 + (1 - even) * 2 + core
            pl.semaphore_signal(bar, inc=1, device_id=(near, qpeer(d)), device_id_type=MESH)

    loads[0].wait()
    u1, _ = unit(act[...].astype(F32))
    n1 = (u1 * spg[...].reshape(1, C)).astype(BF)
    for t in range(3):
        loads[1 + t].wait()
        for hp, part in enumerate(split_pair(nn(n1, spw[t]))):
            qkv_s[hp * 4:hp * 4 + 4, t] = part.astype(BF).reshape(4, 32, 384)
    pl.semaphore_wait(bar, 59)

    def q_copy(d):
        return remote(qkv_s.at[qpeer(d)], qkv_r.at[j], q_ss.at[0], q_rs.at[0], (i, qpeer(d)))

    @pl.loop(1, 8)
    def _(d):
        q_copy(d).start()

    matrix = (even, 1 - even, 2, 3)

    def w1_copy(n, d):
        m = matrix[n]
        return remote(mw_h.at[m, half], mw.at[m, j, half], w1_ss.at[n], w1_rs.at[n], ypeer(d))

    def w2_copy(n):
        part = mw.at[matrix[n], pl.ds(x_hi * 4 + 2 * (1 - x_lo), 2), half]
        return remote(part, part, w2_ss.at[n], w2_rs.at[n], cross)

    def w3_copy(n):
        part = mw.at[matrix[n], pl.ds((1 - x_hi) * 4 + 2 * x_lo, 2), half]
        return remote(part, part, w3_ss.at[n], w3_rs.at[n], beside)

    def w4_copy(n):
        part = mw.at[matrix[n], :, half]
        return remote(part, part, w4_ss.at[n], w4_rs.at[n], sib)

    up, down = mw.at[even, pl.ds(x_hi * 4, 2), half], mw.at[even, pl.ds(x_hi * 4 + 2, 2), half]
    wz = [remote(up, up, wz_ss.at[0], wz_rs.at[0], above),
          remote(down, down, wz_ss.at[1], wz_rs.at[1], below)]

    def wx_copy(n):
        m = matrix[n]
        return remote(mw_h.at[m, half], mw.at[m, j, half], wx_ss.at[n], wx_rs.at[n], cross)

    def wy_copy(n, d):
        part = mw.at[matrix[n], (1 - x_hi) * 4 + y, half]
        return remote(part, part, wy_ss.at[n], wy_rs.at[n], ypeer(d))

    def w1_start(n):
        for d in (1, 3, 2):
            w1_copy(n, d).start()

    def w1_wait(n):
        arrived(mw.at[matrix[n], 0:3, half], w1_ss.at[n], w1_rs.at[n])

    def wy_start(n):
        wx_copy(n).wait()
        for d in (1, 3, 2):
            wy_copy(n, d).start()

    def wy_pass(n):
        arrived(mw.at[matrix[n], 0:3, half], wy_ss.at[n], wy_rs.at[n])
        w4_copy(n).start()

    def w2_pass(n):
        w2_copy(n).wait()
        w3_copy(n).start()

    def w3_pass(n):
        w3_copy(n).wait()
        w4_copy(n).start()

    wx_copy(1).start()
    wx_copy(3).start()
    w1_start(0)

    loads[4].wait()
    scatter_rows(ct_s, nn(row_order(), cot[...]))

    def c_copy(d):
        return remote(ct_s.at[fpeer(d)], ct_r.at[i], c_ss.at[0], c_rs.at[0], (fpeer(d), j))

    @pl.loop(1, 32)
    def _(d):
        c_copy(d).start()

    ct_r[i] = ct_s[i]
    loads[5].wait()
    loads[6].wait()
    qkv_r[j] = qkv_s[j]

    loads[7].wait()
    for t in range(4):
        spt[t] = spw[t].T

    arrived(qkv_r.at[0:7], q_ss.at[0], q_rs.at[0])

    q, k, v = (qkv_r[:, t].reshape(256, 384) for t in range(3))
    out = None
    for h in range(2):
        probs = softmax(head_of(q, h), k)
        prob_s[h] = probs
        term = nn(probs.astype(BF), head_of(v, h))
        out = term if out is None else out + term
    o_s[...] = out.astype(BF).reshape(8, 32, 384)

    def o_copy(d):
        return remote(o_s.at[qpeer(d)], o_r.at[j], o_ss.at[0], o_rs.at[0], (i, qpeer(d)))

    @pl.loop(1, 8)
    def _(d):
        o_copy(d).start()

    o_r[j] = o_s[j]
    w1_start(2)
    w1_wait(0)
    w2_copy(0).start()
    for c in wz:
        c.start()
    wy_start(1)
    w2_pass(0)

    arrived(o_r.at[0:7], o_ss.at[0], o_rs.at[0])

    w1_start(3)
    wy_start(3)
    so = join_pair(o_r[0:4].reshape(128, 384).astype(F32), o_r[4:8].reshape(128, 384).astype(F32)).astype(BF)
    hid[...] = (act[...].astype(F32) + nn(so, spt[3])).astype(BF)
    scatter_rows(hid_s, nn(row_order(), hid[...]))

    def h_copy(d):
        return remote(hid_s.at[fpeer(d)], hid_r.at[i], h_ss.at[0], h_rs.at[0], (fpeer(d), j))

    @pl.loop(1, 32)
    def _(d):
        h_copy(d).start()

    hid_r[i] = hid_s[i]
    w1_wait(2)
    w2_copy(2).start()

    arrived(ct_r.at[0:31], c_ss.at[0], c_rs.at[0])

    gather_rows(tx, ct_r)
    ctt[...] = tx[...].astype(BF)
    loads[9].wait()
    ctp = nn(ctt[...], perm[...]).astype(BF)

    @pl.when(core == 0)
    def _():
        ax[0, 0:128] = ctp

    @pl.when(core == 1)
    def _():
        fx[0] = ctp

    for c in wz:
        c.wait()
    w3_pass(0)
    wy_pass(1)
    w2_pass(2)

    def weight(n):
        return mw[n].reshape(C, W)

    arrived(hid_r.at[0:31], h_ss.at[0], h_rs.at[0])

    gather_rows(tx, hid_r)
    loads[8].wait()
    gain = mgn[...].reshape(1, C)
    u2, r2 = unit(tx[...])
    u2s[...] = u2
    r2s[...] = jnp.broadcast_to(r2, r2s.shape)
    n2s[...] = (u2 * gain + pe[...]).astype(BF)
    n2p = nn(n2s[...], perm[...]).astype(BF)
    ax[1, 0:128] = n2p
    fx[1] = n2p
    w3_pass(2)
    w4_copy(0).wait()
    w4_copy(1).wait()
    for t in range(2):
        mqkv[t] = nn(n2s[...], weight(t)).astype(BF)
    w1_wait(3)
    wy_pass(3)
    for h in range(HEADS):
        prob_t[h] = softmax(head_of(mqkv[0], h), mqkv[1])
    w4_copy(2).wait()
    mqkv[2] = nn(n2s[...], weight(2)).astype(BF)
    out = None
    for h in range(HEADS):
        term = nn(prob_t[h].astype(BF), head_of(mqkv[2], h))
        out = term if out is None else out + term
    mo_t = out.astype(BF)
    w4_copy(3).wait()
    mg = nn(ctt[...], weight(3)).astype(BF)
    dv = None
    for h in range(HEADS):
        term = tn(prob_t[h].astype(BF), head_of(mg, h))
        dv = term if dv is None else dv + term
    dv = dv.astype(BF)

    @pl.when(core == 0)
    def _():
        ay[0, 0:128] = mo_t
        fx[0] = n2p
        fy[0] = dv

    @pl.when(core == 1)
    def _():
        ax[0, 0:128] = n2p
        ay[0, 0:128] = dv
        fy[0] = mo_t

    swap = [remote(fx.at[0], ax.at[0, 128:256], x_ss.at[0], x_rs.at[0], sib),
            remote(fy.at[0], ay.at[0, 128:256], x_ss.at[1], x_rs.at[1], sib),
            remote(fx.at[1], ax.at[1, 128:256], x_ss.at[2], x_rs.at[2], sib)]
    for c in swap:
        c.start()

    scatter_rows(mo_s, mo_t.astype(F32))

    def m_copy(d):
        return remote(mo_s.at[fpeer(d)], mo_r.at[i], m_ss.at[0], m_rs.at[0], (fpeer(d), j))

    @pl.loop(1, 32)
    def _(d):
        m_copy(d).start()

    mo_r[i] = mo_s[i]

    dq = dk = None
    for h in range(HEADS):
        r = prob_t[h]
        dr = nt(head_of(mg, h), mqkv[2])
        delta = jnp.sum(r * dr, axis=-1, keepdims=True)
        ds = (r * (dr - delta) * SCALE).astype(BF)
        a, b = nn(ds, head_of(mqkv[1], h)), tn(ds, head_of(mqkv[0], h))
        dq, dk = (a, b) if dq is None else (dq + a, dk + b)
    dq, dk = dq.astype(BF), dk.astype(BF)

    @pl.when(core == 0)
    def _():
        ay[1, 0:128] = dq
        fy[1] = dk

    @pl.when(core == 1)
    def _():
        ay[1, 0:128] = dk
        fy[1] = dq

    swap_b = remote(fy.at[1], ay.at[1, 128:256], x_ss.at[3], x_rs.at[3], sib)
    swap_b.start()
    for c in swap:
        c.wait()
    wa[...] = tn(ax[0], ay[0]).reshape(2, 2, 2, 2, 2, 40, W).astype(BF)

    own = (x_hi, (x_hi + x_lo) % 2, y // 2, (y // 2 + y) % 2, z % 2)

    def zpeer(zz):
        return (x_lo * 16 + (zz + 8) % 8 * 2 + core, j)

    partner = {
        XA: beside, XB: cross,
        YA: (i, x_hi * 4 + y + 1 - 2 * (y % 2)), YB: (i, x_hi * 4 + 3 - y),
        ZA: zpeer(z + 1 - 2 * (z % 2)), ZB: zpeer(z - 1 + 2 * (z % 2)),
    }

    def left(p, step):
        return [n for n in range(5) if n not in [DIGIT[link] for link in PARTS[p][3][:step]]]

    def block(p, step, digits):
        which, lane, lanes, _ = PARTS[p]
        ref, columns = ((wa, wb)[which], slice(lane, lane + lanes)) if step == 0 else (buffers[6 * p + 2 * step - 1], slice(None))
        return ref, tuple(digits.get(n, slice(None)) for n in left(p, step)) + (slice(None), columns)

    def step_copy(p, step):
        link = PARTS[p][3][step]
        ref, at = block(p, step, {DIGIT[link]: 1 - own[DIGIT[link]]})
        return remote(ref.at[at], buffers[6 * p + 2 * step], p_ss.at[3 * p + step], p_rs.at[3 * p + step], partner[link])

    def direct(p):
        digits = left(p, 2)
        for mask in range(1, 8):
            to = list(own)
            for bit, n in enumerate(digits):
                if mask >> bit & 1:
                    to[n] = 1 - own[n]
            ref, at = block(p, 2, {n: to[n] for n in digits})
            device = ((to[0] + to[1]) % 2 * 16 + z // 2 * 4 + to[4] * 2 + core, to[0] * 4 + to[2] * 2 + (to[2] + to[3]) % 2)
            remote(ref.at[at], buffers[6 * p + 4].at[mask - 1], p_ss.at[3 * p + 2], p_rs.at[3 * p + 2], device).start()

    done = [0] * 7

    def begin(p):
        step_copy(p, 0).start()

    def advance(p):
        step = done[p]
        step_copy(p, step).wait()
        link = PARTS[p][3][step]
        ref, at = block(p, step, {DIGIT[link]: own[DIGIT[link]]})
        buffers[6 * p + 2 * step + 1][...] = (
            ref[at].astype(F32) + buffers[6 * p + 2 * step][...].astype(F32)).astype(BF)
        done[p] = step + 1
        if step == 0:
            step_copy(p, 1).start()
        else:
            direct(p)

    def result(p):
        come = buffers[6 * p + 4]
        arrived(come, p_ss.at[3 * p + 2], p_rs.at[3 * p + 2])
        ref, at = block(p, 2, {n: own[n] for n in left(p, 2)})
        total = ref[at].astype(F32)
        for n in range(7):
            total = total + come[n].astype(F32)
        return total.astype(BF)

    for p in (0, 1, 2):
        begin(p)
    dn2 = nt(dq, weight(0)) + nt(dk, weight(1)) + nt(dv, weight(2))
    u2 = u2s[...]
    gv1[...] = jnp.sum(dn2 * u2, axis=0, keepdims=True)
    back = ctt[...].astype(F32) + unit_back(dn2, u2, r2s[:, 0:1], gain)
    scatter_rows(lb_s, back)

    def l_copy(d):
        return remote(lb_s.at[fpeer(d)], lb_r.at[i], l_ss.at[0], l_rs.at[0], (fpeer(d), j))

    @pl.loop(1, 32)
    def _(d):
        l_copy(d).start()

    lb_r[i] = lb_s[i]

    def v_copy(src, dst, n, dev):
        return remote(src, dst, v_ss.at[n], v_rs.at[n], dev)

    gx = [v_copy(gv1, gr1.at[d - 1], 0, xpeer(d)) for d in range(1, 4)]
    for c in gx:
        c.start()

    swap_b.wait()
    wb[...] = tn(ax[1], ay[1]).reshape(2, 2, 2, 2, 2, 40, W).astype(BF)

    for p in (3, 4, 5, 6):
        begin(p)

    arrived(mo_r.at[0:31], m_ss.at[0], m_rs.at[0])

    gather_rows(mof, mo_r)
    mo = tn(row_order(), mof[...].astype(BF)).astype(BF)
    bo[...] = (hid[...].astype(F32) + nt(mo, weight(3))).astype(BF)
    bo_store = pltpu.make_async_copy(bo, bo_h, st.at[0])
    bo_store.start()

    advance(2)
    advance(0)
    advance(1)

    arrived(lb_r.at[0:31], l_ss.at[0], l_rs.at[0])

    gather_rows(tx, lb_r)
    gh[...] = tn(row_order(), tx[...].astype(BF)).astype(BF)
    for hp, part in enumerate(split_pair(nn(gh[...], spw[3]))):
        gs_s[hp * 4:hp * 4 + 4] = part.astype(BF).reshape(4, 32, 384)

    def gs_copy(d):
        return remote(gs_s.at[qpeer(d)], gs_r.at[j], gs_ss.at[0], gs_rs.at[0], (i, qpeer(d)))

    @pl.loop(1, 8)
    def _(d):
        gs_copy(d).start()

    gs_r[j] = gs_s[j]

    arrived(gr1, v_ss.at[0], v_rs.at[0])
    gv2[...] = gv1[...] + gr1[0] + gr1[1] + gr1[2]
    gy = [v_copy(gv2, gr2.at[d - 1], 1, ypeer(d)) for d in range(1, 4)]
    for c in gy:
        c.start()
    advance(5)
    advance(6)
    advance(4)
    advance(3)
    arrived(gs_r.at[0:7], gs_ss.at[0], gs_rs.at[0])
    advance(2)
    advance(0)
    advance(1)

    q, k, v = (qkv_r[:, t].reshape(256, 384) for t in range(3))
    for t, grad in enumerate(attend_back(q, k, v, gs_r[...].reshape(256, 384), prob_s, 2)):
        dq_s[:, t] = grad.astype(BF).reshape(8, 32, 384)

    advance(5)
    advance(6)
    advance(3)
    advance(4)

    def dq_copy(d):
        return remote(dq_s.at[qpeer(d)], dq_r.at[j], dq_ss.at[0], dq_rs.at[0], (i, qpeer(d)))

    @pl.loop(1, 8)
    def _(d):
        dq_copy(d).start()

    dq_r[j] = dq_s[j]

    arrived(gr2, v_ss.at[1], v_rs.at[1])
    gv3[...] = gv2[...] + gr2[0] + gr2[1] + gr2[2]
    gz = v_copy(gv3, gr3, 2, partner[ZA])
    gz.start()

    row = lax.broadcasted_iota(jnp.int32, (128, 40), 0)
    col = lax.broadcasted_iota(jnp.int32, (128, 40), 1)
    first = jnp.where((row % 16 < 5) & (col == (row // 16) * 5 + row % 16), 1.0, 0.0).astype(BF)
    second = jnp.where((row % 16 >= 5) & (row % 16 < 10) & (col == (row // 16) * 5 + row % 16 - 5), 1.0, 0.0).astype(BF)
    gz.wait()
    gv = gv3[...] + gr3[...]
    sum_a = jnp.concatenate([result(p) for p in (0, 1, 2)], axis=1)
    sum_b = jnp.concatenate([result(p) for p in (3, 4, 5, 6)], axis=1)
    slabs = nn(first, sum_a) + nn(second, sum_b)
    row = lax.broadcasted_iota(jnp.int32, (128, W), 0) % 16
    slabs = jnp.where(row == 10, gv[:, :W], jnp.where(row == 11, gv[:, W:], slabs))
    p3[...] = slabs.astype(BF).reshape(8, 16, W)
    place = z // 2 * 2 + core

    def z_copy(d):
        to = (place + d) % 8
        return remote(p3.at[to], r3.at[place], r3_ss.at[0], r3_rs.at[0],
                      (x_lo * 16 + to // 2 * 4 + z % 2 * 2 + to % 2, j))

    @pl.loop(1, 8)
    def _(d):
        z_copy(d).start()

    r3[place] = p3[place]

    arrived(dq_r.at[0:7], dq_ss.at[0], dq_rs.at[0])

    total = None
    for t in range(3):
        grad = join_pair(dq_r[0:4, t].reshape(128, 384).astype(F32), dq_r[4:8, t].reshape(128, 384).astype(F32)).astype(BF)
        term = nn(grad, spt[t])
        total = term if total is None else total + term
    u1, r1 = unit(act[...].astype(F32))
    ig[...] = (gh[...].astype(F32) + unit_back(total, u1, r1, spg[...].reshape(1, C))).astype(BF)
    ig_store = pltpu.make_async_copy(ig, ig_h, st.at[1])
    ig_store.start()

    arrived(r3.at[0:7], r3_ss.at[0], r3_rs.at[0])

    factor = 1.0 / math.sqrt(128 * 256)
    sums = []
    for c in range(2):
        total = r3[c].astype(F32)
        for n in range(1, 4):
            total = total + r3[2 * n + c].astype(F32)
        sums.append(total * factor)
    wg[0:5, 0] = sums[0][5:10]
    wg[0:5, 1] = sums[1][5:10]
    wg[0:5, 2] = sums[1][0:5]
    wg[0:5, 3] = sums[0][0:5]
    wg[5, 0:2] = (sums[0] + sums[1])[10:12]
    wg_store = pltpu.make_async_copy(wg, wg_h, st.at[2])
    wg_store.start()
    wg_store.wait()
    bo_store.wait()
    ig_store.wait()


def finish(bo_h, ig_h, wg_h, bo, ig, wg, gg, bo_v, ig_v, wg_v, sems):
    rows = [pl.ds(32 * n, 32) for n in range(4)]
    moves = [(wg_h, wg_v, wg_v.at[0:5], wg)]
    for r in rows:
        moves += [(bo_h.at[r], bo_v.at[r], bo_v.at[r], bo.at[r]), (ig_h.at[r], ig_v.at[r], ig_v.at[r], ig.at[r])]
    come = [pltpu.make_async_copy(a, b, sems.at[0, n]) for n, (a, b, _, _) in enumerate(moves)]
    go = [pltpu.make_async_copy(c, d, sems.at[1, n]) for n, (_, _, c, d) in enumerate(moves)]
    for c in come:
        c.start()
    for a, b in zip(come, go):
        a.wait()
        b.start()
    device = lax.axis_index("frame") * 8 + lax.axis_index("quad")
    gain = jnp.concatenate([wg_v[5, 0:1, :], wg_v[5, 1:2, :]], axis=1)
    gg[...] = pltpu.roll(gain, C - device * 5, 1)[0, :5]
    for c in go:
        c.wait()


def positional(frames, channels):
    freq = np.exp(np.arange(channels // 2, dtype=np.float32)[None, :] * np.float32(-2.0 * math.log(10000.0) / channels))
    phases = np.arange(frames, dtype=np.float32)[:, None] * freq.astype(np.float32)
    both = np.stack([np.sin(phases.astype(np.float64)), np.cos(phases.astype(np.float64))], axis=-1)
    return both.reshape(frames, channels).astype(np.float32)


def permutation():
    matrix = np.zeros((C, C), np.float32)
    for m in range(C):
        rest, r = divmod(m, 5)
        rest, core = divmod(rest, 2)
        rest, z_high = divmod(rest, 4)
        xb, xa, yb, ya, z_low = (rest // 16) % 2, (rest // 8) % 2, (rest // 4) % 2, (rest // 2) % 2, rest % 2
        y = yb * 2 + (yb + ya) % 2
        n = (xb + xa) % 2 * 640 + (z_high * 2 + z_low) * 80 + core * 40 + xb * 20 + y * 5 + r
        matrix[n, m] = 1.0
    return matrix


def part_buffers():
    shapes = []
    for _, _, lanes, _ in PARTS:
        shapes += [pltpu.VMEM((2, 2, 2, 2, 40, lanes), BF)] * 2 + [pltpu.VMEM((2, 2, 2, 40, lanes), BF)] * 2
        shapes += [pltpu.VMEM((7, 40, lanes), BF), pltpu.VMEM((8, 128), BF)]
    return shapes


def local(activations, cotangent, spatial_weights, spatial_gain, motion_weights, motion_gain):
    pe = jnp.asarray(positional(128, C))
    perm = jnp.asarray(permutation(), dtype=BF)
    V, D = pltpu.VMEM, pltpu.SemaphoreType.DMA
    any_, vmem = pl.BlockSpec(memory_space=pl.ANY), pl.BlockSpec(memory_space=pltpu.VMEM)
    scratch = [
        V((128, C), BF), V((128, C), BF), V((4, C, W), BF), V((4, W, C), BF), V((4, 8, 160, W), BF), V((128, C), F32), V((C, C), BF),
        V((128, C), BF), V((128, C), BF), V((6, 4, W), F32),
        V((8, 3, 32, 384), BF), V((8, 3, 32, 384), BF), V((8, 32, 384), BF), V((8, 32, 384), BF), V((2, 256, 256), F32),
        V((128, C), BF), V((32, 4, C), BF), V((32, 4, C), BF), V((32, 4, C), BF), V((32, 4, C), BF), V((128, C), BF),
        V((128, C), F32), V((128, C), BF), V((128, C), F32), V((128, 128), F32), V((3, 128, W), BF), V((4, 128, 128), F32),
        V((32, 4, W), BF), V((32, 4, W), BF), V((32, 4, C), BF), V((32, 4, C), BF), V((128, C), BF), V((128, W), F32),
        V((8, 32, 384), BF), V((8, 32, 384), BF), V((8, 3, 32, 384), BF), V((8, 3, 32, 384), BF),
        V((2, 128, C), BF), V((2, 128, W), BF), V((2, 256, C), BF), V((2, 256, W), BF),
        V((2, 2, 2, 2, 2, 40, W), BF), V((2, 2, 2, 2, 2, 40, W), BF), V((8, 16, W), BF), V((8, 16, W), BF),
        V((1, C), F32), V((3, 1, C), F32), V((1, C), F32), V((3, 1, C), F32), V((1, C), F32), V((1, C), F32),
        D((10,)), D((3,))] + [D((4,))] * 14 + [D((1,))] * 16 + [
        D((4,)), D((4,)), D((21,)), D((21,)), D((1,)), D((1,)),
        D((3,)), D((3,)),
    ] + part_buffers()
    tokens = jax.ShapeDtypeStruct((128, C), BF)
    block_output, input_grad, sums = pl.pallas_call(
        kernel,
        out_shape=(tokens, tokens, jax.ShapeDtypeStruct((6, 4, W), F32)),
        in_specs=[any_, any_, any_, vmem, any_, vmem, any_, any_],
        out_specs=(any_, any_, any_),
        scratch_shapes=scratch,
        compiler_params=pltpu.CompilerParams(
            has_side_effects=True, collective_id=0, vmem_limit_bytes=60 * 2 ** 20),
    )(
        activations.reshape(128, C), cotangent.reshape(128, C), spatial_weights, spatial_gain,
        motion_weights, motion_gain, pe, perm,
    )
    block_output, input_grad, weight_grad, gain_grad = pl.pallas_call(
        finish,
        out_shape=(tokens, tokens, jax.ShapeDtypeStruct((5, 4, W), F32), jax.ShapeDtypeStruct((5,), F32)),
        in_specs=[any_, any_, any_],
        out_specs=(any_, any_, any_, vmem),
        scratch_shapes=[V((128, C), BF), V((128, C), BF), V((6, 4, W), F32), D((2, 9))],
        compiler_params=pltpu.CompilerParams(vmem_limit_bytes=60 * 2 ** 20),
    )(block_output, input_grad, sums)
    shape = activations.shape
    return block_output.reshape(shape), input_grad.reshape(shape), weight_grad.transpose(1, 0, 2), gain_grad


def solution(mesh):
    in_specs = (
        P("frame", "quad", None),
        P("frame", "quad", None),
        P(),
        P(),
        P(None, "quad", None),
        P(),
    )
    out_specs = (
        P("frame", "quad", None),
        P("frame", "quad", None),
        P(None, ("frame", "quad"), None),
        P(("frame", "quad")),
    )
    return jax.shard_map(local, mesh=mesh, in_specs=in_specs, out_specs=out_specs, check_vma=False)
```

```python
import math

import jax
import jax.numpy as jnp
import numpy as np
from jax import lax
from jax.experimental import pallas as pl
from jax.experimental.pallas import tpu as pltpu
from jax.sharding import PartitionSpec as P

HEADS = 4
HEAD_DIM = 160
EPSILON = 1e-05
SCALE = HEAD_DIM ** (-0.5)
C = 1280
W = 640
F32 = jnp.float32
BF = jnp.bfloat16
XA, XB, YA, YB, ZA, ZB = range(6)
DIGIT = {XB: 0, XA: 1, YB: 2, YA: 3, ZA: 4, ZB: 4}
PARTS = (
    (0, 0, 256, (XB, ZA)),
    (0, 256, 256, (YA, ZB)),
    (0, 512, 128, (YB, ZA)),
    (1, 0, 128, (XA, YA)),
    (1, 128, 256, (YB, XB)),
    (1, 384, 128, (XB, YB)),
    (1, 512, 128, (YA, XA)),
)
MESH = pl.DeviceIdType.MESH


def nn(a, b):
    return jnp.dot(a, b, preferred_element_type=F32)


def nt(a, b):
    return lax.dot_general(a, b, (((1,), (1,)), ((), ())), preferred_element_type=F32)


def tn(a, b):
    return lax.dot_general(a, b, (((0,), (0,)), ((), ())), preferred_element_type=F32)


def unit(x):
    xc = x - jnp.mean(x, axis=-1, keepdims=True)
    r = lax.rsqrt(jnp.mean(xc * xc, axis=-1, keepdims=True) + EPSILON)
    return xc * r, r


def unit_back(grad, u, r, gain):
    g = grad * gain
    return r * (g - jnp.mean(g, axis=-1, keepdims=True) - u * jnp.mean(g * u, axis=-1, keepdims=True))


def head_of(x, h):
    lane = lax.broadcasted_iota(jnp.int32, x.shape, 1)
    return jnp.where((lane >= h * HEAD_DIM) & (lane < (h + 1) * HEAD_DIM), x, jnp.zeros_like(x))


def split_pair(y):
    return y[:, :384], pltpu.roll(y, 320, 1)[:, :384]


def join_pair(a, b):
    pad = jnp.zeros((a.shape[0], 256), F32)
    left = jnp.concatenate([a, pad], axis=1)
    right = pltpu.roll(jnp.concatenate([b, pad], axis=1), 320, 1)
    lane = lax.broadcasted_iota(jnp.int32, left.shape, 1)
    return jnp.where(lane < 320, left, right)


def row_order():
    row = lax.broadcasted_iota(jnp.int32, (128, 128), 0)
    col = lax.broadcasted_iota(jnp.int32, (128, 128), 1)
    return jnp.where(col == (row % 4) * 32 + row // 4, 1.0, 0.0).astype(BF)


def scatter_rows(to, rows):
    for n in range(32):
        to[n] = rows[4 * n:4 * n + 4, :].astype(BF)


def gather_rows(rows, come):
    for n in range(32):
        rows[4 * n:4 * n + 4, :] = come[n].astype(F32)


def softmax(q, k):
    s = nt(q, k) * SCALE
    e = jnp.exp(s - jnp.max(s, axis=-1, keepdims=True))
    return e / jnp.sum(e, axis=-1, keepdims=True)


def attend_back(q, k, v, g, probs, heads):
    dq = dk = dv = None
    for h in range(heads):
        r = probs[h]
        dr = nt(head_of(g, h), v)
        delta = jnp.sum(r * dr, axis=-1, keepdims=True)
        ds = (r * (dr - delta) * SCALE).astype(BF)
        a, b, c = nn(ds, head_of(k, h)), tn(ds, head_of(q, h)), tn(r.astype(BF), head_of(g, h))
        dq, dk, dv = (a, b, c) if dq is None else (dq + a, dk + b, dv + c)
    return dq, dk, dv


def kernel(act_h, cot_h, spw_h, spg, mw_h, mgn, pe_h, perm_h,
           bo_h, ig_h, wg_h,
           act, cot, spw, spt, mw, pe, perm, bo, ig, wg,
           qkv_s, qkv_r, o_s, o_r, prob_s,
           hid, hid_s, hid_r, ct_s, ct_r, ctt, tx, n2s, u2s, r2s, mqkv, prob_t,
           mo_s, mo_r, lb_s, lb_r, gh, mof,
           gs_s, gs_r, dq_s, dq_r,
           fx, fy, ax, ay, wa, wb, p3, r3,
           gv1, gr1, gv2, gr2, gv3, gr3,
           ld, st, w1_ss, w1_rs, w2_ss, w2_rs, w3_ss, w3_rs, w4_ss, w4_rs, wz_ss, wz_rs, wx_ss, wx_rs, wy_ss, wy_rs,
           q_ss, q_rs, o_ss, o_rs, h_ss, h_rs, c_ss, c_rs,
           m_ss, m_rs, l_ss, l_rs, gs_ss, gs_rs, dq_ss, dq_rs, x_ss, x_rs,
           p_ss, p_rs, r3_ss, r3_rs,
           v_ss, v_rs, *buffers):
    i, j = lax.axis_index("frame"), lax.axis_index("quad")
    core, z, x_lo = i % 2, (i // 2) % 8, i // 16
    y, x_hi = j % 4, j // 4
    x = x_hi * 2 + x_lo
    zc = i % 16
    sib = (i + 1 - 2 * core, j)
    cross = ((1 - x_lo) * 16 + zc, (1 - x_hi) * 4 + y)
    beside = ((1 - x_lo) * 16 + zc, j)
    even = z % 2
    above = (x_lo * 16 + (zc + 2) % 16, j)
    below = (x_lo * 16 + (zc + 14) % 16, j)

    def fpeer(d):
        return (i + d) % 32

    def qpeer(d):
        return (j + d) % 8

    def xpeer(d):
        xx = (x + d) % 4
        return ((xx % 2) * 16 + zc, (xx // 2) * 4 + y)

    def ypeer(d):
        return (i, x_hi * 4 + (y + d) % 4)

    def remote(src, dst, ss, rs, dev):
        return pltpu.make_async_remote_copy(
            src_ref=src, dst_ref=dst, send_sem=ss, recv_sem=rs, device_id=dev, device_id_type=MESH)

    def arrived(part, ss, rs):
        pltpu.make_async_copy(part, part, ss).wait()
        pltpu.make_async_copy(part, part, rs).wait()

    half = pl.ds(pl.multiple_of(core * 80, 16), 80)
    loads = [
        pltpu.make_async_copy(act_h, act, ld.at[0]),
        pltpu.make_async_copy(spw_h.at[0], spw.at[0], ld.at[1]),
        pltpu.make_async_copy(spw_h.at[1], spw.at[1], ld.at[2]),
        pltpu.make_async_copy(spw_h.at[2], spw.at[2], ld.at[3]),
        pltpu.make_async_copy(cot_h, cot, ld.at[5]),
        pltpu.make_async_copy(mw_h.at[even, half], mw.at[even, j, half], ld.at[6]),
        pltpu.make_async_copy(mw_h.at[2:4, half], mw.at[2:4, j, half], ld.at[9]),
        pltpu.make_async_copy(spw_h.at[3], spw.at[3], ld.at[4]),
        pltpu.make_async_copy(pe_h, pe, ld.at[7]),
        pltpu.make_async_copy(perm_h, perm, ld.at[8]),
    ]
    for c in loads:
        c.start()

    bar = pltpu.get_barrier_semaphore()

    @pl.loop(1, 32)
    def _(d):
        pl.semaphore_signal(bar, inc=1, device_id=(fpeer(d), j), device_id_type=MESH)

    @pl.loop(1, 8)
    def _(d):
        pl.semaphore_signal(bar, inc=1, device_id=(i, qpeer(d)), device_id_type=MESH)

    @pl.loop(1, 8)
    def _(d):
        pl.semaphore_signal(bar, inc=1, device_id=((1 - x_lo) * 16 + zc, qpeer(d)), device_id_type=MESH)
        for n in range(2):
            near = n * 16 + z // 2 * 4 + (1 - even) * 2 + core
            pl.semaphore_signal(bar, inc=1, device_id=(near, qpeer(d)), device_id_type=MESH)

    loads[0].wait()
    u1, _ = unit(act[...].astype(F32))
    n1 = (u1 * spg[...].reshape(1, C)).astype(BF)
    for t in range(3):
        loads[1 + t].wait()
        for hp, part in enumerate(split_pair(nn(n1, spw[t]))):
            qkv_s[hp * 4:hp * 4 + 4, t] = part.astype(BF).reshape(4, 32, 384)
    pl.semaphore_wait(bar, 59)

    def q_copy(d):
        return remote(qkv_s.at[qpeer(d)], qkv_r.at[j], q_ss.at[0], q_rs.at[0], (i, qpeer(d)))

    @pl.loop(1, 8)
    def _(d):
        q_copy(d).start()

    matrix = (even, 1 - even, 2, 3)

    def w1_copy(n, d):
        m = matrix[n]
        return remote(mw_h.at[m, half], mw.at[m, j, half], w1_ss.at[n], w1_rs.at[n], ypeer(d))

    def w2_copy(n):
        part = mw.at[matrix[n], pl.ds(x_hi * 4 + 2 * (1 - x_lo), 2), half]
        return remote(part, part, w2_ss.at[n // 2], w2_rs.at[n // 2], cross)

    def w3_copy(n):
        part = mw.at[matrix[n], pl.ds((1 - x_hi) * 4 + 2 * x_lo, 2), half]
        return remote(part, part, w3_ss.at[n // 2], w3_rs.at[n // 2], beside)

    def w4_copy(n):
        part = mw.at[matrix[n], :, half]
        return remote(part, part, w4_ss.at[n], w4_rs.at[n], sib)

    up, down = mw.at[even, pl.ds(x_hi * 4, 2), half], mw.at[even, pl.ds(x_hi * 4 + 2, 2), half]
    wz = [remote(up, up, wz_ss.at[0], wz_rs.at[0], above),
          remote(down, down, wz_ss.at[1], wz_rs.at[1], below)]

    def wx_copy(n):
        m = matrix[n]
        return remote(mw_h.at[m, half], mw.at[m, j, half], wx_ss.at[n // 2], wx_rs.at[n // 2], cross)

    def wy_copy(n, d):
        part = mw.at[matrix[n], (1 - x_hi) * 4 + y, half]
        return remote(part, part, wy_ss.at[n // 2], wy_rs.at[n // 2], ypeer(d))

    def w1_start(n):
        for d in (1, 3, 2):
            w1_copy(n, d).start()

    def w1_wait(n):
        arrived(mw.at[matrix[n], 0:3, half], w1_ss.at[n], w1_rs.at[n])

    def wy_start(n):
        wx_copy(n).wait()
        for d in (1, 3, 2):
            wy_copy(n, d).start()

    def wy_pass(n):
        arrived(mw.at[matrix[n], 0:3, half], wy_ss.at[n // 2], wy_rs.at[n // 2])
        w4_copy(n).start()

    def w2_pass(n):
        w2_copy(n).wait()
        w3_copy(n).start()

    def w3_pass(n):
        w3_copy(n).wait()
        w4_copy(n).start()

    wx_copy(1).start()
    wx_copy(3).start()
    w1_start(0)

    loads[4].wait()
    scatter_rows(ct_s, nn(row_order(), cot[...]))

    def c_copy(d):
        return remote(ct_s.at[fpeer(d)], ct_r.at[i], c_ss.at[0], c_rs.at[0], (fpeer(d), j))

    @pl.loop(1, 32)
    def _(d):
        c_copy(d).start()

    ct_r[i] = ct_s[i]
    loads[5].wait()
    loads[6].wait()
    qkv_r[j] = qkv_s[j]

    loads[7].wait()
    for t in range(4):
        spt[t] = spw[t].T

    arrived(qkv_r.at[0:7], q_ss.at[0], q_rs.at[0])

    q, k, v = (qkv_r[:, t].reshape(256, 384) for t in range(3))
    out = None
    for h in range(2):
        probs = softmax(head_of(q, h), k)
        prob_s[h] = probs
        term = nn(probs.astype(BF), head_of(v, h))
        out = term if out is None else out + term
    o_s[...] = out.astype(BF).reshape(8, 32, 384)

    def o_copy(d):
        return remote(o_s.at[qpeer(d)], o_r.at[j], o_ss.at[0], o_rs.at[0], (i, qpeer(d)))

    @pl.loop(1, 8)
    def _(d):
        o_copy(d).start()

    o_r[j] = o_s[j]
    w1_start(2)
    w1_wait(0)
    w2_copy(0).start()
    for c in wz:
        c.start()
    wy_start(1)
    w2_pass(0)

    arrived(o_r.at[0:7], o_ss.at[0], o_rs.at[0])

    w1_start(3)
    wy_start(3)
    so = join_pair(o_r[0:4].reshape(128, 384).astype(F32), o_r[4:8].reshape(128, 384).astype(F32)).astype(BF)
    hid[...] = (act[...].astype(F32) + nn(so, spt[3])).astype(BF)
    scatter_rows(hid_s, nn(row_order(), hid[...]))

    def h_copy(d):
        return remote(hid_s.at[fpeer(d)], hid_r.at[i], h_ss.at[0], h_rs.at[0], (fpeer(d), j))

    @pl.loop(1, 32)
    def _(d):
        h_copy(d).start()

    hid_r[i] = hid_s[i]
    w1_wait(2)
    w2_copy(2).start()

    arrived(ct_r.at[0:31], c_ss.at[0], c_rs.at[0])

    gather_rows(tx, ct_r)
    ctt[...] = tx[...].astype(BF)
    loads[9].wait()
    ctp = nn(ctt[...], perm[...]).astype(BF)

    @pl.when(core == 0)
    def _():
        ax[0, 0:128] = ctp

    @pl.when(core == 1)
    def _():
        fx[0] = ctp

    for c in wz:
        c.wait()
    w3_pass(0)
    wy_pass(1)
    w2_pass(2)

    def weight(n):
        return mw[n].reshape(C, W)

    arrived(hid_r.at[0:31], h_ss.at[0], h_rs.at[0])

    gather_rows(tx, hid_r)
    loads[8].wait()
    gain = mgn[...].reshape(1, C)
    u2, r2 = unit(tx[...])
    u2s[...] = u2
    r2s[...] = jnp.broadcast_to(r2, r2s.shape)
    n2s[...] = (u2 * gain + pe[...]).astype(BF)
    n2p = nn(n2s[...], perm[...]).astype(BF)
    ax[1, 0:128] = n2p
    fx[1] = n2p
    w3_pass(2)
    w4_copy(0).wait()
    w4_copy(1).wait()
    for t in range(2):
        mqkv[t] = nn(n2s[...], weight(t)).astype(BF)
    w1_wait(3)
    wy_pass(3)
    for h in range(HEADS):
        prob_t[h] = softmax(head_of(mqkv[0], h), mqkv[1])
    w4_copy(2).wait()
    mqkv[2] = nn(n2s[...], weight(2)).astype(BF)
    out = None
    for h in range(HEADS):
        term = nn(prob_t[h].astype(BF), head_of(mqkv[2], h))
        out = term if out is None else out + term
    mo_t = out.astype(BF)
    w4_copy(3).wait()
    mg = nn(ctt[...], weight(3)).astype(BF)
    dv = None
    for h in range(HEADS):
        term = tn(prob_t[h].astype(BF), head_of(mg, h))
        dv = term if dv is None else dv + term
    dv = dv.astype(BF)

    @pl.when(core == 0)
    def _():
        ay[0, 0:128] = mo_t
        fx[0] = n2p
        fy[0] = dv

    @pl.when(core == 1)
    def _():
        ax[0, 0:128] = n2p
        ay[0, 0:128] = dv
        fy[0] = mo_t

    swap = [remote(fx.at[0], ax.at[0, 128:256], x_ss.at[0], x_rs.at[0], sib),
            remote(fy.at[0], ay.at[0, 128:256], x_ss.at[1], x_rs.at[1], sib),
            remote(fx.at[1], ax.at[1, 128:256], x_ss.at[2], x_rs.at[2], sib)]
    for c in swap:
        c.start()

    scatter_rows(mo_s, mo_t.astype(F32))

    def m_copy(d):
        return remote(mo_s.at[fpeer(d)], mo_r.at[i], m_ss.at[0], m_rs.at[0], (fpeer(d), j))

    @pl.loop(1, 32)
    def _(d):
        m_copy(d).start()

    mo_r[i] = mo_s[i]

    dq = dk = None
    for h in range(HEADS):
        r = prob_t[h]
        dr = nt(head_of(mg, h), mqkv[2])
        delta = jnp.sum(r * dr, axis=-1, keepdims=True)
        ds = (r * (dr - delta) * SCALE).astype(BF)
        a, b = nn(ds, head_of(mqkv[1], h)), tn(ds, head_of(mqkv[0], h))
        dq, dk = (a, b) if dq is None else (dq + a, dk + b)
    dq, dk = dq.astype(BF), dk.astype(BF)

    @pl.when(core == 0)
    def _():
        ay[1, 0:128] = dq
        fy[1] = dk

    @pl.when(core == 1)
    def _():
        ay[1, 0:128] = dk
        fy[1] = dq

    swap_b = remote(fy.at[1], ay.at[1, 128:256], x_ss.at[3], x_rs.at[3], sib)
    swap_b.start()
    for c in swap:
        c.wait()
    wa[...] = tn(ax[0], ay[0]).reshape(2, 2, 2, 2, 2, 40, W).astype(BF)

    own = (x_hi, (x_hi + x_lo) % 2, y // 2, (y // 2 + y) % 2, z % 2)

    def zpeer(zz):
        return (x_lo * 16 + (zz + 8) % 8 * 2 + core, j)

    partner = {
        XA: beside, XB: cross,
        YA: (i, x_hi * 4 + y + 1 - 2 * (y % 2)), YB: (i, x_hi * 4 + 3 - y),
        ZA: zpeer(z + 1 - 2 * (z % 2)), ZB: zpeer(z - 1 + 2 * (z % 2)),
    }

    def left(p, step):
        return [n for n in range(5) if n not in [DIGIT[link] for link in PARTS[p][3][:step]]]

    def block(p, step, digits):
        which, lane, lanes, _ = PARTS[p]
        ref, columns = ((wa, wb)[which], slice(lane, lane + lanes)) if step == 0 else (buffers[6 * p + 2 * step - 1], slice(None))
        return ref, tuple(digits.get(n, slice(None)) for n in left(p, step)) + (slice(None), columns)

    def step_copy(p, step):
        link = PARTS[p][3][step]
        ref, at = block(p, step, {DIGIT[link]: 1 - own[DIGIT[link]]})
        return remote(ref.at[at], buffers[6 * p + 2 * step], p_ss.at[3 * p + step], p_rs.at[3 * p + step], partner[link])

    def direct(p):
        digits = left(p, 2)
        for mask in range(1, 8):
            to = list(own)
            for bit, n in enumerate(digits):
                if mask >> bit & 1:
                    to[n] = 1 - own[n]
            ref, at = block(p, 2, {n: to[n] for n in digits})
            device = ((to[0] + to[1]) % 2 * 16 + z // 2 * 4 + to[4] * 2 + core, to[0] * 4 + to[2] * 2 + (to[2] + to[3]) % 2)
            remote(ref.at[at], buffers[6 * p + 4].at[mask - 1], p_ss.at[3 * p + 2], p_rs.at[3 * p + 2], device).start()

    done = [0] * 7

    def begin(p):
        step_copy(p, 0).start()

    def advance(p):
        step = done[p]
        step_copy(p, step).wait()
        link = PARTS[p][3][step]
        ref, at = block(p, step, {DIGIT[link]: own[DIGIT[link]]})
        buffers[6 * p + 2 * step + 1][...] = (
            ref[at].astype(F32) + buffers[6 * p + 2 * step][...].astype(F32)).astype(BF)
        done[p] = step + 1
        if step == 0:
            step_copy(p, 1).start()
        else:
            direct(p)

    def result(p):
        come = buffers[6 * p + 4]
        arrived(come, p_ss.at[3 * p + 2], p_rs.at[3 * p + 2])
        ref, at = block(p, 2, {n: own[n] for n in left(p, 2)})
        total = ref[at].astype(F32)
        for n in range(7):
            total = total + come[n].astype(F32)
        return total.astype(BF)

    for p in (0, 1, 2):
        begin(p)
    dn2 = nt(dq, weight(0)) + nt(dk, weight(1)) + nt(dv, weight(2))
    u2 = u2s[...]
    gv1[...] = jnp.sum(dn2 * u2, axis=0, keepdims=True)
    back = ctt[...].astype(F32) + unit_back(dn2, u2, r2s[:, 0:1], gain)
    scatter_rows(lb_s, back)

    def l_copy(d):
        return remote(lb_s.at[fpeer(d)], lb_r.at[i], l_ss.at[0], l_rs.at[0], (fpeer(d), j))

    @pl.loop(1, 32)
    def _(d):
        l_copy(d).start()

    lb_r[i] = lb_s[i]

    def v_copy(src, dst, n, dev):
        return remote(src, dst, v_ss.at[n], v_rs.at[n], dev)

    gx = [v_copy(gv1, gr1.at[d - 1], 0, xpeer(d)) for d in range(1, 4)]
    for c in gx:
        c.start()

    swap_b.wait()
    wb[...] = tn(ax[1], ay[1]).reshape(2, 2, 2, 2, 2, 40, W).astype(BF)

    for p in (3, 4, 5, 6):
        begin(p)

    arrived(mo_r.at[0:31], m_ss.at[0], m_rs.at[0])

    gather_rows(mof, mo_r)
    mo = tn(row_order(), mof[...].astype(BF)).astype(BF)
    bo[...] = (hid[...].astype(F32) + nt(mo, weight(3))).astype(BF)
    bo_store = pltpu.make_async_copy(bo, bo_h, st.at[0])
    bo_store.start()

    advance(2)
    advance(0)
    advance(1)

    arrived(lb_r.at[0:31], l_ss.at[0], l_rs.at[0])

    gather_rows(tx, lb_r)
    gh[...] = tn(row_order(), tx[...].astype(BF)).astype(BF)
    for hp, part in enumerate(split_pair(nn(gh[...], spw[3]))):
        gs_s[hp * 4:hp * 4 + 4] = part.astype(BF).reshape(4, 32, 384)

    def gs_copy(d):
        return remote(gs_s.at[qpeer(d)], gs_r.at[j], gs_ss.at[0], gs_rs.at[0], (i, qpeer(d)))

    @pl.loop(1, 8)
    def _(d):
        gs_copy(d).start()

    gs_r[j] = gs_s[j]

    arrived(gr1, v_ss.at[0], v_rs.at[0])
    gv2[...] = gv1[...] + gr1[0] + gr1[1] + gr1[2]
    gy = [v_copy(gv2, gr2.at[d - 1], 1, ypeer(d)) for d in range(1, 4)]
    for c in gy:
        c.start()
    advance(5)
    advance(6)
    advance(4)
    advance(3)
    advance(2)
    advance(0)
    advance(1)
    arrived(gs_r.at[0:7], gs_ss.at[0], gs_rs.at[0])

    q, k, v = (qkv_r[:, t].reshape(256, 384) for t in range(3))
    for t, grad in enumerate(attend_back(q, k, v, gs_r[...].reshape(256, 384), prob_s, 2)):
        dq_s[:, t] = grad.astype(BF).reshape(8, 32, 384)

    advance(5)
    advance(6)
    advance(3)
    advance(4)

    def dq_copy(d):
        return remote(dq_s.at[qpeer(d)], dq_r.at[j], dq_ss.at[0], dq_rs.at[0], (i, qpeer(d)))

    @pl.loop(1, 8)
    def _(d):
        dq_copy(d).start()

    dq_r[j] = dq_s[j]

    arrived(gr2, v_ss.at[1], v_rs.at[1])
    gv3[...] = gv2[...] + gr2[0] + gr2[1] + gr2[2]
    gz = v_copy(gv3, gr3, 2, partner[ZA])
    gz.start()

    row = lax.broadcasted_iota(jnp.int32, (128, 40), 0)
    col = lax.broadcasted_iota(jnp.int32, (128, 40), 1)
    first = jnp.where((row % 16 < 5) & (col == (row // 16) * 5 + row % 16), 1.0, 0.0).astype(BF)
    second = jnp.where((row % 16 >= 5) & (row % 16 < 10) & (col == (row // 16) * 5 + row % 16 - 5), 1.0, 0.0).astype(BF)
    gz.wait()
    gv = gv3[...] + gr3[...]
    sum_a = jnp.concatenate([result(p) for p in (0, 1, 2)], axis=1)
    sum_b = jnp.concatenate([result(p) for p in (3, 4, 5, 6)], axis=1)
    slabs = nn(first, sum_a) + nn(second, sum_b)
    row = lax.broadcasted_iota(jnp.int32, (128, W), 0) % 16
    slabs = jnp.where(row == 10, gv[:, :W], jnp.where(row == 11, gv[:, W:], slabs))
    p3[...] = slabs.astype(BF).reshape(8, 16, W)
    place = z // 2 * 2 + core

    def z_copy(d):
        to = (place + d) % 8
        return remote(p3.at[to], r3.at[place], r3_ss.at[0], r3_rs.at[0],
                      (x_lo * 16 + to // 2 * 4 + z % 2 * 2 + to % 2, j))

    @pl.loop(1, 8)
    def _(d):
        z_copy(d).start()

    r3[place] = p3[place]

    arrived(dq_r.at[0:7], dq_ss.at[0], dq_rs.at[0])

    total = None
    for t in range(3):
        grad = join_pair(dq_r[0:4, t].reshape(128, 384).astype(F32), dq_r[4:8, t].reshape(128, 384).astype(F32)).astype(BF)
        term = nn(grad, spt[t])
        total = term if total is None else total + term
    u1, r1 = unit(act[...].astype(F32))
    ig[...] = (gh[...].astype(F32) + unit_back(total, u1, r1, spg[...].reshape(1, C))).astype(BF)
    ig_store = pltpu.make_async_copy(ig, ig_h, st.at[1])
    ig_store.start()

    arrived(r3.at[0:7], r3_ss.at[0], r3_rs.at[0])

    factor = 1.0 / math.sqrt(128 * 256)
    sums = []
    for c in range(2):
        total = r3[c].astype(F32)
        for n in range(1, 4):
            total = total + r3[2 * n + c].astype(F32)
        sums.append(total * factor)
    wg[0:5, 0] = sums[0][5:10]
    wg[0:5, 1] = sums[1][5:10]
    wg[0:5, 2] = sums[1][0:5]
    wg[0:5, 3] = sums[0][0:5]
    wg[5, 0:2] = (sums[0] + sums[1])[10:12]
    wg_store = pltpu.make_async_copy(wg, wg_h, st.at[2])
    wg_store.start()
    wg_store.wait()
    bo_store.wait()
    ig_store.wait()


def finish(bo_h, ig_h, wg_h, bo, ig, wg, gg, bo_v, ig_v, wg_v, sems):
    rows = [pl.ds(32 * n, 32) for n in range(4)]
    moves = [(wg_h, wg_v, wg_v.at[0:5], wg)]
    for r in rows:
        moves += [(bo_h.at[r], bo_v.at[r], bo_v.at[r], bo.at[r]), (ig_h.at[r], ig_v.at[r], ig_v.at[r], ig.at[r])]
    come = [pltpu.make_async_copy(a, b, sems.at[0, n]) for n, (a, b, _, _) in enumerate(moves)]
    go = [pltpu.make_async_copy(c, d, sems.at[1, n]) for n, (_, _, c, d) in enumerate(moves)]
    for c in come:
        c.start()
    for a, b in zip(come, go):
        a.wait()
        b.start()
    device = lax.axis_index("frame") * 8 + lax.axis_index("quad")
    gain = jnp.concatenate([wg_v[5, 0:1, :], wg_v[5, 1:2, :]], axis=1)
    gg[...] = pltpu.roll(gain, (C - device * 5) % C, 1)[0, :5]
    for c in go:
        c.wait()


def positional(frames, channels):
    freq = np.exp(np.arange(channels // 2, dtype=np.float32)[None, :] * np.float32(-2.0 * math.log(10000.0) / channels))
    phases = np.arange(frames, dtype=np.float32)[:, None] * freq.astype(np.float32)
    both = np.stack([np.sin(phases.astype(np.float64)), np.cos(phases.astype(np.float64))], axis=-1)
    return both.reshape(frames, channels).astype(np.float32)


def permutation():
    matrix = np.zeros((C, C), np.float32)
    for m in range(C):
        rest, r = divmod(m, 5)
        rest, core = divmod(rest, 2)
        rest, z_high = divmod(rest, 4)
        xb, xa, yb, ya, z_low = (rest // 16) % 2, (rest // 8) % 2, (rest // 4) % 2, (rest // 2) % 2, rest % 2
        y = yb * 2 + (yb + ya) % 2
        n = (xb + xa) % 2 * 640 + (z_high * 2 + z_low) * 80 + core * 40 + xb * 20 + y * 5 + r
        matrix[n, m] = 1.0
    return matrix


def part_buffers():
    shapes = []
    for _, _, lanes, _ in PARTS:
        shapes += [pltpu.VMEM((2, 2, 2, 2, 40, lanes), BF)] * 2 + [pltpu.VMEM((2, 2, 2, 40, lanes), BF)] * 2
        shapes += [pltpu.VMEM((7, 40, lanes), BF), pltpu.VMEM((8, 128), BF)]
    return shapes


def local(activations, cotangent, spatial_weights, spatial_gain, motion_weights, motion_gain):
    pe = jnp.asarray(positional(128, C))
    perm = jnp.asarray(permutation(), dtype=BF)
    V, D = pltpu.VMEM, pltpu.SemaphoreType.DMA
    any_, vmem = pl.BlockSpec(memory_space=pl.ANY), pl.BlockSpec(memory_space=pltpu.VMEM)
    scratch = [
        V((128, C), BF), V((128, C), BF), V((4, C, W), BF), V((4, W, C), BF), V((4, 8, 160, W), BF), V((128, C), F32), V((C, C), BF),
        V((128, C), BF), V((128, C), BF), V((6, 4, W), F32),
        V((8, 3, 32, 384), BF), V((8, 3, 32, 384), BF), V((8, 32, 384), BF), V((8, 32, 384), BF), V((2, 256, 256), F32),
        V((128, C), BF), V((32, 4, C), BF), V((32, 4, C), BF), V((32, 4, C), BF), V((32, 4, C), BF), V((128, C), BF),
        V((128, C), F32), V((128, C), BF), V((128, C), F32), V((128, 128), F32), V((3, 128, W), BF), V((4, 128, 128), F32),
        V((32, 4, W), BF), V((32, 4, W), BF), V((32, 4, C), BF), V((32, 4, C), BF), V((128, C), BF), V((128, W), F32),
        V((8, 32, 384), BF), V((8, 32, 384), BF), V((8, 3, 32, 384), BF), V((8, 3, 32, 384), BF),
        V((2, 128, C), BF), V((2, 128, W), BF), V((2, 256, C), BF), V((2, 256, W), BF),
        V((2, 2, 2, 2, 2, 40, W), BF), V((2, 2, 2, 2, 2, 40, W), BF), V((8, 16, W), BF), V((8, 16, W), BF),
        V((1, C), F32), V((3, 1, C), F32), V((1, C), F32), V((3, 1, C), F32), V((1, C), F32), V((1, C), F32),
        D((10,)), D((3,))] + [D((4,))] * 2 + [D((2,))] * 4 + [D((4,))] * 2 + [D((2,))] * 6 + [D((1,))] * 16 + [
        D((4,)), D((4,)), D((21,)), D((21,)), D((1,)), D((1,)),
        D((3,)), D((3,)),
    ] + part_buffers()
    tokens = jax.ShapeDtypeStruct((128, C), BF)
    block_output, input_grad, sums = pl.pallas_call(
        kernel,
        out_shape=(tokens, tokens, jax.ShapeDtypeStruct((6, 4, W), F32)),
        in_specs=[any_, any_, any_, vmem, any_, vmem, any_, any_],
        out_specs=(any_, any_, any_),
        scratch_shapes=scratch,
        compiler_params=pltpu.CompilerParams(
            has_side_effects=True, collective_id=0, vmem_limit_bytes=60 * 2 ** 20),
    )(
        activations.reshape(128, C), cotangent.reshape(128, C), spatial_weights, spatial_gain,
        motion_weights, motion_gain, pe, perm,
    )
    block_output, input_grad, weight_grad, gain_grad = pl.pallas_call(
        finish,
        out_shape=(tokens, tokens, jax.ShapeDtypeStruct((5, 4, W), F32), jax.ShapeDtypeStruct((5,), F32)),
        in_specs=[any_, any_, any_],
        out_specs=(any_, any_, any_, vmem),
        scratch_shapes=[V((128, C), BF), V((128, C), BF), V((6, 4, W), F32), D((2, 9))],
        compiler_params=pltpu.CompilerParams(vmem_limit_bytes=60 * 2 ** 20),
    )(block_output, input_grad, sums)
    shape = activations.shape
    return block_output.reshape(shape), input_grad.reshape(shape), weight_grad.transpose(1, 0, 2), gain_grad


def solution(mesh):
    in_specs = (
        P("frame", "quad", None),
        P("frame", "quad", None),
        P(),
        P(),
        P(None, "quad", None),
        P(),
    )
    out_specs = (
        P("frame", "quad", None),
        P("frame", "quad", None),
        P(None, ("frame", "quad"), None),
        P(("frame", "quad")),
    )
    return jax.shard_map(local, mesh=mesh, in_specs=in_specs, out_specs=out_specs, check_vma=False)
```

```python
import math

import jax
import jax.numpy as jnp
import numpy as np
from jax import lax
from jax.experimental import pallas as pl
from jax.experimental.pallas import tpu as pltpu
from jax.sharding import PartitionSpec as P

HEADS = 4
HEAD_DIM = 160
EPSILON = 1e-05
SCALE = HEAD_DIM ** (-0.5)
C = 1280
W = 640
F32 = jnp.float32
BF = jnp.bfloat16
XA, XB, YA, YB, ZA, ZB = range(6)
DIGIT = {XB: 0, XA: 1, YB: 2, YA: 3, ZA: 4, ZB: 4}
PARTS = (
    (0, 0, 256, (XB, ZA)),
    (0, 256, 256, (YA, ZB)),
    (0, 512, 128, (YB, ZA)),
    (1, 0, 128, (XA, YA)),
    (1, 128, 256, (YB, XB)),
    (1, 384, 128, (XB, YB)),
    (1, 512, 128, (YA, XA)),
)
MESH = pl.DeviceIdType.MESH


def nn(a, b):
    return jnp.dot(a, b, preferred_element_type=F32)


def nt(a, b):
    return lax.dot_general(a, b, (((1,), (1,)), ((), ())), preferred_element_type=F32)


def tn(a, b):
    return lax.dot_general(a, b, (((0,), (0,)), ((), ())), preferred_element_type=F32)


def unit(x):
    xc = x - jnp.mean(x, axis=-1, keepdims=True)
    r = lax.rsqrt(jnp.mean(xc * xc, axis=-1, keepdims=True) + EPSILON)
    return xc * r, r


def unit_back(grad, u, r, gain):
    g = grad * gain
    return r * (g - jnp.mean(g, axis=-1, keepdims=True) - u * jnp.mean(g * u, axis=-1, keepdims=True))


def head_of(x, h):
    lane = lax.broadcasted_iota(jnp.int32, x.shape, 1)
    return jnp.where((lane >= h * HEAD_DIM) & (lane < (h + 1) * HEAD_DIM), x, jnp.zeros_like(x))


def split_pair(y):
    return y[:, :384], pltpu.roll(y, 320, 1)[:, :384]


def join_pair(a, b):
    pad = jnp.zeros((a.shape[0], 256), F32)
    left = jnp.concatenate([a, pad], axis=1)
    right = pltpu.roll(jnp.concatenate([b, pad], axis=1), 320, 1)
    lane = lax.broadcasted_iota(jnp.int32, left.shape, 1)
    return jnp.where(lane < 320, left, right)


def row_order():
    row = lax.broadcasted_iota(jnp.int32, (128, 128), 0)
    col = lax.broadcasted_iota(jnp.int32, (128, 128), 1)
    return jnp.where(col == (row % 4) * 32 + row // 4, 1.0, 0.0).astype(BF)


def scatter_rows(to, rows):
    for n in range(32):
        to[n] = rows[4 * n:4 * n + 4, :].astype(BF)


def gather_rows(rows, come):
    for n in range(32):
        rows[4 * n:4 * n + 4, :] = come[n].astype(F32)


def softmax(q, k):
    s = nt(q, k) * SCALE
    e = jnp.exp(s - jnp.max(s, axis=-1, keepdims=True))
    return e / jnp.sum(e, axis=-1, keepdims=True)


def attend_back(q, k, v, g, probs, heads):
    dq = dk = dv = None
    for h in range(heads):
        r = probs[h]
        dr = nt(head_of(g, h), v)
        delta = jnp.sum(r * dr, axis=-1, keepdims=True)
        ds = (r * (dr - delta) * SCALE).astype(BF)
        a, b, c = nn(ds, head_of(k, h)), tn(ds, head_of(q, h)), tn(r.astype(BF), head_of(g, h))
        dq, dk, dv = (a, b, c) if dq is None else (dq + a, dk + b, dv + c)
    return dq, dk, dv


def kernel(act_h, cot_h, spw_h, spg, mw_h, mgn, pe_h, perm_h,
           bo_h, ig_h, wg_h,
           act, cot, spw, spt, mw, pe, perm, bo, ig, wg,
           qkv_s, qkv_r, o_s, o_r, prob_s,
           hid, hid_s, hid_r, ct_s, ct_r, ctt, tx, n2s, u2s, r2s, mqkv, prob_t,
           mo_s, mo_r, lb_s, lb_r, gh, mof,
           gs_s, gs_r, dq_s, dq_r,
           fx, fy, ax, ay, wa, wb, p3, r3,
           gv1, gr1, gv2, gr2, gv3, gr3,
           ld, st, w1_ss, w1_rs, w2_ss, w2_rs, w3_ss, w3_rs, w4_ss, w4_rs, wz_ss, wz_rs, wx_ss, wx_rs, wy_ss, wy_rs,
           q_ss, q_rs, o_ss, o_rs, h_ss, h_rs, c_ss, c_rs,
           m_ss, m_rs, l_ss, l_rs, gs_ss, gs_rs, dq_ss, dq_rs, x_ss, x_rs,
           p_ss, p_rs, r3_ss, r3_rs,
           v_ss, v_rs, *buffers):
    i, j = lax.axis_index("frame"), lax.axis_index("quad")
    core, z, x_lo = i % 2, (i // 2) % 8, i // 16
    y, x_hi = j % 4, j // 4
    x = x_hi * 2 + x_lo
    zc = i % 16
    sib = (i + 1 - 2 * core, j)
    cross = ((1 - x_lo) * 16 + zc, (1 - x_hi) * 4 + y)
    beside = ((1 - x_lo) * 16 + zc, j)
    even = z % 2
    above = (x_lo * 16 + (zc + 2) % 16, j)
    below = (x_lo * 16 + (zc + 14) % 16, j)

    def fpeer(d):
        return (i + d) % 32

    def qpeer(d):
        return (j + d) % 8

    def xpeer(d):
        xx = (x + d) % 4
        return ((xx % 2) * 16 + zc, (xx // 2) * 4 + y)

    def ypeer(d):
        return (i, x_hi * 4 + (y + d) % 4)

    def remote(src, dst, ss, rs, dev):
        return pltpu.make_async_remote_copy(
            src_ref=src, dst_ref=dst, send_sem=ss, recv_sem=rs, device_id=dev, device_id_type=MESH)

    def arrived(part, ss, rs):
        pltpu.make_async_copy(part, part, ss).wait()
        pltpu.make_async_copy(part, part, rs).wait()

    half = pl.ds(pl.multiple_of(core * 80, 16), 80)
    loads = [
        pltpu.make_async_copy(act_h, act, ld.at[0]),
        pltpu.make_async_copy(spw_h.at[0], spw.at[0], ld.at[1]),
        pltpu.make_async_copy(spw_h.at[1], spw.at[1], ld.at[2]),
        pltpu.make_async_copy(spw_h.at[2], spw.at[2], ld.at[3]),
        pltpu.make_async_copy(cot_h, cot, ld.at[5]),
        pltpu.make_async_copy(mw_h.at[even, half], mw.at[even, j, half], ld.at[6]),
        pltpu.make_async_copy(mw_h.at[2:4, half], mw.at[2:4, j, half], ld.at[9]),
        pltpu.make_async_copy(spw_h.at[3], spw.at[3], ld.at[4]),
        pltpu.make_async_copy(pe_h, pe, ld.at[7]),
        pltpu.make_async_copy(perm_h, perm, ld.at[8]),
    ]
    for c in loads:
        c.start()

    bar = pltpu.get_barrier_semaphore()

    @pl.loop(1, 32)
    def _(d):
        pl.semaphore_signal(bar, inc=1, device_id=(fpeer(d), j), device_id_type=MESH)

    @pl.loop(1, 8)
    def _(d):
        pl.semaphore_signal(bar, inc=1, device_id=(i, qpeer(d)), device_id_type=MESH)

    @pl.loop(1, 8)
    def _(d):
        pl.semaphore_signal(bar, inc=1, device_id=((1 - x_lo) * 16 + zc, qpeer(d)), device_id_type=MESH)
        for n in range(2):
            near = n * 16 + z // 2 * 4 + (1 - even) * 2 + core
            pl.semaphore_signal(bar, inc=1, device_id=(near, qpeer(d)), device_id_type=MESH)

    loads[0].wait()
    u1, _ = unit(act[...].astype(F32))
    n1 = (u1 * spg[...].reshape(1, C)).astype(BF)
    for t in range(3):
        loads[1 + t].wait()
        for hp, part in enumerate(split_pair(nn(n1, spw[t]))):
            qkv_s[hp * 4:hp * 4 + 4, t] = part.astype(BF).reshape(4, 32, 384)
    pl.semaphore_wait(bar, 59)

    def q_copy(d):
        return remote(qkv_s.at[qpeer(d)], qkv_r.at[j], q_ss.at[0], q_rs.at[0], (i, qpeer(d)))

    @pl.loop(1, 8)
    def _(d):
        q_copy(d).start()

    matrix = (even, 1 - even, 2, 3)

    def w1_copy(n, d):
        m = matrix[n]
        return remote(mw_h.at[m, half], mw.at[m, j, half], w1_ss.at[n], w1_rs.at[n], ypeer(d))

    def w2_copy(n):
        part = mw.at[matrix[n], pl.ds(x_hi * 4 + 2 * (1 - x_lo), 2), half]
        return remote(part, part, w2_ss.at[n // 2], w2_rs.at[n // 2], cross)

    def w3_copy(n):
        part = mw.at[matrix[n], pl.ds((1 - x_hi) * 4 + 2 * x_lo, 2), half]
        return remote(part, part, w3_ss.at[n // 2], w3_rs.at[n // 2], beside)

    def w4_copy(n):
        part = mw.at[matrix[n], :, half]
        return remote(part, part, w4_ss.at[n], w4_rs.at[n], sib)

    up, down = mw.at[even, pl.ds(x_hi * 4, 2), half], mw.at[even, pl.ds(x_hi * 4 + 2, 2), half]
    wz = [remote(up, up, wz_ss.at[0], wz_rs.at[0], above),
          remote(down, down, wz_ss.at[1], wz_rs.at[1], below)]

    def wx_copy(n):
        m = matrix[n]
        return remote(mw_h.at[m, half], mw.at[m, j, half], wx_ss.at[n // 2], wx_rs.at[n // 2], cross)

    def wy_copy(n, d):
        part = mw.at[matrix[n], (1 - x_hi) * 4 + y, half]
        return remote(part, part, wy_ss.at[n // 2], wy_rs.at[n // 2], ypeer(d))

    def w1_start(n):
        for d in (1, 3, 2):
            w1_copy(n, d).start()

    def w1_wait(n):
        arrived(mw.at[matrix[n], 0:3, half], w1_ss.at[n], w1_rs.at[n])

    def wy_start(n):
        wx_copy(n).wait()
        for d in (1, 3, 2):
            wy_copy(n, d).start()

    def wy_pass(n):
        arrived(mw.at[matrix[n], 0:3, half], wy_ss.at[n // 2], wy_rs.at[n // 2])
        w4_copy(n).start()

    def w2_pass(n):
        w2_copy(n).wait()
        w3_copy(n).start()

    def w3_pass(n):
        w3_copy(n).wait()
        w4_copy(n).start()

    wx_copy(1).start()
    wx_copy(3).start()
    w1_start(0)

    loads[4].wait()
    scatter_rows(ct_s, nn(row_order(), cot[...]))

    def c_copy(d):
        return remote(ct_s.at[fpeer(d)], ct_r.at[i], c_ss.at[0], c_rs.at[0], (fpeer(d), j))

    @pl.loop(1, 32)
    def _(d):
        c_copy(d).start()

    ct_r[i] = ct_s[i]
    loads[5].wait()
    loads[6].wait()
    qkv_r[j] = qkv_s[j]

    loads[7].wait()
    for t in range(4):
        spt[t] = spw[t].T

    arrived(qkv_r.at[0:7], q_ss.at[0], q_rs.at[0])

    q, k, v = (qkv_r[:, t].reshape(256, 384) for t in range(3))
    out = None
    for h in range(2):
        probs = softmax(head_of(q, h), k)
        prob_s[h] = probs
        term = nn(probs.astype(BF), head_of(v, h))
        out = term if out is None else out + term
    o_s[...] = out.astype(BF).reshape(8, 32, 384)

    def o_copy(d):
        return remote(o_s.at[qpeer(d)], o_r.at[j], o_ss.at[0], o_rs.at[0], (i, qpeer(d)))

    @pl.loop(1, 8)
    def _(d):
        o_copy(d).start()

    o_r[j] = o_s[j]
    w1_start(2)
    w1_wait(0)
    w2_copy(0).start()
    for c in wz:
        c.start()
    wy_start(1)
    w2_pass(0)

    arrived(o_r.at[0:7], o_ss.at[0], o_rs.at[0])

    w1_start(3)
    wy_start(3)
    so = join_pair(o_r[0:4].reshape(128, 384).astype(F32), o_r[4:8].reshape(128, 384).astype(F32)).astype(BF)
    hid[...] = (act[...].astype(F32) + nn(so, spt[3])).astype(BF)
    scatter_rows(hid_s, nn(row_order(), hid[...]))

    def h_copy(d):
        return remote(hid_s.at[fpeer(d)], hid_r.at[i], h_ss.at[0], h_rs.at[0], (fpeer(d), j))

    @pl.loop(1, 32)
    def _(d):
        h_copy(d).start()

    hid_r[i] = hid_s[i]
    w1_wait(2)
    w2_copy(2).start()

    arrived(ct_r.at[0:31], c_ss.at[0], c_rs.at[0])

    gather_rows(tx, ct_r)
    ctt[...] = tx[...].astype(BF)
    loads[9].wait()
    ctp = nn(ctt[...], perm[...]).astype(BF)

    @pl.when(core == 0)
    def _():
        ax[0, 0:128] = ctp

    @pl.when(core == 1)
    def _():
        fx[0] = ctp

    for c in wz:
        c.wait()
    w3_pass(0)
    wy_pass(1)
    w2_pass(2)

    def weight(n):
        return mw[n].reshape(C, W)

    arrived(hid_r.at[0:31], h_ss.at[0], h_rs.at[0])

    gather_rows(tx, hid_r)
    loads[8].wait()
    gain = mgn[...].reshape(1, C)
    u2, r2 = unit(tx[...])
    u2s[...] = u2
    r2s[...] = jnp.broadcast_to(r2, r2s.shape)
    n2s[...] = (u2 * gain + pe[...]).astype(BF)
    n2p = nn(n2s[...], perm[...]).astype(BF)
    ax[1, 0:128] = n2p
    fx[1] = n2p
    w3_pass(2)
    w4_copy(0).wait()
    w4_copy(1).wait()
    for t in range(2):
        mqkv[t] = nn(n2s[...], weight(t)).astype(BF)
    w1_wait(3)
    wy_pass(3)
    for h in range(HEADS):
        prob_t[h] = softmax(head_of(mqkv[0], h), mqkv[1])
    w4_copy(2).wait()
    mqkv[2] = nn(n2s[...], weight(2)).astype(BF)
    out = None
    for h in range(HEADS):
        term = nn(prob_t[h].astype(BF), head_of(mqkv[2], h))
        out = term if out is None else out + term
    mo_t = out.astype(BF)
    w4_copy(3).wait()
    mg = nn(ctt[...], weight(3)).astype(BF)
    dv = None
    for h in range(HEADS):
        term = tn(prob_t[h].astype(BF), head_of(mg, h))
        dv = term if dv is None else dv + term
    dv = dv.astype(BF)

    @pl.when(core == 0)
    def _():
        ay[0, 0:128] = mo_t
        fx[0] = n2p
        fy[0] = dv

    @pl.when(core == 1)
    def _():
        ax[0, 0:128] = n2p
        ay[0, 0:128] = dv
        fy[0] = mo_t

    swap = [remote(fx.at[0], ax.at[0, 128:256], x_ss.at[0], x_rs.at[0], sib),
            remote(fy.at[0], ay.at[0, 128:256], x_ss.at[1], x_rs.at[1], sib),
            remote(fx.at[1], ax.at[1, 128:256], x_ss.at[2], x_rs.at[2], sib)]
    for c in swap:
        c.start()

    scatter_rows(mo_s, mo_t.astype(F32))

    def m_copy(d):
        return remote(mo_s.at[fpeer(d)], mo_r.at[i], m_ss.at[0], m_rs.at[0], (fpeer(d), j))

    @pl.loop(1, 32)
    def _(d):
        m_copy(d).start()

    mo_r[i] = mo_s[i]

    dq = dk = None
    for h in range(HEADS):
        r = prob_t[h]
        dr = nt(head_of(mg, h), mqkv[2])
        delta = jnp.sum(r * dr, axis=-1, keepdims=True)
        ds = (r * (dr - delta) * SCALE).astype(BF)
        a, b = nn(ds, head_of(mqkv[1], h)), tn(ds, head_of(mqkv[0], h))
        dq, dk = (a, b) if dq is None else (dq + a, dk + b)
    dq, dk = dq.astype(BF), dk.astype(BF)

    @pl.when(core == 0)
    def _():
        ay[1, 0:128] = dq
        fy[1] = dk

    @pl.when(core == 1)
    def _():
        ay[1, 0:128] = dk
        fy[1] = dq

    swap_b = remote(fy.at[1], ay.at[1, 128:256], x_ss.at[3], x_rs.at[3], sib)
    swap_b.start()
    for c in swap:
        c.wait()
    wa[...] = tn(ax[0], ay[0]).reshape(2, 2, 2, 2, 2, 40, W).astype(BF)

    own = (x_hi, (x_hi + x_lo) % 2, y // 2, (y // 2 + y) % 2, z % 2)

    def zpeer(zz):
        return (x_lo * 16 + (zz + 8) % 8 * 2 + core, j)

    partner = {
        XA: beside, XB: cross,
        YA: (i, x_hi * 4 + y + 1 - 2 * (y % 2)), YB: (i, x_hi * 4 + 3 - y),
        ZA: zpeer(z + 1 - 2 * (z % 2)), ZB: zpeer(z - 1 + 2 * (z % 2)),
    }

    def left(p, step):
        return [n for n in range(5) if n not in [DIGIT[link] for link in PARTS[p][3][:step]]]

    def block(p, step, digits):
        which, lane, lanes, _ = PARTS[p]
        ref, columns = ((wa, wb)[which], slice(lane, lane + lanes)) if step == 0 else (buffers[6 * p + 2 * step - 1], slice(None))
        return ref, tuple(digits.get(n, slice(None)) for n in left(p, step)) + (slice(None), columns)

    def step_copy(p, step):
        link = PARTS[p][3][step]
        ref, at = block(p, step, {DIGIT[link]: 1 - own[DIGIT[link]]})
        return remote(ref.at[at], buffers[6 * p + 2 * step], p_ss.at[3 * p + step], p_rs.at[3 * p + step], partner[link])

    def direct(p):
        digits = left(p, 2)
        for mask in range(1, 8):
            to = list(own)
            for bit, n in enumerate(digits):
                if mask >> bit & 1:
                    to[n] = 1 - own[n]
            ref, at = block(p, 2, {n: to[n] for n in digits})
            device = ((to[0] + to[1]) % 2 * 16 + z // 2 * 4 + to[4] * 2 + core, to[0] * 4 + to[2] * 2 + (to[2] + to[3]) % 2)
            remote(ref.at[at], buffers[6 * p + 4].at[mask - 1], p_ss.at[3 * p + 2], p_rs.at[3 * p + 2], device).start()

    done = [0] * 7

    def begin(p):
        step_copy(p, 0).start()

    def advance(p):
        step = done[p]
        step_copy(p, step).wait()
        link = PARTS[p][3][step]
        ref, at = block(p, step, {DIGIT[link]: own[DIGIT[link]]})
        buffers[6 * p + 2 * step + 1][...] = (
            ref[at].astype(F32) + buffers[6 * p + 2 * step][...].astype(F32)).astype(BF)
        done[p] = step + 1
        if step == 0:
            step_copy(p, 1).start()
        else:
            direct(p)

    def result(p):
        come = buffers[6 * p + 4]
        arrived(come, p_ss.at[3 * p + 2], p_rs.at[3 * p + 2])
        ref, at = block(p, 2, {n: own[n] for n in left(p, 2)})
        total = ref[at].astype(F32)
        for n in range(7):
            total = total + come[n].astype(F32)
        return total.astype(BF)

    for p in (0, 1, 2):
        begin(p)
    dn2 = nt(dq, weight(0)) + nt(dk, weight(1)) + nt(dv, weight(2))
    u2 = u2s[...]
    gv1[...] = jnp.sum(dn2 * u2, axis=0, keepdims=True)
    back = ctt[...].astype(F32) + unit_back(dn2, u2, r2s[:, 0:1], gain)
    scatter_rows(lb_s, back)

    def l_copy(d):
        return remote(lb_s.at[fpeer(d)], lb_r.at[i], l_ss.at[0], l_rs.at[0], (fpeer(d), j))

    @pl.loop(1, 32)
    def _(d):
        l_copy(d).start()

    lb_r[i] = lb_s[i]

    def v_copy(src, dst, n, dev):
        return remote(src, dst, v_ss.at[n], v_rs.at[n], dev)

    gx = [v_copy(gv1, gr1.at[d - 1], 0, xpeer(d)) for d in range(1, 4)]
    for c in gx:
        c.start()

    swap_b.wait()
    wb[...] = tn(ax[1], ay[1]).reshape(2, 2, 2, 2, 2, 40, W).astype(BF)

    for p in (3, 4, 5, 6):
        begin(p)

    arrived(mo_r.at[0:31], m_ss.at[0], m_rs.at[0])

    gather_rows(mof, mo_r)
    mo = tn(row_order(), mof[...].astype(BF)).astype(BF)
    bo[...] = (hid[...].astype(F32) + nt(mo, weight(3))).astype(BF)
    bo_store = pltpu.make_async_copy(bo, bo_h, st.at[0])
    bo_store.start()

    advance(2)
    advance(0)
    advance(1)

    arrived(lb_r.at[0:31], l_ss.at[0], l_rs.at[0])

    gather_rows(tx, lb_r)
    gh[...] = tn(row_order(), tx[...].astype(BF)).astype(BF)
    for hp, part in enumerate(split_pair(nn(gh[...], spw[3]))):
        gs_s[hp * 4:hp * 4 + 4] = part.astype(BF).reshape(4, 32, 384)

    def gs_copy(d):
        return remote(gs_s.at[qpeer(d)], gs_r.at[j], gs_ss.at[0], gs_rs.at[0], (i, qpeer(d)))

    @pl.loop(1, 8)
    def _(d):
        gs_copy(d).start()

    gs_r[j] = gs_s[j]

    arrived(gr1, v_ss.at[0], v_rs.at[0])
    gv2[...] = gv1[...] + gr1[0] + gr1[1] + gr1[2]
    gy = [v_copy(gv2, gr2.at[d - 1], 1, ypeer(d)) for d in range(1, 4)]
    for c in gy:
        c.start()
    advance(5)
    advance(6)
    advance(4)
    advance(3)
    advance(2)
    advance(0)
    advance(1)
    arrived(gs_r.at[0:7], gs_ss.at[0], gs_rs.at[0])

    q, k, v = (qkv_r[:, t].reshape(256, 384) for t in range(3))
    for t, grad in enumerate(attend_back(q, k, v, gs_r[...].reshape(256, 384), prob_s, 2)):
        dq_s[:, t] = grad.astype(BF).reshape(8, 32, 384)

    advance(5)
    advance(6)
    advance(3)
    advance(4)

    def dq_copy(d):
        return remote(dq_s.at[qpeer(d)], dq_r.at[j], dq_ss.at[0], dq_rs.at[0], (i, qpeer(d)))

    @pl.loop(1, 8)
    def _(d):
        dq_copy(d).start()

    dq_r[j] = dq_s[j]

    arrived(gr2, v_ss.at[1], v_rs.at[1])
    gv3[...] = gv2[...] + gr2[0] + gr2[1] + gr2[2]
    gz = v_copy(gv3, gr3, 2, partner[ZA])
    gz.start()

    row = lax.broadcasted_iota(jnp.int32, (128, 40), 0)
    col = lax.broadcasted_iota(jnp.int32, (128, 40), 1)
    first = jnp.where((row % 16 < 5) & (col == (row // 16) * 5 + row % 16), 1.0, 0.0).astype(BF)
    second = jnp.where((row % 16 >= 5) & (row % 16 < 10) & (col == (row // 16) * 5 + row % 16 - 5), 1.0, 0.0).astype(BF)
    gz.wait()
    gv = gv3[...] + gr3[...]
    sum_a = jnp.concatenate([result(p) for p in (0, 1, 2)], axis=1)
    sum_b = jnp.concatenate([result(p) for p in (3, 4, 5, 6)], axis=1)
    slabs = nn(first, sum_a) + nn(second, sum_b)
    row = lax.broadcasted_iota(jnp.int32, (128, W), 0) % 16
    slabs = jnp.where(row == 10, gv[:, :W], jnp.where(row == 11, gv[:, W:], slabs))
    p3[...] = slabs.astype(BF).reshape(8, 16, W)
    place = z // 2 * 2 + core

    def z_copy(d):
        to = (place + d) % 8
        return remote(p3.at[to], r3.at[place], r3_ss.at[0], r3_rs.at[0],
                      (x_lo * 16 + to // 2 * 4 + z % 2 * 2 + to % 2, j))

    @pl.loop(1, 8)
    def _(d):
        z_copy(d).start()

    r3[place] = p3[place]

    u1, r1 = unit(act[...].astype(F32))
    arrived(dq_r.at[0:7], dq_ss.at[0], dq_rs.at[0])

    total = None
    for t in range(3):
        grad = join_pair(dq_r[0:4, t].reshape(128, 384).astype(F32), dq_r[4:8, t].reshape(128, 384).astype(F32)).astype(BF)
        term = nn(grad, spt[t])
        total = term if total is None else total + term
    ig[...] = (gh[...].astype(F32) + unit_back(total, u1, r1, spg[...].reshape(1, C))).astype(BF)
    ig_store = pltpu.make_async_copy(ig, ig_h, st.at[1])
    ig_store.start()

    arrived(r3.at[0:7], r3_ss.at[0], r3_rs.at[0])

    factor = 1.0 / math.sqrt(128 * 256)
    sums = []
    for c in range(2):
        total = r3[c].astype(F32)
        for n in range(1, 4):
            total = total + r3[2 * n + c].astype(F32)
        sums.append(total * factor)
    wg[0:5, 0] = sums[0][5:10]
    wg[0:5, 1] = sums[1][5:10]
    wg[0:5, 2] = sums[1][0:5]
    wg[0:5, 3] = sums[0][0:5]
    wg[5, 0:2] = (sums[0] + sums[1])[10:12]
    wg_store = pltpu.make_async_copy(wg, wg_h, st.at[2])
    wg_store.start()
    wg_store.wait()
    bo_store.wait()
    ig_store.wait()


def finish(bo_h, ig_h, wg_h, bo, ig, wg, gg, bo_v, ig_v, wg_v, sems):
    rows = [pl.ds(32 * n, 32) for n in range(4)]
    moves = [(wg_h, wg_v, wg_v.at[0:5], wg)]
    for r in rows:
        moves += [(bo_h.at[r], bo_v.at[r], bo_v.at[r], bo.at[r]), (ig_h.at[r], ig_v.at[r], ig_v.at[r], ig.at[r])]
    come = [pltpu.make_async_copy(a, b, sems.at[0, n]) for n, (a, b, _, _) in enumerate(moves)]
    go = [pltpu.make_async_copy(c, d, sems.at[1, n]) for n, (_, _, c, d) in enumerate(moves)]
    for c in come:
        c.start()
    for a, b in zip(come, go):
        a.wait()
        b.start()
    device = lax.axis_index("frame") * 8 + lax.axis_index("quad")
    gain = jnp.concatenate([wg_v[5, 0:1, :], wg_v[5, 1:2, :]], axis=1)
    gg[...] = pltpu.roll(gain, (C - device * 5) % C, 1)[0, :5]
    for c in go:
        c.wait()


def positional(frames, channels):
    freq = np.exp(np.arange(channels // 2, dtype=np.float32)[None, :] * np.float32(-2.0 * math.log(10000.0) / channels))
    phases = np.arange(frames, dtype=np.float32)[:, None] * freq.astype(np.float32)
    both = np.stack([np.sin(phases.astype(np.float64)), np.cos(phases.astype(np.float64))], axis=-1)
    return both.reshape(frames, channels).astype(np.float32)


def permutation():
    matrix = np.zeros((C, C), np.float32)
    for m in range(C):
        rest, r = divmod(m, 5)
        rest, core = divmod(rest, 2)
        rest, z_high = divmod(rest, 4)
        xb, xa, yb, ya, z_low = (rest // 16) % 2, (rest // 8) % 2, (rest // 4) % 2, (rest // 2) % 2, rest % 2
        y = yb * 2 + (yb + ya) % 2
        n = (xb + xa) % 2 * 640 + (z_high * 2 + z_low) * 80 + core * 40 + xb * 20 + y * 5 + r
        matrix[n, m] = 1.0
    return matrix


def part_buffers():
    shapes = []
    for _, _, lanes, _ in PARTS:
        shapes += [pltpu.VMEM((2, 2, 2, 2, 40, lanes), BF)] * 2 + [pltpu.VMEM((2, 2, 2, 40, lanes), BF)] * 2
        shapes += [pltpu.VMEM((7, 40, lanes), BF), pltpu.VMEM((8, 128), BF)]
    return shapes


def local(activations, cotangent, spatial_weights, spatial_gain, motion_weights, motion_gain):
    pe = jnp.asarray(positional(128, C))
    perm = jnp.asarray(permutation(), dtype=BF)
    V, D = pltpu.VMEM, pltpu.SemaphoreType.DMA
    any_, vmem = pl.BlockSpec(memory_space=pl.ANY), pl.BlockSpec(memory_space=pltpu.VMEM)
    scratch = [
        V((128, C), BF), V((128, C), BF), V((4, C, W), BF), V((4, W, C), BF), V((4, 8, 160, W), BF), V((128, C), F32), V((C, C), BF),
        V((128, C), BF), V((128, C), BF), V((6, 4, W), F32),
        V((8, 3, 32, 384), BF), V((8, 3, 32, 384), BF), V((8, 32, 384), BF), V((8, 32, 384), BF), V((2, 256, 256), F32),
        V((128, C), BF), V((32, 4, C), BF), V((32, 4, C), BF), V((32, 4, C), BF), V((32, 4, C), BF), V((128, C), BF),
        V((128, C), F32), V((128, C), BF), V((128, C), F32), V((128, 128), F32), V((3, 128, W), BF), V((4, 128, 128), F32),
        V((32, 4, W), BF), V((32, 4, W), BF), V((32, 4, C), BF), V((32, 4, C), BF), V((128, C), BF), V((128, W), F32),
        V((8, 32, 384), BF), V((8, 32, 384), BF), V((8, 3, 32, 384), BF), V((8, 3, 32, 384), BF),
        V((2, 128, C), BF), V((2, 128, W), BF), V((2, 256, C), BF), V((2, 256, W), BF),
        V((2, 2, 2, 2, 2, 40, W), BF), V((2, 2, 2, 2, 2, 40, W), BF), V((8, 16, W), BF), V((8, 16, W), BF),
        V((1, C), F32), V((3, 1, C), F32), V((1, C), F32), V((3, 1, C), F32), V((1, C), F32), V((1, C), F32),
        D((10,)), D((3,))] + [D((4,))] * 2 + [D((2,))] * 4 + [D((4,))] * 2 + [D((2,))] * 6 + [D((1,))] * 16 + [
        D((4,)), D((4,)), D((21,)), D((21,)), D((1,)), D((1,)),
        D((3,)), D((3,)),
    ] + part_buffers()
    tokens = jax.ShapeDtypeStruct((128, C), BF)
    block_output, input_grad, sums = pl.pallas_call(
        kernel,
        out_shape=(tokens, tokens, jax.ShapeDtypeStruct((6, 4, W), F32)),
        in_specs=[any_, any_, any_, vmem, any_, vmem, any_, any_],
        out_specs=(any_, any_, any_),
        scratch_shapes=scratch,
        compiler_params=pltpu.CompilerParams(
            has_side_effects=True, collective_id=0, vmem_limit_bytes=60 * 2 ** 20),
    )(
        activations.reshape(128, C), cotangent.reshape(128, C), spatial_weights, spatial_gain,
        motion_weights, motion_gain, pe, perm,
    )
    block_output, input_grad, weight_grad, gain_grad = pl.pallas_call(
        finish,
        out_shape=(tokens, tokens, jax.ShapeDtypeStruct((5, 4, W), F32), jax.ShapeDtypeStruct((5,), F32)),
        in_specs=[any_, any_, any_],
        out_specs=(any_, any_, any_, vmem),
        scratch_shapes=[V((128, C), BF), V((128, C), BF), V((6, 4, W), F32), D((2, 9))],
        compiler_params=pltpu.CompilerParams(vmem_limit_bytes=60 * 2 ** 20),
    )(block_output, input_grad, sums)
    shape = activations.shape
    return block_output.reshape(shape), input_grad.reshape(shape), weight_grad.transpose(1, 0, 2), gain_grad


def solution(mesh):
    in_specs = (
        P("frame", "quad", None),
        P("frame", "quad", None),
        P(),
        P(),
        P(None, "quad", None),
        P(),
    )
    out_specs = (
        P("frame", "quad", None),
        P("frame", "quad", None),
        P(None, ("frame", "quad"), None),
        P(("frame", "quad")),
    )
    return jax.shard_map(local, mesh=mesh, in_specs=in_specs, out_specs=out_specs, check_vma=False)
```
